256 devices in a mesh: elem: 64 (over x, z, core), sub: 4 (over y).
Axes of the slice: x: 4, y: 4, z: 8, core: 2. Of those that a mesh axis runs over, the one named last changes fastest.
Arguments:
- velocity: float32 [3, 512, 64, 128], P(None, 'elem', 'sub'), may hold values from -6 to 6
Outputs:
- advected: float32 [3, 512, 64, 128], P(None, 'elem', 'sub')
- pressure: float32 [512, 64, 128], P('elem', 'sub')
The draws below stay inside these ranges and needn't reach their ends.
All inputs are finite; a program needn't handle non-finite values.
Results may differ from the reference program's by a relative error of at most 0.00021.
Values sent between devices are 32-bit elements; how exact they have to be, the bound alone decides.
A program may use at most 128 MiB of HBM per device.

```python
import jax
import jax.numpy as jnp
import numpy as np
from jax import lax

POINTS = 8
SUBSTEPS = 3
MG_ITERS = 3
COARSE_ITERS = 4
ZP = 512
XP = 64
YP = 128


def levels(stream_key, extent, shards, least, top_value):
    def one(dim, parts):
        steps = jax.random.uniform(jax.random.fold_in(jax.random.fold_in(stream_key, 6), dim), (parts,), jnp.float32, least / len(shards), top_value / len(shards))
        return jnp.repeat(jnp.exp(steps), extent[dim] // parts).reshape((-1,) + (1,) * (len(extent) - dim - 1))

    loudness = one(*shards[0])
    for cut in shards[1:]:
        loudness = loudness * one(*cut)
    return loudness


def normal_values(own_key, extent, width, reach, pieces=(), held_as=jnp.bfloat16):
    values = width * jax.random.normal(own_key, extent, jnp.float32)
    if pieces:
        values = values * levels(own_key, extent, pieces, -0.22, 0.18)
    return jnp.clip(values, -reach, reach).astype(held_as)


def setup_inputs(seed: int = 0) -> dict:
    keys = jax.random.split(jax.random.key(seed), 2)
    velocity = normal_values(keys[0], (3, ZP, XP, YP), 1.0, 6.0, ((1, 64), (2, 4)), jnp.float32)
    return dict(velocity=velocity)


TIME_STEP = 0.005
SHIFT_COEF = 0.05
RELAXATION = 0.6
SOURCE_GAIN = 20.0


def legendre_last(points, degree):
    previous = points * 0.0 + 1.0
    current = points + 0.0
    for level in range(2, degree + 1):
        following = ((2 * level - 1) * points * current - (level - 1) * previous) / level
        previous = current
        current = following
    return previous, current


def gll_tables(count):
    degree = count - 1
    points = -np.cos(np.pi * np.arange(count) / degree)
    for sweep in range(100):
        before_last, last_value = legendre_last(points, degree)
        points = points - (points * last_value - before_last) / (count * last_value)
    abscissae = points
    before_last, legendre = legendre_last(abscissae, degree)
    weights = 2.0 / (degree * (degree + 1) * legendre ** 2)
    spacing = abscissae[:, None] - abscissae[None, :] + np.eye(count)
    matrix = legendre[:, None] / (legendre[None, :] * spacing) * (1.0 - np.eye(count))
    matrix[0, 0] = -degree * (degree + 1) / 4.0
    matrix[degree, degree] = degree * (degree + 1) / 4.0
    return abscissae, weights, matrix


def apply_axis(field, axis, matrix):
    table = jnp.asarray(matrix, jnp.float32)
    out_count, in_count = matrix.shape
    layout = field.shape
    blocks = layout[axis] // in_count
    split = layout[:axis] + (blocks, in_count) + layout[axis + 1:]
    forms = {1: "ij,kejxy->keixy", 2: "ij,kzejy->kzeiy", 3: "ij,kzxej->kzxei"}
    result = jnp.einsum(forms[axis], table, field.reshape(split), precision=lax.Precision.HIGHEST)
    return result.reshape(layout[:axis] + (blocks * out_count,) + layout[axis + 1:])


def weight_field(layout, weights):
    count = weights.shape[0]
    along_z = np.tile(weights, layout[1] // count)
    along_x = np.tile(weights, layout[2] // count)
    along_y = np.tile(weights, layout[3] // count)
    table = along_z[:, None, None] * along_x[None, :, None] * along_y[None, None, :] / 8.0
    return jnp.asarray(table[None], jnp.float32)


def add_faces(padded, axis, count):
    length = padded.shape[axis] - 2
    center = lax.slice_in_dim(padded, 1, length + 1, axis=axis)
    after = lax.slice_in_dim(padded, 2, length + 2, axis=axis)
    before = lax.slice_in_dim(padded, 0, length, axis=axis)
    position = lax.broadcasted_iota(jnp.int32, center.shape, axis) % count
    return center + jnp.where(position == count - 1, after, 0.0) + jnp.where(position == 0, before, 0.0)


def share_global(field, count):
    padded = jnp.concatenate([field[:, -1:], field, field[:, :1]], axis=1)
    field = add_faces(padded, 1, count)
    padded = jnp.concatenate([field[:, :, -1:], field, field[:, :, :1]], axis=2)
    field = add_faces(padded, 2, count)
    padded = jnp.pad(field, ((0, 0), (0, 0), (0, 0), (1, 1)))
    return add_faces(padded, 3, count)


def local_operator(field, mass_local, matrix):
    total = SHIFT_COEF * mass_local * field
    for axis in (1, 2, 3):
        slope = apply_axis(field, axis, matrix)
        total = total + 4.0 * apply_axis(mass_local * slope, axis, matrix.T)
    return total


def local_diagonal(mass_local, matrix):
    total = SHIFT_COEF * mass_local
    for axis in (1, 2, 3):
        total = total + 4.0 * apply_axis(mass_local, axis, (matrix * matrix).T)
    return total


def conjugate(right_side, operator, inner):
    solution = jnp.zeros_like(right_side)
    residual = right_side
    direction = right_side
    norm_now = inner(residual, residual)
    for sweep in range(COARSE_ITERS):
        image = operator(direction)
        alpha = norm_now / inner(direction, image)
        solution = solution + alpha * direction
        residual = residual - alpha * image
        norm_next = inner(residual, residual)
        direction = residual + (norm_next / norm_now) * direction
        norm_now = norm_next
    return solution


def reference(velocity):
    abscissae, weights, matrix = gll_tables(POINTS)
    coarse_xi, coarse_weights, coarse_matrix = gll_tables(2)
    lift = np.stack([(1.0 - abscissae) / 2.0, (1.0 + abscissae) / 2.0], axis=1)
    layout = (1,) + velocity.shape[1:]
    mass_local = weight_field(layout, weights)
    setup = share_global(jnp.concatenate([mass_local, jnp.ones(layout, jnp.float32), local_diagonal(mass_local, matrix)], 0), POINTS)
    mass_sum = setup[0:1]
    multiplicity = setup[1:2]
    diagonal = setup[2:3]
    for sub_step in range(SUBSTEPS):
        term = jnp.zeros_like(velocity)
        for axis in (1, 2, 3):
            term = term + velocity[axis - 1:axis] * apply_axis(velocity, axis, matrix)
        term = 2.0 * mass_local * term
        velocity = velocity - TIME_STEP * share_global(term, POINTS) / mass_sum
    divergence = jnp.zeros(layout, jnp.float32)
    for axis in (1, 2, 3):
        divergence = divergence + apply_axis(velocity[axis - 1:axis], axis, matrix)
    source = -SOURCE_GAIN * share_global(mass_local * divergence, POINTS)
    coarse_layout = (1, layout[1] // POINTS * 2, layout[2] // POINTS * 2, layout[3] // POINTS * 2)
    coarse_mass = jnp.full(coarse_layout, 0.125, jnp.float32)
    coarse_count = share_global(jnp.ones(coarse_layout, jnp.float32), 2)

    def coarse_apply(field):
        return share_global(local_operator(field, coarse_mass, coarse_matrix), 2)

    def coarse_inner(left_side, right_part):
        return jnp.sum(left_side * right_part / coarse_count)

    def fine_apply(field):
        return share_global(local_operator(field, mass_local, matrix), POINTS)

    pressure = jnp.zeros(layout, jnp.float32)
    for cycle in range(MG_ITERS):
        residual = source if cycle == 0 else source - fine_apply(pressure)
        pressure = pressure + RELAXATION * residual / diagonal
        residual = source - fine_apply(pressure)
        reduced = residual / multiplicity
        for axis in (1, 2, 3):
            reduced = apply_axis(reduced, axis, lift.T)
        correction = conjugate(share_global(reduced, 2), coarse_apply, coarse_inner)
        for axis in (1, 2, 3):
            correction = apply_axis(correction, axis, lift)
        pressure = pressure + correction
        residual = source - fine_apply(pressure)
        pressure = pressure + RELAXATION * residual / diagonal
    return velocity, pressure[0]
```

```python
import functools

import jax
import jax.numpy as jnp
import ml_dtypes
import numpy as np
from jax import lax
from jax.experimental import pallas as pl
from jax.experimental.pallas import tpu as pltpu
from jax.sharding import PartitionSpec as P

POINTS = 8
SUBSTEPS = 3
MG_ITERS = 3
COARSE_ITERS = 4

TIME_STEP = 0.005
SHIFT_COEF = 0.05
RELAXATION = 0.6
SOURCE_GAIN = 20.0

MESH = pl.DeviceIdType.MESH
ROUNDS = SUBSTEPS + 2 * MG_ITERS


def legendre_last(points, degree):
    previous = points * 0.0 + 1.0
    current = points + 0.0
    for level in range(2, degree + 1):
        following = ((2 * level - 1) * points * current - (level - 1) * previous) / level
        previous = current
        current = following
    return (previous, current)


def gll_tables(count):
    degree = count - 1
    points = -np.cos(np.pi * np.arange(count) / degree)
    for sweep in range(100):
        before_last, last_value = legendre_last(points, degree)
        points = points - (points * last_value - before_last) / (count * last_value)
    before_last, legendre = legendre_last(points, degree)
    weights = 2.0 / (degree * (degree + 1) * legendre**2)
    spacing = points[:, None] - points[None, :] + np.eye(count)
    matrix = legendre[:, None] / (legendre[None, :] * spacing) * (1.0 - np.eye(count))
    matrix[0, 0] = -degree * (degree + 1) / 4.0
    matrix[degree, degree] = degree * (degree + 1) / 4.0
    return (points, weights, matrix)


def assembled(values, walls):
    blocks = values.reshape(-1, POINTS)
    out = blocks.copy()
    out[:, 0] += blocks[:, -1]
    out[:, -1] += blocks[:, 0]
    if walls:
        out[0, 0] = blocks[0, 0]
        out[-1, -1] = blocks[-1, -1]
    return out.reshape(-1)


def coarse_tables(elements, lift, stiff, walls):
    count = elements * POINTS
    vertices = elements + 1
    interp = np.zeros((count, vertices + 2))
    slope = np.zeros((count, vertices + 2))
    edge = stiff @ lift
    for element in range(elements):
        for point in range(POINTS):
            row = element * POINTS + point
            pairs = [(element, point)]
            if point == 0 and not (walls and element == 0):
                pairs.append((element - 1, POINTS - 1))
            if point == POINTS - 1 and not (walls and element == elements - 1):
                pairs.append((element + 1, 0))
            for side in (0, 1):
                interp[row, element + side + 1] += lift[point, side]
                for other, at in pairs:
                    slope[row, other + side + 1] += edge[at, side]
    slope[np.abs(slope) < 1e-12] = 0.0
    return (interp[:, 1:-1], slope[:, 1:-1]) if walls else (interp, slope)


def halves(matrix):
    whole = np.asarray(matrix, np.float32)
    high = whole.astype(ml_dtypes.bfloat16)
    low = (whole - high.astype(np.float32)).astype(ml_dtypes.bfloat16)
    return np.stack([high, low])


def make_tables():
    points, weights, deriv = gll_tables(POINTS)
    stiff = deriv.T @ np.diag(weights) @ deriv
    scaled = np.diag(1.0 / weights) @ stiff
    squares = (deriv * deriv).T @ weights
    lift = np.stack([(1.0 - points) / 2.0, (1.0 + points) / 2.0], axis=1)
    kron, eye = np.kron, np.eye
    wz, wx, wy = weights, np.tile(weights, 2), np.tile(weights, 16)
    waz, wax, way = assembled(wz, False), assembled(wx, False), assembled(wy, True)
    saz = assembled(squares, False)
    sax = assembled(np.tile(squares, 2), False)
    say = assembled(np.tile(squares, 16), True)

    def outer(a, b, c):
        return kron(a, b)[:, None] * c[None, :]

    local = outer(wz, wx, wy) / 8.0
    mass = outer(waz, wax, way) / 8.0
    diagonal = 0.5 * (outer(saz, wax, way) + outer(waz, sax, way) + outer(waz, wax, say))
    diagonal = diagonal + SHIFT_COEF * mass
    jz, kz = coarse_tables(1, lift, stiff, False)
    jx, kx = coarse_tables(2, lift, stiff, False)
    jy, ky = coarse_tables(16, lift, stiff, True)

    def lanes(table):
        out = np.zeros((table.shape[0], 128))
        out[:, :68] = np.tile(table, (1, 4))
        return out

    left = kron(scaled, eye(16)) + kron(eye(8), kron(eye(2), scaled)) + SHIFT_COEF / 4.0 * eye(128)
    matrices = [
        kron(deriv, eye(16)),
        kron(eye(8), kron(eye(2), deriv)),
        kron(eye(16), deriv).T,
        left,
        kron(eye(16), scaled).T,
        lanes(way[:, None] * jy),
        lanes(ky),
        lanes(jy),
        lanes(jy).T,
        lanes(ky).T,
    ]
    matrices = np.stack([halves(one) for one in matrices])
    fields = np.stack(
        [
            4.0 * local,
            local / mass,
            RELAXATION / diagonal,
            0.5 * outer(waz, wax, np.ones(128)),
        ]
    ).astype(np.float32)
    lane = np.arange(128)
    inner = lane % POINTS
    level = lane % 17
    valid = lane < 68
    rows = np.zeros((8, 128), np.float32)
    rows[0] = (inner == 0) & (lane > 0)
    rows[1] = (inner == POINTS - 1) & (lane < 127)
    rows[2] = way
    rows[3] = np.where(valid, np.where((level == 0) | (level == 16), 1.0, 2.0), 0.0)
    rows[4] = valid & (level < 16)
    rows[5] = valid & (level > 0)
    kinds = [jx, wax[:, None] * jx, 0.5 * kx + SHIFT_COEF / 8.0 * wax[:, None] * jx]
    spans = np.zeros((4, 6, 16, 128), np.float32)
    for sub in range(4):
        for kind, table in enumerate(kinds):
            for half in range(2):
                for slot in range(4):
                    column = (2 * slot + half - 2 * sub + 1) % 8
                    if column < 5:
                        spans[sub, kind * 2 + half, :, slot * 17 : slot * 17 + 17] = table[
                            :, column : column + 1
                        ]
    return matrices, fields, rows, spans, jz, kz, waz


M_DZ, M_DX, M_DY, M_LEFT, M_RIGHT, M_JYW, M_KY, M_JY, M_JYT, M_KYT = range(10)


def kernel(
    zcoef,
    count,
    vel_in,
    mats,
    fields,
    rows,
    spans,
    adv_out,
    p_out,
    vel,
    sloc,
    pres,
    csrc,
    work,
    acc,
    xs,
    co,
    zr,
    xr,
    cr,
    g1,
    g2,
    ext,
    n_send,
    n_recv,
    a_send,
    a_recv,
    b_send,
    b_recv,
):
    jz, kz, waz = zcoef
    blocks = count // 4
    tiles = blocks // 2
    elem = lax.axis_index("elem")
    sub = lax.axis_index("sub")
    block = elem // 4
    place = elem % 4
    slot = place * 4 + sub

    def near(de, ds):
        return (lax.rem(elem + de + count, count), lax.rem(sub + ds + 4, 4))

    near_ids = [
        near(1, 1),
        near(1, -1),
        near(-1, 1),
        near(-1, -1),
        near(1, 0),
        near(-1, 0),
        near(0, 1),
        near(0, -1),
    ]
    a_ids = [
        (block * 4 + lax.rem(place + dj, 4), lax.rem(sub + ds, 4))
        for dj in range(4)
        for ds in range(4)
        if dj or ds
    ]
    b_ids = [(lax.rem(block + db, blocks) * 4 + place, sub) for db in range(1, blocks)]

    barrier = pltpu.get_barrier_semaphore()
    partners = near_ids + a_ids + b_ids
    for one in partners:
        pl.semaphore_signal(barrier, inc=1, device_id=one, device_id_type=MESH)

    sublane = lax.broadcasted_iota(jnp.int32, (8, 128), 0)
    low_lane, high_lane = rows[0:1, :], rows[1:2, :]

    def split(x):
        high = x.astype(jnp.bfloat16)
        return high, (x - high.astype(jnp.float32)).astype(jnp.bfloat16)

    def mul(a, b):
        return jnp.dot(a, b, preferred_element_type=jnp.float32)

    def left_dot(index, parts):
        high, low = parts
        return mul(mats[index, 0], high) + (mul(mats[index, 0], low) + mul(mats[index, 1], high))

    def right_dot(parts, index):
        high, low = parts
        return mul(high, mats[index, 0]) + (mul(low, mats[index, 0]) + mul(high, mats[index, 1]))

    def near_copies(r, comps):
        pairs = [
            (co.at[r, 0], cr.at[r, 0]),
            (co.at[r, 1], cr.at[r, 1]),
            (co.at[r, 2], cr.at[r, 2]),
            (co.at[r, 3], cr.at[r, 3]),
            (work.at[r, pl.ds(0, comps), pl.ds(112, 16)], zr.at[r, 0, pl.ds(0, comps)]),
            (work.at[r, pl.ds(0, comps), pl.ds(0, 16)], zr.at[r, 1, pl.ds(0, comps)]),
            (xs.at[r, 1, pl.ds(0, comps)], xr.at[r, 0, pl.ds(0, comps)]),
            (xs.at[r, 0, pl.ds(0, comps)], xr.at[r, 1, pl.ds(0, comps)]),
        ]
        return [
            pltpu.make_async_remote_copy(
                src_ref=src,
                dst_ref=dst,
                send_sem=n_send.at[r, k],
                recv_sem=n_recv.at[r, k],
                device_id=near_ids[k],
                device_id_type=MESH,
            )
            for k, (src, dst) in enumerate(pairs)
        ]

    def start_near(r, comps):
        for corner, row in enumerate((127, 112, 15, 0)):
            tile = jnp.zeros((8, 128), jnp.float32)
            for c in range(comps):
                tile = jnp.where(sublane == c, work[r, c, row : row + 1, :], tile)
            co[r, corner] = tile
        for c in range(comps):
            xs[r, 0, c] = work[r, c, pl.ds(0, 8, stride=16), :]
            xs[r, 1, c] = work[r, c, pl.ds(15, 8, stride=16), :]
        for copy in near_copies(r, comps):
            copy.start()

    def finish_near(r, comps):
        for copy in near_copies(r, comps):
            copy.wait_recv()
        out = []
        for c in range(comps):
            acc[c, 0:16] = work[r, c, 0:16] + zr[r, 0, c]
            acc[c, 16:112] = work[r, c, 16:112]
            acc[c, 112:128] = work[r, c, 112:128] + zr[r, 1, c]
            both = acc[c, pl.ds(7, 8, stride=16), :] + acc[c, pl.ds(8, 8, stride=16), :]
            acc[c, pl.ds(7, 8, stride=16), :] = both
            acc[c, pl.ds(8, 8, stride=16), :] = both
            for side, row in ((0, 0), (1, 15)):
                face = xr[r, side, c]
                face = face + jnp.where(sublane == 0, cr[r, side, c : c + 1, :], 0.0)
                face = face + jnp.where(sublane == 7, cr[r, 2 + side, c : c + 1, :], 0.0)
                acc[c, pl.ds(row, 8, stride=16), :] = acc[c, pl.ds(row, 8, stride=16), :] + face
            field = acc[c]
            field = (
                field
                + low_lane * pltpu.roll(field, 1, 1)
                + high_lane * pltpu.roll(field, 127, 1)
            )
            out.append(field)
        return out

    for c in range(3):
        vel[c] = vel_in[c].reshape(128, 128)
    pl.semaphore_wait(barrier, len(partners))

    def substep(i, carry):
        parts = [split(vel[c]) for c in range(3)]
        for c in range(3):
            term = vel[0] * left_dot(M_DZ, parts[c])
            term = term + vel[1] * left_dot(M_DX, parts[c])
            term = term + vel[2] * right_dot(parts[c], M_DY)
            work[i, c] = term * ((2.0 * TIME_STEP) * fields[1])
        start_near(i, 3)
        shared = finish_near(i, 3)
        for c in range(3):
            vel[c] = vel[c] - shared[c]
        return carry

    lax.fori_loop(0, SUBSTEPS, substep, 0)

    for c in range(3):
        adv_out[c] = vel[c].reshape(8, 16, 128)
    divergence = left_dot(M_DZ, split(vel[0])) + left_dot(M_DX, split(vel[1]))
    divergence = divergence + right_dot(split(vel[2]), M_DY)
    source = (-SOURCE_GAIN / 4.0) * fields[0] * divergence
    sloc[...] = source
    pres[...] = jnp.zeros_like(source)
    direct = right_dot(split(source), M_JY).reshape(8, 16, 128)
    for half in range(2):
        span = spans[sub, half]
        for zi in range(4):
            total = None
            for z in range(8):
                if jz[z, zi] != 0.0:
                    one = float(jz[z, zi]) * direct[z]
                    total = one if total is None else total + one
            if total is None:
                row = jnp.zeros((1, 128), jnp.float32)
            else:
                row = jnp.sum(total * span, axis=0, keepdims=True)
            csrc[half * 4 + zi : half * 4 + zi + 1, :] = row

    def weighted(table, zi, field):
        total = None
        for z in range(8):
            if table[z, zi] != 0.0:
                one = float(table[z, zi]) * field[z]
                total = one if total is None else total + one
        return total

    wjz = waz[:, None] * jz

    def minus_laplace(field):
        parts = split(field)
        return sloc[...] - fields[0] * (left_dot(M_LEFT, parts) + right_dot(parts, M_RIGHT))

    def a_copies(it):
        return [
            pltpu.make_async_remote_copy(
                src_ref=g1.at[it, slot],
                dst_ref=g1.at[it, slot],
                send_sem=a_send.at[it, k],
                recv_sem=a_recv.at[it, k],
                device_id=one,
                device_id_type=MESH,
            )
            for k, one in enumerate(a_ids)
        ]

    def b_copies(it):
        return [
            pltpu.make_async_remote_copy(
                src_ref=g2.at[it, block],
                dst_ref=g2.at[it, block],
                send_sem=b_send.at[it, k],
                recv_sem=b_recv.at[it, k],
                device_id=one,
                device_id_type=MESH,
            )
            for k, one in enumerate(b_ids)
        ]

    def coarse_apply(pair):
        my, up, down = rows[3:4, :], rows[4:5, :], rows[5:6, :]
        even, odd = pair
        across = (
            odd + pltpu.roll(odd, 17, 1) + pltpu.roll(odd, 77, 1),
            even + pltpu.roll(even, 111, 1) + pltpu.roll(even, 51, 1),
        )
        out = []
        for u, near_x in zip(pair, across):
            near_z = pltpu.roll(u, 1, 0) + pltpu.roll(u, u.shape[0] - 1, 0)
            one = my * (3.025 * u - 0.5 * (near_z + near_x))
            out.append(one - up * pltpu.roll(u, 127, 1) - down * pltpu.roll(u, 1, 1))
        return out

    def inner(a, b):
        return jnp.sum(a[0] * b[0] + a[1] * b[1], keepdims=True)

    def conjugate(right_side):
        solution = None
        residual = right_side
        direction = right_side
        norm_now = inner(residual, residual)
        for sweep in range(COARSE_ITERS):
            image = coarse_apply(direction)
            alpha = norm_now / inner(direction, image)
            step = [alpha * d for d in direction]
            solution = step if solution is None else [x + d for x, d in zip(solution, step)]
            if sweep == COARSE_ITERS - 1:
                break
            residual = [x - alpha * d for x, d in zip(residual, image)]
            norm_next = inner(residual, residual)
            beta = norm_next / norm_now
            direction = [x + beta * d for x, d in zip(residual, direction)]
            norm_now = norm_next
        return solution

    def cycle(it, carry):
        first = SUBSTEPS + 2 * it
        second = first + 1
        pressure = pres[...]
        local = minus_laplace(pressure)
        work[first, 0] = local
        mixed = split(pressure * fields[1] + fields[2] * local)
        flat = right_dot(mixed, M_JYW).reshape(8, 16, 128)
        bent = right_dot(mixed, M_KY).reshape(8, 16, 128)
        for zi in range(4):
            edge = 0.5 * weighted(kz, zi, flat)
            body = weighted(wjz, zi, flat)
            if body is not None:
                edge = edge + 0.5 * weighted(wjz, zi, bent)
            for half in range(2):
                total = edge * spans[sub, 2 + half]
                if body is not None:
                    total = total + body * spans[sub, 4 + half]
                at = half * 4 + zi
                row = jnp.sum(total, axis=0, keepdims=True)
                g1[it, slot, at : at + 1, :] = csrc[at : at + 1, :] - row
        for copy in a_copies(it):
            copy.start()
        start_near(first, 1)

        for copy in a_copies(it):
            copy.wait_recv()
        tops = []
        for j in range(4):
            tops.append(g1[it, 4 * j] + g1[it, 4 * j + 1] + (g1[it, 4 * j + 2] + g1[it, 4 * j + 3]))
        odd_block = lax.rem(block, 2) == 1
        for half in range(2):
            total = None
            for j in range(4):
                shift = (j - 4 * half) % 8
                moved = pltpu.roll(tops[j], shift, 0) if shift else tops[j]
                moved = jnp.where((sublane >= j) & (sublane < j + 4), moved, 0.0)
                total = moved if total is None else total + moved
            total = jnp.where(odd_block, pltpu.roll(total, 3, 0), pltpu.roll(total, 7, 0))
            g2[it, block, half * 8 : half * 8 + 8, :] = total
        for copy in b_copies(it):
            copy.start()

        shared = finish_near(first, 1)[0]
        pressure = pressure + fields[2] * shared
        pres[...] = pressure
        work[second, 0] = minus_laplace(pressure)
        start_near(second, 1)

        for copy in b_copies(it):
            copy.wait_recv()
        right_side = []
        for half in range(2):
            at = slice(half * 8, half * 8 + 8)
            pieces = []
            for t in range(tiles):
                one = jnp.where(sublane < 6, g2[it, 2 * t, at, :], 0.0)
                one = one + jnp.where(sublane >= 3, g2[it, 2 * t + 1, at, :], 0.0)
                one = one + jnp.where(sublane == 7, g2[it, (2 * t + 2) % blocks, at, :], 0.0)
                one = one + jnp.where(sublane < 2, g2[it, (2 * t - 1) % blocks, at, :], 0.0)
                pieces.append(one)
            right_side.append(jnp.concatenate(pieces, axis=0))
        answer = conjugate(right_side)
        vertex = []
        for half in range(2):
            ext[half, 0:8] = answer[half][count - 8 : count]
            ext[half, 8 : 8 + count] = answer[half]
            ext[half, 8 + count : 16 + count] = answer[half][0:8]
            vertex.append([ext[half, pl.ds(elem + 7 + v, 1), :] for v in range(4)])

        interp, image = [], []
        for z in range(8):
            one, two = None, None
            for half in range(2):
                value = float(jz[z, 1]) * vertex[half][1] + float(jz[z, 2]) * vertex[half][2]
                part = value * spans[sub, half]
                one = part if one is None else one + part
                part = (float(waz[z]) * value) * spans[sub, 4 + half]
                if np.any(kz[z] != 0.0):
                    bend = None
                    for v in range(4):
                        if kz[z, v] != 0.0:
                            term = (0.5 * float(kz[z, v])) * vertex[half][v]
                            bend = term if bend is None else bend + term
                    part = part + bend * spans[sub, 2 + half]
                two = part if two is None else two + part
            interp.append(one)
            image.append(two)
        interp = split(jnp.concatenate(interp, axis=0))
        image = split(jnp.concatenate(image, axis=0))
        correction = right_dot(interp, M_JYT)
        applied = rows[2:3, :] * right_dot(image, M_JYT)
        applied = applied + fields[3] * right_dot(interp, M_KYT)
        shared = finish_near(second, 1)[0]
        pres[...] = pres[...] + correction + fields[2] * (shared - applied)
        return carry

    lax.fori_loop(0, MG_ITERS, cycle, 0)
    p_out[...] = pres[...].reshape(8, 16, 128)

    def drain_substep(i, carry):
        for copy in near_copies(i, 3):
            copy.wait_send()
        return carry

    lax.fori_loop(0, SUBSTEPS, drain_substep, 0)

    def drain_cycle(it, carry):
        for r in (SUBSTEPS + 2 * it, SUBSTEPS + 2 * it + 1):
            for copy in near_copies(r, 1):
                copy.wait_send()
        for copy in a_copies(it) + b_copies(it):
            copy.wait_send()
        return carry

    lax.fori_loop(0, MG_ITERS, drain_cycle, 0)


def solution(mesh):
    count = mesh.shape["elem"]
    matrices, fields, rows, spans, jz, kz, waz = make_tables()
    blocks = count // 4
    f32 = jnp.float32

    def shards(velocity):
        vmem = pl.BlockSpec(memory_space=pltpu.VMEM)
        return pl.pallas_call(
            functools.partial(kernel, (jz, kz, waz), count),
            out_shape=(
                jax.ShapeDtypeStruct((3, 8, 16, 128), f32),
                jax.ShapeDtypeStruct((8, 16, 128), f32),
            ),
            in_specs=[vmem] * 5,
            out_specs=(vmem, vmem),
            scratch_shapes=[
                pltpu.VMEM((3, 128, 128), f32),
                pltpu.VMEM((128, 128), f32),
                pltpu.VMEM((128, 128), f32),
                pltpu.VMEM((8, 128), f32),
                pltpu.VMEM((ROUNDS, 3, 128, 128), f32),
                pltpu.VMEM((3, 128, 128), f32),
                pltpu.VMEM((ROUNDS, 2, 3, 8, 128), f32),
                pltpu.VMEM((ROUNDS, 4, 8, 128), f32),
                pltpu.VMEM((ROUNDS, 2, 3, 16, 128), f32),
                pltpu.VMEM((ROUNDS, 2, 3, 8, 128), f32),
                pltpu.VMEM((ROUNDS, 4, 8, 128), f32),
                pltpu.VMEM((MG_ITERS, 16, 8, 128), f32),
                pltpu.VMEM((MG_ITERS, blocks, 16, 128), f32),
                pltpu.VMEM((2, count + 16, 128), f32),
                pltpu.SemaphoreType.DMA((ROUNDS, 8)),
                pltpu.SemaphoreType.DMA((ROUNDS, 8)),
                pltpu.SemaphoreType.DMA((MG_ITERS, 15)),
                pltpu.SemaphoreType.DMA((MG_ITERS, 15)),
                pltpu.SemaphoreType.DMA((MG_ITERS, blocks - 1)),
                pltpu.SemaphoreType.DMA((MG_ITERS, blocks - 1)),
            ],
            compiler_params=pltpu.CompilerParams(
                collective_id=0, has_side_effects=True, vmem_limit_bytes=32 * 1024 * 1024
            ),
        )(
            velocity,
            jnp.asarray(matrices),
            jnp.asarray(fields),
            jnp.asarray(rows),
            jnp.asarray(spans),
        )

    return jax.shard_map(
        shards,
        mesh=mesh,
        in_specs=(P(None, "elem", "sub", None),),
        out_specs=(P(None, "elem", "sub", None), P("elem", "sub", None)),
        check_vma=False,
    )
```

```python
import functools

import jax
import jax.numpy as jnp
import ml_dtypes
import numpy as np
from jax import lax
from jax.experimental import pallas as pl
from jax.experimental.pallas import tpu as pltpu
from jax.sharding import PartitionSpec as P

POINTS = 8
SUBSTEPS = 3
MG_ITERS = 3
COARSE_ITERS = 4

TIME_STEP = 0.005
SHIFT_COEF = 0.05
RELAXATION = 0.6
SOURCE_GAIN = 20.0

MESH = pl.DeviceIdType.MESH
ROUNDS = SUBSTEPS + 2 * MG_ITERS


def legendre_last(points, degree):
    previous = points * 0.0 + 1.0
    current = points + 0.0
    for level in range(2, degree + 1):
        following = ((2 * level - 1) * points * current - (level - 1) * previous) / level
        previous = current
        current = following
    return (previous, current)


def gll_tables(count):
    degree = count - 1
    points = -np.cos(np.pi * np.arange(count) / degree)
    for sweep in range(100):
        before_last, last_value = legendre_last(points, degree)
        points = points - (points * last_value - before_last) / (count * last_value)
    before_last, legendre = legendre_last(points, degree)
    weights = 2.0 / (degree * (degree + 1) * legendre**2)
    spacing = points[:, None] - points[None, :] + np.eye(count)
    matrix = legendre[:, None] / (legendre[None, :] * spacing) * (1.0 - np.eye(count))
    matrix[0, 0] = -degree * (degree + 1) / 4.0
    matrix[degree, degree] = degree * (degree + 1) / 4.0
    return (points, weights, matrix)


def assembled(values, walls):
    blocks = values.reshape(-1, POINTS)
    out = blocks.copy()
    out[:, 0] += blocks[:, -1]
    out[:, -1] += blocks[:, 0]
    if walls:
        out[0, 0] = blocks[0, 0]
        out[-1, -1] = blocks[-1, -1]
    return out.reshape(-1)


def coarse_tables(elements, lift, stiff, walls):
    count = elements * POINTS
    vertices = elements + 1
    interp = np.zeros((count, vertices + 2))
    slope = np.zeros((count, vertices + 2))
    edge = stiff @ lift
    for element in range(elements):
        for point in range(POINTS):
            row = element * POINTS + point
            pairs = [(element, point)]
            if point == 0 and not (walls and element == 0):
                pairs.append((element - 1, POINTS - 1))
            if point == POINTS - 1 and not (walls and element == elements - 1):
                pairs.append((element + 1, 0))
            for side in (0, 1):
                interp[row, element + side + 1] += lift[point, side]
                for other, at in pairs:
                    slope[row, other + side + 1] += edge[at, side]
    slope[np.abs(slope) < 1e-12] = 0.0
    return (interp[:, 1:-1], slope[:, 1:-1]) if walls else (interp, slope)


def halves(matrix):
    whole = np.asarray(matrix, np.float32)
    high = whole.astype(ml_dtypes.bfloat16)
    low = (whole - high.astype(np.float32)).astype(ml_dtypes.bfloat16)
    return np.stack([high, low])


def make_tables():
    points, weights, deriv = gll_tables(POINTS)
    stiff = deriv.T @ np.diag(weights) @ deriv
    scaled = np.diag(1.0 / weights) @ stiff
    squares = (deriv * deriv).T @ weights
    lift = np.stack([(1.0 - points) / 2.0, (1.0 + points) / 2.0], axis=1)
    kron, eye = np.kron, np.eye
    wz, wx, wy = weights, np.tile(weights, 2), np.tile(weights, 16)
    waz, wax, way = assembled(wz, False), assembled(wx, False), assembled(wy, True)
    saz = assembled(squares, False)
    sax = assembled(np.tile(squares, 2), False)
    say = assembled(np.tile(squares, 16), True)

    def outer(a, b, c):
        return kron(a, b)[:, None] * c[None, :]

    local = outer(wz, wx, wy) / 8.0
    mass = outer(waz, wax, way) / 8.0
    diagonal = 0.5 * (outer(saz, wax, way) + outer(waz, sax, way) + outer(waz, wax, say))
    diagonal = diagonal + SHIFT_COEF * mass
    jz, kz = coarse_tables(1, lift, stiff, False)
    jx, kx = coarse_tables(2, lift, stiff, False)
    jy, ky = coarse_tables(16, lift, stiff, True)

    def lanes(table):
        out = np.zeros((table.shape[0], 128))
        out[:, :68] = np.tile(table, (1, 4))
        return out

    left = kron(scaled, eye(16)) + kron(eye(8), kron(eye(2), scaled)) + SHIFT_COEF / 4.0 * eye(128)
    matrices = [
        kron(deriv, eye(16)),
        kron(eye(8), kron(eye(2), deriv)),
        kron(eye(16), deriv).T,
        left,
        kron(eye(16), scaled).T,
        lanes(way[:, None] * jy),
        lanes(ky),
        lanes(jy),
        lanes(jy).T,
        lanes(ky).T,
    ]
    matrices = np.stack([halves(one) for one in matrices])
    fields = np.stack(
        [
            4.0 * local,
            local / mass,
            RELAXATION / diagonal,
            0.5 * outer(waz, wax, np.ones(128)),
        ]
    ).astype(np.float32)
    lane = np.arange(128)
    inner = lane % POINTS
    level = lane % 17
    valid = lane < 68
    rows = np.zeros((8, 128), np.float32)
    rows[0] = (inner == 0) & (lane > 0)
    rows[1] = (inner == POINTS - 1) & (lane < 127)
    rows[2] = way
    rows[3] = np.where(valid, np.where((level == 0) | (level == 16), 1.0, 2.0), 0.0)
    rows[4] = valid & (level < 16)
    rows[5] = valid & (level > 0)
    kinds = [jx, wax[:, None] * jx, 0.5 * kx + SHIFT_COEF / 8.0 * wax[:, None] * jx]
    spans = np.zeros((4, 6, 16, 128), np.float32)
    for sub in range(4):
        for kind, table in enumerate(kinds):
            for half in range(2):
                for slot in range(4):
                    column = (2 * slot + half - 2 * sub + 1) % 8
                    if column < 5:
                        spans[sub, kind * 2 + half, :, slot * 17 : slot * 17 + 17] = table[
                            :, column : column + 1
                        ]
    return matrices, fields, rows, spans, jz, kz, waz


M_DZ, M_DX, M_DY, M_LEFT, M_RIGHT, M_JYW, M_KY, M_JY, M_JYT, M_KYT = range(10)


def kernel(
    zcoef,
    count,
    vel_in,
    mats_in,
    fields_in,
    rows_in,
    spans_in,
    adv_out,
    p_out,
    vel,
    mats,
    fields,
    rows,
    spans,
    sloc,
    pres,
    csrc,
    work,
    acc,
    xs,
    co,
    zr,
    xr,
    cr,
    g1,
    g2,
    ext,
    gauge,
    load,
    n_send,
    n_recv,
    a_send,
    a_recv,
    b_send,
    b_recv,
    known_side,
    known_row,
):
    jz, kz, waz = zcoef
    blocks = count // 4
    tiles = blocks // 2
    elem = lax.axis_index("elem")
    sub = lax.axis_index("sub")
    block = elem // 4
    place = elem % 4
    slot = place * 4 + sub

    def near(de, ds):
        return (lax.rem(elem + de + count, count), lax.rem(sub + ds + 4, 4))

    def at_block(dx, dz):
        bx, bz = block // 4, block % 4
        other = lax.rem(bx + dx, blocks // 4) * 4 + lax.rem(bz + dz, 4)
        return (other * 4 + place, sub)

    near_ids = [
        near(1, 1),
        near(1, -1),
        near(-1, 1),
        near(-1, -1),
        near(1, 0),
        near(-1, 0),
        near(0, 1),
        near(0, -1),
    ]
    a_ids = [
        (block * 4 + lax.rem(place + dj, 4), lax.rem(sub + ds, 4))
        for ds in (2, 1, 3, 0)
        for dj in (2, 1, 3, 0)
        if dj or ds
    ]
    b_ids = [
        at_block(dx, dz)
        for dz in (2, 1, 3, 0)
        for dx in (2, 1, 3, 0)
        if (dx or dz) and dx < blocks // 4
    ]
    row_ids = [at_block(dx, 0) for dx in range(1, blocks // 4)]
    side_ids = [at_block(0, 1), at_block(0, 3)]

    loads = [
        pltpu.make_async_copy(src, dst, load.at[k])
        for k, (src, dst) in enumerate(
            ((vel_in, vel), (mats_in, mats), (fields_in, fields), (rows_in, rows), (spans_in, spans))
        )
    ]
    for copy in loads:
        copy.start()
    barrier = pltpu.get_barrier_semaphore()
    partners = near_ids + side_ids + row_ids
    for one in partners:
        pl.semaphore_signal(barrier, inc=1, device_id=one, device_id_type=MESH)

    sublane = lax.broadcasted_iota(jnp.int32, (8, 128), 0)
    lane = lax.broadcasted_iota(jnp.int32, (1, 128), 1)
    low_lane = jnp.where((lane % 8 == 0) & (lane > 0), 1.0, 0.0)
    high_lane = jnp.where((lane % 8 == 7) & (lane < 127), 1.0, 0.0)

    def split(x):
        high = x.astype(jnp.bfloat16)
        return high, (x - high.astype(jnp.float32)).astype(jnp.bfloat16)

    def mul(a, b):
        return jnp.dot(a, b, preferred_element_type=jnp.float32)

    def left_dot(index, parts):
        high, low = parts
        return mul(mats[index, 0], high) + (mul(mats[index, 0], low) + mul(mats[index, 1], high))

    def right_dot(parts, index):
        high, low = parts
        return mul(high, mats[index, 0]) + (mul(low, mats[index, 0]) + mul(high, mats[index, 1]))

    def near_copies(r, comps):
        pairs = [
            (co.at[r, 0], cr.at[r, 0]),
            (co.at[r, 1], cr.at[r, 1]),
            (co.at[r, 2], cr.at[r, 2]),
            (co.at[r, 3], cr.at[r, 3]),
            (work.at[r, pl.ds(0, comps), pl.ds(112, 16)], zr.at[r, 0, pl.ds(0, comps)]),
            (work.at[r, pl.ds(0, comps), pl.ds(0, 16)], zr.at[r, 1, pl.ds(0, comps)]),
            (xs.at[r, 1, pl.ds(0, comps)], xr.at[r, 0, pl.ds(0, comps)]),
            (xs.at[r, 0, pl.ds(0, comps)], xr.at[r, 1, pl.ds(0, comps)]),
        ]
        return [
            pltpu.make_async_remote_copy(
                src_ref=src,
                dst_ref=dst,
                send_sem=n_send.at[r],
                recv_sem=n_recv.at[r],
                device_id=near_ids[k],
                device_id_type=MESH,
            )
            for k, (src, dst) in enumerate(pairs)
        ]

    def take(sem, count_rows):
        part = gauge.at[pl.ds(0, count_rows)]
        pltpu.make_async_copy(part, part, sem).wait()

    def near_rows(comps):
        return 32 + 48 * comps

    def start_near(r, comps):
        for corner, row in enumerate((127, 112, 15, 0)):
            tile = jnp.zeros((8, 128), jnp.float32)
            for c in range(comps):
                tile = jnp.where(sublane == c, work[r, c, row : row + 1, :], tile)
            co[r, corner] = tile
        for c in range(comps):
            xs[r, 0, c] = work[r, c, pl.ds(0, 8, stride=16), :]
            xs[r, 1, c] = work[r, c, pl.ds(15, 8, stride=16), :]
        for copy in near_copies(r, comps):
            copy.start()

    def share_y(field):
        return (
            field
            + low_lane * pltpu.roll(field, 1, 1)
            + high_lane * pltpu.roll(field, 127, 1)
        )

    def finish_near(r, comps):
        for c in range(comps):
            acc[c] = share_y(work[r, c])
            both = acc[c, pl.ds(7, 8, stride=16), :] + acc[c, pl.ds(8, 8, stride=16), :]
            acc[c, pl.ds(7, 8, stride=16), :] = both
            acc[c, pl.ds(8, 8, stride=16), :] = both
        take(n_recv.at[r], near_rows(comps))
        for c in range(comps):
            for side, row in ((0, 0), (1, 112)):
                first = zr[r, side, c, 0:8]
                second = zr[r, side, c, 8:16]
                both = share_y(first + jnp.where(sublane == 7, pltpu.roll(second, 7, 0), 0.0))
                acc[c, row : row + 8] = acc[c, row : row + 8] + both
                both = share_y(second + jnp.where(sublane == 0, pltpu.roll(first, 1, 0), 0.0))
                acc[c, row + 8 : row + 16] = acc[c, row + 8 : row + 16] + both
            for side, row in ((0, 0), (1, 15)):
                face = xr[r, side, c]
                face = face + jnp.where(sublane == 0, cr[r, side, c : c + 1, :], 0.0)
                face = face + jnp.where(sublane == 7, cr[r, 2 + side, c : c + 1, :], 0.0)
                acc[c, pl.ds(row, 8, stride=16), :] = acc[c, pl.ds(row, 8, stride=16), :] + share_y(face)

    def advect(i):
        parts = [split(vel[c]) for c in range(3)]
        for c in range(3):
            term = vel[0] * left_dot(M_DZ, parts[c])
            term = term + vel[1] * left_dot(M_DX, parts[c])
            term = term + vel[2] * right_dot(parts[c], M_DY)
            work[i, c] = term * ((2.0 * TIME_STEP) * fields[1])

    for copy in loads:
        copy.wait()
    advect(0)
    pl.semaphore_wait(barrier, len(partners))

    def pass_on(known, ids):
        for one in ids:
            pl.semaphore_signal(known, inc=1, device_id=one, device_id_type=MESH)
        pl.semaphore_wait(known, len(ids))

    def substep(i, carry):
        start_near(i, 3)

        @pl.when(i == 0)
        def _():
            pass_on(known_side, side_ids)

        @pl.when(i == 1)
        def _():
            pass_on(known_row, row_ids)

        finish_near(i, 3)
        for c in range(3):
            vel[c] = vel[c] - acc[c]

        @pl.when(i < SUBSTEPS - 1)
        def _():
            advect(i + 1)

        return carry

    lax.fori_loop(0, SUBSTEPS, substep, 0)

    for c in range(3):
        adv_out[c] = vel[c]
    divergence = left_dot(M_DZ, split(vel[0])) + left_dot(M_DX, split(vel[1]))
    divergence = divergence + right_dot(split(vel[2]), M_DY)
    source = (-SOURCE_GAIN / 4.0) * fields[0] * divergence
    sloc[...] = source
    pres[...] = jnp.zeros_like(source)
    direct = right_dot(split(source), M_JY).reshape(8, 16, 128)
    for half in range(2):
        span = spans[sub, half]
        for zi in range(4):
            total = None
            for z in range(8):
                if jz[z, zi] != 0.0:
                    one = float(jz[z, zi]) * direct[z]
                    total = one if total is None else total + one
            if total is None:
                row = jnp.zeros((1, 128), jnp.float32)
            else:
                row = jnp.sum(total * span, axis=0, keepdims=True)
            csrc[half * 4 + zi : half * 4 + zi + 1, :] = row

    def weighted(table, zi, field):
        total = None
        for z in range(8):
            if table[z, zi] != 0.0:
                one = float(table[z, zi]) * field[z]
                total = one if total is None else total + one
        return total

    wjz = waz[:, None] * jz

    def minus_laplace(field):
        parts = split(field)
        return sloc[...] - fields[0] * (left_dot(M_LEFT, parts) + right_dot(parts, M_RIGHT))

    a_rows = 8 * len(a_ids)
    b_rows = 16 * len(b_ids)

    def a_copies(it):
        return [
            pltpu.make_async_remote_copy(
                src_ref=g1.at[it, slot],
                dst_ref=g1.at[it, slot],
                send_sem=a_send.at[it],
                recv_sem=a_recv.at[it],
                device_id=one,
                device_id_type=MESH,
            )
            for one in a_ids
        ]

    def b_copies(it):
        return [
            pltpu.make_async_remote_copy(
                src_ref=g2.at[it, block],
                dst_ref=g2.at[it, block],
                send_sem=b_send.at[it],
                recv_sem=b_recv.at[it],
                device_id=one,
                device_id_type=MESH,
            )
            for one in b_ids
        ]

    def coarse_apply(pair):
        my, up, down = rows[3:4, :], rows[4:5, :], rows[5:6, :]
        even, odd = pair
        across = (
            odd + pltpu.roll(odd, 17, 1) + pltpu.roll(odd, 77, 1),
            even + pltpu.roll(even, 111, 1) + pltpu.roll(even, 51, 1),
        )
        out = []
        for u, near_x in zip(pair, across):
            near_z = pltpu.roll(u, 1, 0) + pltpu.roll(u, u.shape[0] - 1, 0)
            one = my * (3.025 * u - 0.5 * (near_z + near_x))
            out.append(one - up * pltpu.roll(u, 127, 1) - down * pltpu.roll(u, 1, 1))
        return out

    def inner(a, b):
        return jnp.sum(a[0] * b[0] + a[1] * b[1], keepdims=True)

    def conjugate(right_side):
        residual = right_side
        image = coarse_apply(residual)
        norm_now = inner(residual, residual)
        alpha = norm_now / inner(residual, image)
        direction, moved = residual, image
        solution = [alpha * d for d in direction]
        for sweep in range(1, COARSE_ITERS):
            residual = [x - alpha * d for x, d in zip(residual, moved)]
            image = coarse_apply(residual)
            norm_next = inner(residual, residual)
            energy = inner(residual, image)
            beta = norm_next / norm_now
            alpha = norm_next / (energy - beta * norm_next / alpha)
            direction = [x + beta * d for x, d in zip(residual, direction)]
            moved = [x + beta * d for x, d in zip(image, moved)]
            solution = [x + alpha * d for x, d in zip(solution, direction)]
            norm_now = norm_next
        return solution

    def cycle(it, carry):
        first = SUBSTEPS + 2 * it
        second = first + 1
        pressure = pres[...]
        local = minus_laplace(pressure)
        work[first, 0] = local
        mixed = split(pressure * fields[1] + fields[2] * local)
        flat = right_dot(mixed, M_JYW).reshape(8, 16, 128)
        bent = right_dot(mixed, M_KY).reshape(8, 16, 128)
        for zi in range(4):
            edge = 0.5 * weighted(kz, zi, flat)
            body = weighted(wjz, zi, flat)
            if body is not None:
                edge = edge + 0.5 * weighted(wjz, zi, bent)
            for half in range(2):
                total = edge * spans[sub, 2 + half]
                if body is not None:
                    total = total + body * spans[sub, 4 + half]
                at = half * 4 + zi
                row = jnp.sum(total, axis=0, keepdims=True)
                g1[it, slot, at : at + 1, :] = csrc[at : at + 1, :] - row
        for copy in a_copies(it):
            copy.start()
        start_near(first, 1)

        take(a_recv.at[it], a_rows)
        tops = []
        for j in range(4):
            tops.append(g1[it, 4 * j] + g1[it, 4 * j + 1] + (g1[it, 4 * j + 2] + g1[it, 4 * j + 3]))
        odd_block = lax.rem(block, 2) == 1
        for half in range(2):
            total = None
            for j in range(4):
                shift = (j - 4 * half) % 8
                moved = pltpu.roll(tops[j], shift, 0) if shift else tops[j]
                moved = jnp.where((sublane >= j) & (sublane < j + 4), moved, 0.0)
                total = moved if total is None else total + moved
            total = jnp.where(odd_block, pltpu.roll(total, 3, 0), pltpu.roll(total, 7, 0))
            g2[it, block, half * 8 : half * 8 + 8, :] = total
        for copy in b_copies(it):
            copy.start()

        finish_near(first, 1)
        pressure = pressure + fields[2] * acc[0]
        pres[...] = pressure
        work[second, 0] = minus_laplace(pressure)
        start_near(second, 1)

        take(b_recv.at[it], b_rows)
        right_side = []
        for half in range(2):
            at = slice(half * 8, half * 8 + 8)
            pieces = []
            for t in range(tiles):
                one = jnp.where(sublane < 6, g2[it, 2 * t, at, :], 0.0)
                one = one + jnp.where(sublane >= 3, g2[it, 2 * t + 1, at, :], 0.0)
                one = one + jnp.where(sublane == 7, g2[it, (2 * t + 2) % blocks, at, :], 0.0)
                one = one + jnp.where(sublane < 2, g2[it, (2 * t - 1) % blocks, at, :], 0.0)
                pieces.append(one)
            right_side.append(jnp.concatenate(pieces, axis=0))
        answer = conjugate(right_side)
        vertex = []
        for half in range(2):
            ext[half, 0:8] = answer[half][count - 8 : count]
            ext[half, 8 : 8 + count] = answer[half]
            ext[half, 8 + count : 16 + count] = answer[half][0:8]
            vertex.append([ext[half, pl.ds(elem + 7 + v, 1), :] for v in range(4)])

        interp, image = [], []
        for z in range(8):
            one, two = None, None
            for half in range(2):
                value = float(jz[z, 1]) * vertex[half][1] + float(jz[z, 2]) * vertex[half][2]
                part = value * spans[sub, half]
                one = part if one is None else one + part
                part = (float(waz[z]) * value) * spans[sub, 4 + half]
                if np.any(kz[z] != 0.0):
                    bend = None
                    for v in range(4):
                        if kz[z, v] != 0.0:
                            term = (0.5 * float(kz[z, v])) * vertex[half][v]
                            bend = term if bend is None else bend + term
                    part = part + bend * spans[sub, 2 + half]
                two = part if two is None else two + part
            interp.append(one)
            image.append(two)
        interp = split(jnp.concatenate(interp, axis=0))
        image = split(jnp.concatenate(image, axis=0))
        correction = right_dot(interp, M_JYT)
        applied = rows[2:3, :] * right_dot(image, M_JYT)
        applied = applied + fields[3] * right_dot(interp, M_KYT)
        finish_near(second, 1)
        pres[...] = pres[...] + correction + fields[2] * (acc[0] - applied)
        return carry

    lax.fori_loop(0, MG_ITERS, cycle, 0)
    p_out[...] = pres[...]

    for r in range(ROUNDS):
        take(n_send.at[r], near_rows(3 if r < SUBSTEPS else 1))
    for it in range(MG_ITERS):
        take(a_send.at[it], a_rows)
        take(b_send.at[it], b_rows)


def solution(mesh):
    count = mesh.shape["elem"]
    matrices, fields, rows, spans, jz, kz, waz = make_tables()
    blocks = count // 4
    f32 = jnp.float32

    def shards(velocity):
        vmem = pl.BlockSpec(memory_space=pltpu.VMEM)
        hbm = pl.BlockSpec(memory_space=pltpu.HBM)
        advected, pressure = pl.pallas_call(
            functools.partial(kernel, (jz, kz, waz), count),
            out_shape=(
                jax.ShapeDtypeStruct((3, 128, 128), f32),
                jax.ShapeDtypeStruct((128, 128), f32),
            ),
            in_specs=[hbm] * 5,
            out_specs=(vmem, vmem),
            scratch_shapes=[
                pltpu.VMEM((3, 128, 128), f32),
                pltpu.VMEM(matrices.shape, jnp.bfloat16),
                pltpu.VMEM(fields.shape, f32),
                pltpu.VMEM(rows.shape, f32),
                pltpu.VMEM(spans.shape, f32),
                pltpu.VMEM((128, 128), f32),
                pltpu.VMEM((128, 128), f32),
                pltpu.VMEM((8, 128), f32),
                pltpu.VMEM((ROUNDS, 3, 128, 128), f32),
                pltpu.VMEM((3, 128, 128), f32),
                pltpu.VMEM((ROUNDS, 2, 3, 8, 128), f32),
                pltpu.VMEM((ROUNDS, 4, 8, 128), f32),
                pltpu.VMEM((ROUNDS, 2, 3, 16, 128), f32),
                pltpu.VMEM((ROUNDS, 2, 3, 8, 128), f32),
                pltpu.VMEM((ROUNDS, 4, 8, 128), f32),
                pltpu.VMEM((MG_ITERS, 16, 8, 128), f32),
                pltpu.VMEM((MG_ITERS, blocks, 16, 128), f32),
                pltpu.VMEM((2, count + 16, 128), f32),
                pltpu.VMEM((240, 128), f32),
                pltpu.SemaphoreType.DMA((5,)),
                pltpu.SemaphoreType.DMA((ROUNDS,)),
                pltpu.SemaphoreType.DMA((ROUNDS,)),
                pltpu.SemaphoreType.DMA((MG_ITERS,)),
                pltpu.SemaphoreType.DMA((MG_ITERS,)),
                pltpu.SemaphoreType.DMA((MG_ITERS,)),
                pltpu.SemaphoreType.DMA((MG_ITERS,)),
                pltpu.SemaphoreType.REGULAR,
                pltpu.SemaphoreType.REGULAR,
            ],
            compiler_params=pltpu.CompilerParams(
                collective_id=0, has_side_effects=True, vmem_limit_bytes=32 * 1024 * 1024
            ),
        )(
            velocity.reshape(3, 128, 128),
            jnp.asarray(matrices),
            jnp.asarray(fields),
            jnp.asarray(rows),
            jnp.asarray(spans),
        )
        return advected.reshape(3, 8, 16, 128), pressure.reshape(8, 16, 128)

    return jax.shard_map(
        shards,
        mesh=mesh,
        in_specs=(P(None, "elem", "sub", None),),
        out_specs=(P(None, "elem", "sub", None), P("elem", "sub", None)),
        check_vma=False,
    )
```

```python
import functools

import jax
import jax.numpy as jnp
import ml_dtypes
import numpy as np
from jax import lax
from jax.experimental import pallas as pl
from jax.experimental.pallas import tpu as pltpu
from jax.sharding import PartitionSpec as P

POINTS = 8
SUBSTEPS = 3
MG_ITERS = 3
COARSE_ITERS = 4

TIME_STEP = 0.005
SHIFT_COEF = 0.05
RELAXATION = 0.6
SOURCE_GAIN = 20.0

MESH = pl.DeviceIdType.MESH
ROUNDS = SUBSTEPS + 2 * MG_ITERS
WALL_LANES = [95, 111, 127, 94, 110]


def legendre_last(points, degree):
    previous = points * 0.0 + 1.0
    current = points + 0.0
    for level in range(2, degree + 1):
        following = ((2 * level - 1) * points * current - (level - 1) * previous) / level
        previous = current
        current = following
    return (previous, current)


def gll_tables(count):
    degree = count - 1
    points = -np.cos(np.pi * np.arange(count) / degree)
    for sweep in range(100):
        before_last, last_value = legendre_last(points, degree)
        points = points - (points * last_value - before_last) / (count * last_value)
    before_last, legendre = legendre_last(points, degree)
    weights = 2.0 / (degree * (degree + 1) * legendre**2)
    spacing = points[:, None] - points[None, :] + np.eye(count)
    matrix = legendre[:, None] / (legendre[None, :] * spacing) * (1.0 - np.eye(count))
    matrix[0, 0] = -degree * (degree + 1) / 4.0
    matrix[degree, degree] = degree * (degree + 1) / 4.0
    return (points, weights, matrix)


def assembled(values, walls):
    blocks = values.reshape(-1, POINTS)
    out = blocks.copy()
    out[:, 0] += blocks[:, -1]
    out[:, -1] += blocks[:, 0]
    if walls:
        out[0, 0] = blocks[0, 0]
        out[-1, -1] = blocks[-1, -1]
    return out.reshape(-1)


def coarse_tables(elements, lift, stiff, walls):
    count = elements * POINTS
    vertices = elements + 1
    interp = np.zeros((count, vertices + 2))
    slope = np.zeros((count, vertices + 2))
    edge = stiff @ lift
    for element in range(elements):
        for point in range(POINTS):
            row = element * POINTS + point
            pairs = [(element, point)]
            if point == 0 and not (walls and element == 0):
                pairs.append((element - 1, POINTS - 1))
            if point == POINTS - 1 and not (walls and element == elements - 1):
                pairs.append((element + 1, 0))
            for side in (0, 1):
                interp[row, element + side + 1] += lift[point, side]
                for other, at in pairs:
                    slope[row, other + side + 1] += edge[at, side]
    slope[np.abs(slope) < 1e-12] = 0.0
    return (interp[:, 1:-1], slope[:, 1:-1]) if walls else (interp, slope)


def halves(matrix):
    whole = np.asarray(matrix, np.float32)
    high = whole.astype(ml_dtypes.bfloat16)
    low = (whole - high.astype(np.float32)).astype(ml_dtypes.bfloat16)
    return np.stack([high, low])


def make_tables():
    points, weights, deriv = gll_tables(POINTS)
    stiff = deriv.T @ np.diag(weights) @ deriv
    scaled = np.diag(1.0 / weights) @ stiff
    squares = (deriv * deriv).T @ weights
    lift = np.stack([(1.0 - points) / 2.0, (1.0 + points) / 2.0], axis=1)
    kron, eye = np.kron, np.eye
    wz, wx, wy = weights, np.tile(weights, 2), np.tile(weights, 16)
    waz, wax, way = assembled(wz, False), assembled(wx, False), assembled(wy, True)
    saz = assembled(squares, False)
    sax = assembled(np.tile(squares, 2), False)
    say = assembled(np.tile(squares, 16), True)

    def outer(a, b, c):
        return kron(a, b)[:, None] * c[None, :]

    local = outer(wz, wx, wy) / 8.0
    mass = outer(waz, wax, way) / 8.0
    diagonal = 0.5 * (outer(saz, wax, way) + outer(waz, sax, way) + outer(waz, wax, say))
    diagonal = diagonal + SHIFT_COEF * mass
    jz, kz = coarse_tables(1, lift, stiff, False)
    jx, kx = coarse_tables(2, lift, stiff, False)
    jy, ky = coarse_tables(16, lift, stiff, True)

    def lanes(table):
        out = np.zeros((table.shape[0], 128))
        out[:, :80] = np.tile(table[:, :16], (1, 5))
        out[:, WALL_LANES] = table[:, 16:17]
        return out

    def across(table):
        out = np.zeros((table.shape[0], 128))
        out[:, :80] = np.repeat(table, 16, axis=1)
        out[:, WALL_LANES] = table
        return out

    left = kron(scaled, eye(16)) + kron(eye(8), kron(eye(2), scaled)) + SHIFT_COEF / 4.0 * eye(128)
    matrices = [
        kron(deriv, eye(16)),
        kron(eye(8), kron(eye(2), deriv)),
        kron(eye(16), deriv).T,
        left,
        kron(eye(16), scaled).T,
        lanes(way[:, None] * jy),
        lanes(ky),
        lanes(jy),
        lanes(jy).T,
        lanes(ky).T,
    ]
    matrices = np.stack([halves(one) for one in matrices])
    fields = np.stack(
        [
            4.0 * local,
            local / mass,
            RELAXATION / diagonal,
            0.5 * outer(waz, wax, np.ones(128)),
        ]
    ).astype(np.float32)
    lane = np.arange(128)
    level = lane % 16
    rows = np.zeros((32, 128), np.float32)
    rows[0] = way
    rows[1] = np.where(level == 0, 1.0, 2.0)
    rows[2] = level < 15
    rows[3] = level > 0
    rows[4] = level == 15
    for k in range(5):
        spot = lane if k == 4 else (lane - 32 * k + 16) % 128
        rows[8 + 3 * k] = spot < 80
        rows[9 + 3 * k] = (spot >= 80) & (spot % 16 == 15)
        rows[10 + 3 * k] = (spot >= 80) & (spot < 112) & (spot % 16 == 14)
    kinds = [jx, wax[:, None] * jx, 0.5 * kx + SHIFT_COEF / 8.0 * wax[:, None] * jx]
    spans = np.stack([across(one) for one in kinds]).astype(np.float32)
    return matrices, fields, rows, spans, jz, kz, waz


M_DZ, M_DX, M_DY, M_LEFT, M_RIGHT, M_JYW, M_KY, M_JY, M_JYT, M_KYT = range(10)


def kernel(
    zcoef,
    count,
    vel_in,
    mats_in,
    fields_in,
    rows_in,
    spans_in,
    adv_out,
    p_out,
    vel,
    mats,
    fields,
    rows,
    spans,
    sloc,
    pres,
    csrc,
    work,
    acc,
    xs,
    co,
    zr,
    xr,
    cr,
    g1,
    g2,
    ext,
    gauge,
    load,
    n_send,
    n_recv,
    a_send,
    a_recv,
    b_send,
    b_recv,
    known_side,
    known_row,
):
    jz, kz, waz = zcoef
    planes = count // 16
    elem = lax.axis_index("elem")
    sub = lax.axis_index("sub")
    plane = elem // 16
    place = elem % 16
    slot = plane * 4 + sub
    turn = lax.rem(32 * sub + 112, 128)

    def near(de, ds):
        return (lax.rem(elem + de + count, count), lax.rem(sub + ds + 4, 4))

    def along(dj):
        return (plane * 16 + lax.rem(place + dj, 16), sub)

    def over(dx, ds):
        return (lax.rem(plane + dx, planes) * 16 + place, lax.rem(sub + ds, 4))

    near_ids = [
        near(1, 1),
        near(1, -1),
        near(-1, 1),
        near(-1, -1),
        near(1, 0),
        near(-1, 0),
        near(0, 1),
        near(0, -1),
    ]
    a_ids = [along(dj) for dj in sorted(range(1, 16), key=lambda d: -min(d, 16 - d))]
    steps = [(dx, ds) for dx in range(planes) for ds in range(4) if dx or ds]
    steps = sorted(steps, key=lambda d: -(min(d[0], planes - d[0]) + min(d[1], 4 - d[1])))
    b_ids = [over(dx, ds) for dx, ds in steps]
    side_ids = [along(4), along(12)]
    row_ids = [over(dx, 0) for dx in range(1, planes)]

    loads = [
        pltpu.make_async_copy(src, dst, load.at[k])
        for k, (src, dst) in enumerate(
            ((vel_in, vel), (mats_in, mats), (fields_in, fields), (rows_in, rows), (spans_in, spans))
        )
    ]
    for copy in loads:
        copy.start()
    barrier = pltpu.get_barrier_semaphore()
    partners = near_ids + side_ids + [along(2), along(14)] + row_ids
    for one in partners:
        pl.semaphore_signal(barrier, inc=1, device_id=one, device_id_type=MESH)

    sublane = lax.broadcasted_iota(jnp.int32, (8, 128), 0)
    lane = lax.broadcasted_iota(jnp.int32, (1, 128), 1)
    low_lane = jnp.where((lane % 8 == 0) & (lane > 0), 1.0, 0.0)
    high_lane = jnp.where((lane % 8 == 7) & (lane < 127), 1.0, 0.0)

    def split(x):
        high = x.astype(jnp.bfloat16)
        return high, (x - high.astype(jnp.float32)).astype(jnp.bfloat16)

    def mul(a, b):
        return jnp.dot(a, b, preferred_element_type=jnp.float32)

    def left_dot(index, parts):
        high, low = parts
        return mul(mats[index, 0], high) + (mul(mats[index, 0], low) + mul(mats[index, 1], high))

    def right_dot(parts, index):
        high, low = parts
        return mul(high, mats[index, 0]) + (mul(low, mats[index, 0]) + mul(high, mats[index, 1]))

    def near_copies(r, comps):
        pairs = [
            (co.at[r, 0], cr.at[r, 0]),
            (co.at[r, 1], cr.at[r, 1]),
            (co.at[r, 2], cr.at[r, 2]),
            (co.at[r, 3], cr.at[r, 3]),
            (work.at[r, pl.ds(0, comps), pl.ds(112, 16)], zr.at[r, 0, pl.ds(0, comps)]),
            (work.at[r, pl.ds(0, comps), pl.ds(0, 16)], zr.at[r, 1, pl.ds(0, comps)]),
            (xs.at[r, 1, pl.ds(0, comps)], xr.at[r, 0, pl.ds(0, comps)]),
            (xs.at[r, 0, pl.ds(0, comps)], xr.at[r, 1, pl.ds(0, comps)]),
        ]
        return [
            pltpu.make_async_remote_copy(
                src_ref=src,
                dst_ref=dst,
                send_sem=n_send.at[r],
                recv_sem=n_recv.at[r],
                device_id=near_ids[k],
                device_id_type=MESH,
            )
            for k, (src, dst) in enumerate(pairs)
        ]

    def take(sem, count_rows):
        part = gauge.at[pl.ds(0, count_rows)]
        pltpu.make_async_copy(part, part, sem).wait()

    def near_rows(comps):
        return 32 + 48 * comps

    def start_near(r, comps):
        for corner, row in enumerate((127, 112, 15, 0)):
            tile = jnp.zeros((8, 128), jnp.float32)
            for c in range(comps):
                tile = jnp.where(sublane == c, work[r, c, row : row + 1, :], tile)
            co[r, corner] = tile
        for c in range(comps):
            xs[r, 0, c] = work[r, c, pl.ds(0, 8, stride=16), :]
            xs[r, 1, c] = work[r, c, pl.ds(15, 8, stride=16), :]
        for copy in near_copies(r, comps):
            copy.start()

    def share_y(field):
        return (
            field
            + low_lane * pltpu.roll(field, 1, 1)
            + high_lane * pltpu.roll(field, 127, 1)
        )

    def finish_near(r, comps):
        for c in range(comps):
            acc[c] = share_y(work[r, c])
            both = acc[c, pl.ds(7, 8, stride=16), :] + acc[c, pl.ds(8, 8, stride=16), :]
            acc[c, pl.ds(7, 8, stride=16), :] = both
            acc[c, pl.ds(8, 8, stride=16), :] = both
        take(n_recv.at[r], near_rows(comps))
        for c in range(comps):
            for side, row in ((0, 0), (1, 112)):
                first = zr[r, side, c, 0:8]
                second = zr[r, side, c, 8:16]
                both = share_y(first + jnp.where(sublane == 7, pltpu.roll(second, 7, 0), 0.0))
                acc[c, row : row + 8] = acc[c, row : row + 8] + both
                both = share_y(second + jnp.where(sublane == 0, pltpu.roll(first, 1, 0), 0.0))
                acc[c, row + 8 : row + 16] = acc[c, row + 8 : row + 16] + both
            for side, row in ((0, 0), (1, 15)):
                face = xr[r, side, c]
                face = face + jnp.where(sublane == 0, cr[r, side, c : c + 1, :], 0.0)
                face = face + jnp.where(sublane == 7, cr[r, 2 + side, c : c + 1, :], 0.0)
                acc[c, pl.ds(row, 8, stride=16), :] = acc[c, pl.ds(row, 8, stride=16), :] + share_y(face)

    def advect(i):
        parts = [split(vel[c]) for c in range(3)]
        for c in range(3):
            term = vel[0] * left_dot(M_DZ, parts[c])
            term = term + vel[1] * left_dot(M_DX, parts[c])
            term = term + vel[2] * right_dot(parts[c], M_DY)
            work[i, c] = term * ((2.0 * TIME_STEP) * fields[1])

    for copy in loads:
        copy.wait()
    advect(0)
    pl.semaphore_wait(barrier, len(partners))

    def pass_on(known, ids):
        for one in ids:
            pl.semaphore_signal(known, inc=1, device_id=one, device_id_type=MESH)
        pl.semaphore_wait(known, len(ids))

    def substep(i, carry):
        start_near(i, 3)

        @pl.when(i == 0)
        def _():
            pass_on(known_side, side_ids)

        @pl.when(i == 1)
        def _():
            pass_on(known_row, row_ids)

        finish_near(i, 3)
        for c in range(3):
            vel[c] = vel[c] - acc[c]

        @pl.when(i < SUBSTEPS - 1)
        def _():
            advect(i + 1)

        return carry

    lax.fori_loop(0, SUBSTEPS, substep, 0)

    for c in range(3):
        adv_out[c] = vel[c]
    def weighted(table, zi, field):
        total = None
        for z in range(8):
            if table[z, zi] != 0.0:
                one = float(table[z, zi]) * field[z]
                total = one if total is None else total + one
        return total

    divergence = left_dot(M_DZ, split(vel[0])) + left_dot(M_DX, split(vel[1]))
    divergence = divergence + right_dot(split(vel[2]), M_DY)
    source = (-SOURCE_GAIN / 4.0) * fields[0] * divergence
    sloc[...] = source
    pres[...] = jnp.zeros_like(source)
    direct = right_dot(split(source), M_JY).reshape(8, 16, 128)
    for zi in (1, 2):
        row = jnp.sum(weighted(jz, zi, direct) * spans[0], axis=0, keepdims=True)
        csrc[zi : zi + 1, :] = row

    wjz = waz[:, None] * jz

    def minus_laplace(field):
        parts = split(field)
        return sloc[...] - fields[0] * (left_dot(M_LEFT, parts) + right_dot(parts, M_RIGHT))

    a_rows = 8 * len(a_ids)
    b_rows = 24 * len(b_ids)

    def a_copies(it):
        return [
            pltpu.make_async_remote_copy(
                src_ref=g1.at[it, place],
                dst_ref=g1.at[it, place],
                send_sem=a_send.at[it],
                recv_sem=a_recv.at[it],
                device_id=one,
                device_id_type=MESH,
            )
            for one in a_ids
        ]

    def b_copies(it):
        return [
            pltpu.make_async_remote_copy(
                src_ref=g2.at[it, slot],
                dst_ref=g2.at[it, slot],
                send_sem=b_send.at[it],
                recv_sem=b_recv.at[it],
                device_id=one,
                device_id_type=MESH,
            )
            for one in b_ids
        ]

    def coarse_apply(pair):
        my, up, down, top = rows[1:2, :], rows[2:3, :], rows[3:4, :], rows[4:5, :]

        def middle(u):
            near_x = pltpu.roll(u, 16, 1) + pltpu.roll(u, 112, 1)
            near_z = pltpu.roll(u, 1, 0) + pltpu.roll(u, count - 1, 0)
            return 3.025 * u - 0.5 * (near_z + near_x)

        u, wall = pair
        body = my * middle(u) - up * pltpu.roll(u, 127, 1) - down * pltpu.roll(u, 1, 1)
        return [body - top * wall, top * (middle(wall) - u)]

    def inner(a, b):
        return jnp.sum(a[0] * b[0] + a[1] * b[1], keepdims=True)

    def conjugate(right_side):
        residual = right_side
        image = coarse_apply(residual)
        norm_now = inner(residual, residual)
        alpha = norm_now / inner(residual, image)
        direction, moved = residual, image
        solution = [alpha * d for d in direction]
        for sweep in range(1, COARSE_ITERS):
            residual = [x - alpha * d for x, d in zip(residual, moved)]
            image = coarse_apply(residual)
            norm_next = inner(residual, residual)
            energy = inner(residual, image)
            beta = norm_next / norm_now
            alpha = norm_next / (energy - beta * norm_next / alpha)
            direction = [x + beta * d for x, d in zip(residual, direction)]
            moved = [x + beta * d for x, d in zip(image, moved)]
            solution = [x + alpha * d for x, d in zip(solution, direction)]
            norm_now = norm_next
        return solution

    def cycle(it, carry):
        first = SUBSTEPS + 2 * it
        second = first + 1
        pressure = pres[...]
        local = minus_laplace(pressure)
        work[first, 0] = local
        mixed = split(pressure * fields[1] + fields[2] * local)
        flat = right_dot(mixed, M_JYW).reshape(8, 16, 128)
        bent = right_dot(mixed, M_KY).reshape(8, 16, 128)
        tile = jnp.zeros((8, 128), jnp.float32)
        for zi in range(4):
            total = (0.5 * weighted(kz, zi, flat)) * spans[1]
            if zi in (1, 2):
                total = total + (0.5 * weighted(wjz, zi, bent)) * spans[1]
                total = total + weighted(wjz, zi, flat) * spans[2]
            row = -jnp.sum(total, axis=0, keepdims=True)
            if zi in (1, 2):
                row = csrc[zi : zi + 1, :] + row
            tile = jnp.where(sublane == lax.rem(place + zi + 7, 8), row, tile)
        g1[it, place] = tile
        for copy in a_copies(it):
            copy.start()
        start_near(first, 1)

        take(a_recv.at[it], a_rows)
        lower, upper = sublane < 4, sublane >= 4

        def some(mask, x):
            return jnp.where(mask, x, 0.0)

        first_edge = g1[it, 6] + g1[it, 7] + g1[it, 8]
        last_edge = g1[it, 14] + g1[it, 15]
        base = g1[it, 0]
        tops = [
            (g1[it, 1] + g1[it, 2]) + (g1[it, 3] + g1[it, 4]) + (g1[it, 5] + some(lower, base))
            + some(upper, first_edge),
            (g1[it, 9] + g1[it, 10]) + (g1[it, 11] + g1[it, 12]) + g1[it, 13]
            + (some(lower, first_edge) + some(upper, last_edge)),
            some(lower, last_edge) + some(upper, base),
        ]
        for k in range(3):
            g2[it, slot, 8 * k : 8 * k + 8, :] = pltpu.roll(tops[k], turn, 1)
        for copy in b_copies(it):
            copy.start()

        finish_near(first, 1)
        pressure = pressure + fields[2] * acc[0]
        pres[...] = pressure
        work[second, 0] = minus_laplace(pressure)
        start_near(second, 1)

        take(b_recv.at[it], b_rows)
        pieces, walls = [], []
        for x in range(planes):
            before, after = (x - 1) % planes, (x + 1) % planes
            for k in range(2):
                sums = [None] * 3
                for sy in range(4):
                    one = g2[it, 4 * x + sy, 8 * k : 8 * k + 8, :]
                    if k == 0:
                        one = one + some(lower, g2[it, 4 * before + sy, 16:24, :])
                    else:
                        one = one + some(upper, g2[it, 4 * after + sy, 16:24, :])
                    for n in range(3):
                        at = 8 + 3 * sy + n
                        part = one * rows[at : at + 1, :]
                        sums[n] = part if sums[n] is None else sums[n] + part
                pieces.append(sums[0])
                walls.append(pltpu.roll(sums[1], 48, 1) + pltpu.roll(sums[2], 97, 1))
        right_side = [jnp.concatenate(pieces, axis=0), jnp.concatenate(walls, axis=0)]
        answer = conjugate(right_side)
        for half in range(2):
            ext[half, 0:8] = answer[half][count - 8 : count]
            ext[half, 8 : 8 + count] = answer[half]
            ext[half, 8 + count : 16 + count] = answer[half][0:8]
        body = ext[0, pl.ds(elem + 7, 8), :]
        wall = ext[1, pl.ds(elem + 7, 8), :]
        own = rows[20:21, :] * pltpu.roll(body, lax.rem(256 - turn, 128), 1)
        own = own + rows[21:22, :] * pltpu.roll(wall, lax.rem(208 - turn, 128), 1)
        own = own + rows[22:23, :] * pltpu.roll(wall, lax.rem(159 - turn, 128), 1)
        vertex = [own[v : v + 1, :] for v in range(4)]

        interp, image = [], []
        for z in range(8):
            value = float(jz[z, 1]) * vertex[1] + float(jz[z, 2]) * vertex[2]
            interp.append(value * spans[0])
            part = (float(waz[z]) * value) * spans[2]
            if np.any(kz[z] != 0.0):
                bend = None
                for v in range(4):
                    if kz[z, v] != 0.0:
                        term = (0.5 * float(kz[z, v])) * vertex[v]
                        bend = term if bend is None else bend + term
                part = part + bend * spans[1]
            image.append(part)
        interp = split(jnp.concatenate(interp, axis=0))
        image = split(jnp.concatenate(image, axis=0))
        correction = right_dot(interp, M_JYT)
        applied = rows[0:1, :] * right_dot(image, M_JYT)
        applied = applied + fields[3] * right_dot(interp, M_KYT)
        finish_near(second, 1)
        pres[...] = pres[...] + correction + fields[2] * (acc[0] - applied)
        return carry

    lax.fori_loop(0, MG_ITERS, cycle, 0)
    p_out[...] = pres[...]

    for r in range(ROUNDS):
        take(n_send.at[r], near_rows(3 if r < SUBSTEPS else 1))
    for it in range(MG_ITERS):
        take(a_send.at[it], a_rows)
        take(b_send.at[it], b_rows)


def solution(mesh):
    count = mesh.shape["elem"]
    matrices, fields, rows, spans, jz, kz, waz = make_tables()
    planes = count // 16
    f32 = jnp.float32

    def shards(velocity):
        vmem = pl.BlockSpec(memory_space=pltpu.VMEM)
        hbm = pl.BlockSpec(memory_space=pltpu.HBM)
        advected, pressure = pl.pallas_call(
            functools.partial(kernel, (jz, kz, waz), count),
            out_shape=(
                jax.ShapeDtypeStruct((3, 128, 128), f32),
                jax.ShapeDtypeStruct((128, 128), f32),
            ),
            in_specs=[hbm] * 5,
            out_specs=(vmem, vmem),
            scratch_shapes=[
                pltpu.VMEM((3, 128, 128), f32),
                pltpu.VMEM(matrices.shape, jnp.bfloat16),
                pltpu.VMEM(fields.shape, f32),
                pltpu.VMEM(rows.shape, f32),
                pltpu.VMEM(spans.shape, f32),
                pltpu.VMEM((128, 128), f32),
                pltpu.VMEM((128, 128), f32),
                pltpu.VMEM((8, 128), f32),
                pltpu.VMEM((ROUNDS, 3, 128, 128), f32),
                pltpu.VMEM((3, 128, 128), f32),
                pltpu.VMEM((ROUNDS, 2, 3, 8, 128), f32),
                pltpu.VMEM((ROUNDS, 4, 8, 128), f32),
                pltpu.VMEM((ROUNDS, 2, 3, 16, 128), f32),
                pltpu.VMEM((ROUNDS, 2, 3, 8, 128), f32),
                pltpu.VMEM((ROUNDS, 4, 8, 128), f32),
                pltpu.VMEM((MG_ITERS, 16, 8, 128), f32),
                pltpu.VMEM((MG_ITERS, 4 * planes, 24, 128), f32),
                pltpu.VMEM((2, count + 16, 128), f32),
                pltpu.VMEM((360, 128), f32),
                pltpu.SemaphoreType.DMA((5,)),
                pltpu.SemaphoreType.DMA((ROUNDS,)),
                pltpu.SemaphoreType.DMA((ROUNDS,)),
                pltpu.SemaphoreType.DMA((MG_ITERS,)),
                pltpu.SemaphoreType.DMA((MG_ITERS,)),
                pltpu.SemaphoreType.DMA((MG_ITERS,)),
                pltpu.SemaphoreType.DMA((MG_ITERS,)),
                pltpu.SemaphoreType.REGULAR,
                pltpu.SemaphoreType.REGULAR,
            ],
            compiler_params=pltpu.CompilerParams(
                collective_id=0, has_side_effects=True, vmem_limit_bytes=60 * 1024 * 1024
            ),
        )(
            velocity.reshape(3, 128, 128),
            jnp.asarray(matrices),
            jnp.asarray(fields),
            jnp.asarray(rows),
            jnp.asarray(spans),
        )
        return advected.reshape(3, 8, 16, 128), pressure.reshape(8, 16, 128)

    return jax.shard_map(
        shards,
        mesh=mesh,
        in_specs=(P(None, "elem", "sub", None),),
        out_specs=(P(None, "elem", "sub", None), P("elem", "sub", None)),
        check_vma=False,
    )
```

```python
import functools

import jax
import jax.numpy as jnp
import ml_dtypes
import numpy as np
from jax import lax
from jax.experimental import pallas as pl
from jax.experimental.pallas import tpu as pltpu
from jax.sharding import PartitionSpec as P

POINTS = 8
SUBSTEPS = 3
MG_ITERS = 3
COARSE_ITERS = 4

TIME_STEP = 0.005
SHIFT_COEF = 0.05
RELAXATION = 0.6
SOURCE_GAIN = 20.0

MESH = pl.DeviceIdType.MESH
ROUNDS = SUBSTEPS + 2 * MG_ITERS
WALL_LANES = [95, 111, 127, 94, 110]


def legendre_last(points, degree):
    previous = points * 0.0 + 1.0
    current = points + 0.0
    for level in range(2, degree + 1):
        following = ((2 * level - 1) * points * current - (level - 1) * previous) / level
        previous = current
        current = following
    return (previous, current)


def gll_tables(count):
    degree = count - 1
    points = -np.cos(np.pi * np.arange(count) / degree)
    for sweep in range(100):
        before_last, last_value = legendre_last(points, degree)
        points = points - (points * last_value - before_last) / (count * last_value)
    before_last, legendre = legendre_last(points, degree)
    weights = 2.0 / (degree * (degree + 1) * legendre**2)
    spacing = points[:, None] - points[None, :] + np.eye(count)
    matrix = legendre[:, None] / (legendre[None, :] * spacing) * (1.0 - np.eye(count))
    matrix[0, 0] = -degree * (degree + 1) / 4.0
    matrix[degree, degree] = degree * (degree + 1) / 4.0
    return (points, weights, matrix)


def assembled(values, walls):
    blocks = values.reshape(-1, POINTS)
    out = blocks.copy()
    out[:, 0] += blocks[:, -1]
    out[:, -1] += blocks[:, 0]
    if walls:
        out[0, 0] = blocks[0, 0]
        out[-1, -1] = blocks[-1, -1]
    return out.reshape(-1)


def coarse_tables(elements, lift, stiff, walls):
    count = elements * POINTS
    vertices = elements + 1
    interp = np.zeros((count, vertices + 2))
    slope = np.zeros((count, vertices + 2))
    edge = stiff @ lift
    for element in range(elements):
        for point in range(POINTS):
            row = element * POINTS + point
            pairs = [(element, point)]
            if point == 0 and not (walls and element == 0):
                pairs.append((element - 1, POINTS - 1))
            if point == POINTS - 1 and not (walls and element == elements - 1):
                pairs.append((element + 1, 0))
            for side in (0, 1):
                interp[row, element + side + 1] += lift[point, side]
                for other, at in pairs:
                    slope[row, other + side + 1] += edge[at, side]
    slope[np.abs(slope) < 1e-12] = 0.0
    return (interp[:, 1:-1], slope[:, 1:-1]) if walls else (interp, slope)


def halves(matrix):
    whole = np.asarray(matrix, np.float32)
    high = whole.astype(ml_dtypes.bfloat16)
    low = (whole - high.astype(np.float32)).astype(ml_dtypes.bfloat16)
    return np.stack([high, low])


def make_tables():
    points, weights, deriv = gll_tables(POINTS)
    stiff = deriv.T @ np.diag(weights) @ deriv
    scaled = np.diag(1.0 / weights) @ stiff
    squares = (deriv * deriv).T @ weights
    lift = np.stack([(1.0 - points) / 2.0, (1.0 + points) / 2.0], axis=1)
    kron, eye = np.kron, np.eye
    wz, wx, wy = weights, np.tile(weights, 2), np.tile(weights, 16)
    waz, wax, way = assembled(wz, False), assembled(wx, False), assembled(wy, True)
    saz = assembled(squares, False)
    sax = assembled(np.tile(squares, 2), False)
    say = assembled(np.tile(squares, 16), True)

    def outer(a, b, c):
        return kron(a, b)[:, None] * c[None, :]

    local = outer(wz, wx, wy) / 8.0
    mass = outer(waz, wax, way) / 8.0
    diagonal = 0.5 * (outer(saz, wax, way) + outer(waz, sax, way) + outer(waz, wax, say))
    diagonal = diagonal + SHIFT_COEF * mass
    jz, kz = coarse_tables(1, lift, stiff, False)
    jx, kx = coarse_tables(2, lift, stiff, False)
    jy, ky = coarse_tables(16, lift, stiff, True)

    def lanes(table):
        out = np.zeros((table.shape[0], 128))
        out[:, :80] = np.tile(table[:, :16], (1, 5))
        out[:, WALL_LANES] = table[:, 16:17]
        return out

    def across(table):
        out = np.zeros((table.shape[0], 128))
        out[:, :80] = np.repeat(table, 16, axis=1)
        out[:, WALL_LANES] = table
        return out

    left = kron(scaled, eye(16)) + kron(eye(8), kron(eye(2), scaled)) + SHIFT_COEF / 4.0 * eye(128)
    matrices = [
        kron(deriv, eye(16)),
        kron(eye(8), kron(eye(2), deriv)),
        kron(eye(16), deriv).T,
        left,
        kron(eye(16), scaled).T,
        lanes(way[:, None] * jy),
        lanes(ky),
        lanes(jy),
        lanes(jy).T,
        lanes(ky).T,
    ]
    matrices = np.stack([halves(one) for one in matrices])
    fields = np.stack(
        [
            4.0 * local,
            local / mass,
            RELAXATION / diagonal,
            0.5 * outer(waz, wax, np.ones(128)),
        ]
    ).astype(np.float32)
    lane = np.arange(128)
    level = lane % 16
    rows = np.zeros((32, 128), np.float32)
    rows[0] = way
    rows[1] = np.where(level == 0, 1.0, 2.0)
    rows[2] = level < 15
    rows[3] = level > 0
    rows[4] = level == 15
    for k in range(5):
        spot = lane if k == 4 else (lane - 32 * k + 16) % 128
        rows[8 + 3 * k] = spot < 80
        rows[9 + 3 * k] = (spot >= 80) & (spot % 16 == 15)
        rows[10 + 3 * k] = (spot >= 80) & (spot < 112) & (spot % 16 == 14)
    kinds = [jx, wax[:, None] * jx, 0.5 * kx + SHIFT_COEF / 8.0 * wax[:, None] * jx]
    spans = np.stack([across(one) for one in kinds]).astype(np.float32)
    small = np.concatenate([fields.reshape(-1, 128), rows, spans.reshape(-1, 128)])
    return matrices, small, jz, kz, waz


M_DZ, M_DX, M_DY, M_LEFT, M_RIGHT, M_JYW, M_KY, M_JY, M_JYT, M_KYT = range(10)


def kernel(
    zcoef,
    count,
    vel_in,
    mats_in,
    small_in,
    adv_out,
    p_out,
    vel,
    mats,
    small,
    sloc,
    pres,
    csrc,
    work,
    acc,
    xs,
    co,
    zr,
    xr,
    cr,
    g1,
    g2,
    ext,
    gauge,
    load,
    n_send,
    n_recv,
    a_send,
    a_recv,
    b_send,
    b_recv,
    known_side,
    known_row,
):
    jz, kz, waz = zcoef
    planes = count // 16
    fields = [small.at[pl.ds(128 * k, 128)] for k in range(4)]
    rows = small.at[pl.ds(512, 32)]
    spans = [small.at[pl.ds(544 + 16 * k, 16)] for k in range(3)]
    elem = lax.axis_index("elem")
    sub = lax.axis_index("sub")
    plane = elem // 16
    place = elem % 16
    slot = plane * 4 + sub
    turn = lax.rem(32 * sub + 112, 128)

    def near(de, ds):
        return (lax.rem(elem + de + count, count), lax.rem(sub + ds + 4, 4))

    def along(dj):
        return (plane * 16 + lax.rem(place + dj, 16), sub)

    def over(dx, ds):
        return (lax.rem(plane + dx, planes) * 16 + place, lax.rem(sub + ds, 4))

    near_ids = [
        near(1, 1),
        near(1, -1),
        near(-1, 1),
        near(-1, -1),
        near(1, 0),
        near(-1, 0),
        near(0, 1),
        near(0, -1),
    ]
    a_ids = [along(dj) for dj in sorted(range(1, 16), key=lambda d: -min(d, 16 - d))]
    steps = [(dx, ds) for dx in range(planes) for ds in range(4) if dx or ds]
    steps = sorted(steps, key=lambda d: -(min(d[0], planes - d[0]) + min(d[1], 4 - d[1])))
    b_ids = [over(dx, ds) for dx, ds in steps]
    side_ids = [along(4), along(12)]
    row_ids = [over(dx, 0) for dx in range(1, planes)]

    loads = [
        pltpu.make_async_copy(src, dst, load.at[k])
        for k, (src, dst) in enumerate(
            ((vel_in, vel), (mats_in, mats), (small_in, small))
        )
    ]
    barrier = pltpu.get_barrier_semaphore()
    partners = near_ids + side_ids + [along(2), along(14)] + row_ids
    for one in partners:
        pl.semaphore_signal(barrier, inc=1, device_id=one, device_id_type=MESH)
    for copy in loads:
        copy.start()

    sublane = lax.broadcasted_iota(jnp.int32, (8, 128), 0)
    lane = lax.broadcasted_iota(jnp.int32, (1, 128), 1)
    low_lane = jnp.where((lane % 8 == 0) & (lane > 0), 1.0, 0.0)
    high_lane = jnp.where((lane % 8 == 7) & (lane < 127), 1.0, 0.0)

    def split(x):
        high = x.astype(jnp.bfloat16)
        return high, (x - high.astype(jnp.float32)).astype(jnp.bfloat16)

    def mul(a, b):
        return jnp.dot(a, b, preferred_element_type=jnp.float32)

    def left_dot(index, parts):
        high, low = parts
        return mul(mats[index, 0], high) + (mul(mats[index, 0], low) + mul(mats[index, 1], high))

    def right_dot(parts, index):
        high, low = parts
        return mul(high, mats[index, 0]) + (mul(low, mats[index, 0]) + mul(high, mats[index, 1]))

    def near_copies(r, comps):
        pairs = [
            (co.at[r, 0], cr.at[r, 0]),
            (co.at[r, 1], cr.at[r, 1]),
            (co.at[r, 2], cr.at[r, 2]),
            (co.at[r, 3], cr.at[r, 3]),
            (work.at[r, pl.ds(0, comps), pl.ds(112, 16)], zr.at[r, 0, pl.ds(0, comps)]),
            (work.at[r, pl.ds(0, comps), pl.ds(0, 16)], zr.at[r, 1, pl.ds(0, comps)]),
            (xs.at[r, 1, pl.ds(0, comps)], xr.at[r, 0, pl.ds(0, comps)]),
            (xs.at[r, 0, pl.ds(0, comps)], xr.at[r, 1, pl.ds(0, comps)]),
        ]
        return [
            pltpu.make_async_remote_copy(
                src_ref=src,
                dst_ref=dst,
                send_sem=n_send.at[r],
                recv_sem=n_recv.at[r],
                device_id=near_ids[k],
                device_id_type=MESH,
            )
            for k, (src, dst) in enumerate(pairs)
        ]

    def take(sem, count_rows):
        part = gauge.at[pl.ds(0, count_rows)]
        pltpu.make_async_copy(part, part, sem).wait()

    def near_rows(comps):
        return 32 + 48 * comps

    def stage_near(r, comps):
        for corner, row in enumerate((127, 112, 15, 0)):
            tile = jnp.zeros((8, 128), jnp.float32)
            for c in range(comps):
                tile = jnp.where(sublane == c, work[r, c, row : row + 1, :], tile)
            co[r, corner] = tile
        for c in range(comps):
            xs[r, 0, c] = work[r, c, pl.ds(0, 8, stride=16), :]
            xs[r, 1, c] = work[r, c, pl.ds(15, 8, stride=16), :]

    def send_near(r, comps, part=slice(None)):
        for copy in near_copies(r, comps)[part]:
            copy.start()

    def share_y(field):
        return (
            field
            + low_lane * pltpu.roll(field, 1, 1)
            + high_lane * pltpu.roll(field, 127, 1)
        )

    def finish_near(r, comps):
        for c in range(comps):
            acc[c] = share_y(work[r, c])
            both = acc[c, pl.ds(7, 8, stride=16), :] + acc[c, pl.ds(8, 8, stride=16), :]
            acc[c, pl.ds(7, 8, stride=16), :] = both
            acc[c, pl.ds(8, 8, stride=16), :] = both
        take(n_recv.at[r], near_rows(comps))
        for c in range(comps):
            for side, row in ((0, 0), (1, 112)):
                first = zr[r, side, c, 0:8]
                second = zr[r, side, c, 8:16]
                both = share_y(first + jnp.where(sublane == 7, pltpu.roll(second, 7, 0), 0.0))
                acc[c, row : row + 8] = acc[c, row : row + 8] + both
                both = share_y(second + jnp.where(sublane == 0, pltpu.roll(first, 1, 0), 0.0))
                acc[c, row + 8 : row + 16] = acc[c, row + 8 : row + 16] + both
            for side, row in ((0, 0), (1, 15)):
                face = xr[r, side, c]
                face = face + jnp.where(sublane == 0, cr[r, side, c : c + 1, :], 0.0)
                face = face + jnp.where(sublane == 7, cr[r, 2 + side, c : c + 1, :], 0.0)
                acc[c, pl.ds(row, 8, stride=16), :] = acc[c, pl.ds(row, 8, stride=16), :] + share_y(face)

    def advect(i):
        parts = [split(vel[c]) for c in range(3)]
        for c in range(3):
            term = vel[0] * left_dot(M_DZ, parts[c])
            term = term + vel[1] * left_dot(M_DX, parts[c])
            term = term + vel[2] * right_dot(parts[c], M_DY)
            work[i, c] = term * ((2.0 * TIME_STEP) * fields[1][...])

    for copy in loads:
        copy.wait()
    advect(0)
    stage_near(0, 3)
    pl.semaphore_wait(barrier, len(partners))

    def pass_on(known, ids):
        for one in ids:
            pl.semaphore_signal(known, inc=1, device_id=one, device_id_type=MESH)
        pl.semaphore_wait(known, len(ids))

    def substep(i, carry):
        send_near(i, 3)

        @pl.when(i == 0)
        def _():
            pass_on(known_side, side_ids)

        @pl.when(i == 1)
        def _():
            pass_on(known_row, row_ids)

        finish_near(i, 3)
        for c in range(3):
            vel[c] = vel[c] - acc[c]

        @pl.when(i < SUBSTEPS - 1)
        def _():
            advect(i + 1)
            stage_near(i + 1, 3)

        return carry

    lax.fori_loop(0, SUBSTEPS, substep, 0)

    for c in range(3):
        adv_out[c] = vel[c]
    def weighted(table, zi, field):
        total = None
        for z in range(8):
            if table[z, zi] != 0.0:
                one = float(table[z, zi]) * field[z]
                total = one if total is None else total + one
        return total

    divergence = left_dot(M_DZ, split(vel[0])) + left_dot(M_DX, split(vel[1]))
    divergence = divergence + right_dot(split(vel[2]), M_DY)
    source = (-SOURCE_GAIN / 4.0) * fields[0][...] * divergence
    sloc[...] = source
    pres[...] = jnp.zeros_like(source)
    direct = right_dot(split(source), M_JY).reshape(8, 16, 128)
    for zi in (1, 2):
        row = jnp.sum(weighted(jz, zi, direct) * spans[0][...], axis=0, keepdims=True)
        csrc[zi : zi + 1, :] = row

    wjz = waz[:, None] * jz

    def minus_laplace(field):
        parts = split(field)
        return sloc[...] - fields[0][...] * (left_dot(M_LEFT, parts) + right_dot(parts, M_RIGHT))

    a_rows = 8 * len(a_ids)
    b_rows = 24 * len(b_ids)

    def a_copies(it):
        return [
            pltpu.make_async_remote_copy(
                src_ref=g1.at[it, place],
                dst_ref=g1.at[it, place],
                send_sem=a_send.at[it],
                recv_sem=a_recv.at[it],
                device_id=one,
                device_id_type=MESH,
            )
            for one in a_ids
        ]

    def b_copies(it):
        return [
            pltpu.make_async_remote_copy(
                src_ref=g2.at[it, slot],
                dst_ref=g2.at[it, slot],
                send_sem=b_send.at[it],
                recv_sem=b_recv.at[it],
                device_id=one,
                device_id_type=MESH,
            )
            for one in b_ids
        ]

    def coarse_apply(pair):
        my, up, down, top = rows[1:2, :], rows[2:3, :], rows[3:4, :], rows[4:5, :]

        def middle(u):
            near_x = pltpu.roll(u, 16, 1) + pltpu.roll(u, 112, 1)
            near_z = pltpu.roll(u, 1, 0) + pltpu.roll(u, count - 1, 0)
            return 3.025 * u - 0.5 * (near_z + near_x)

        u, wall = pair
        body = my * middle(u) - up * pltpu.roll(u, 127, 1) - down * pltpu.roll(u, 1, 1)
        return [body - top * wall, top * (middle(wall) - u)]

    def inner(a, b):
        total = jnp.sum((a[0] * b[0]).reshape(count // 8, 8, 128), axis=0)
        total = total + jnp.sum((a[1] * b[1]).reshape(-1, 8, 128), axis=0)
        return jnp.sum(jnp.sum(total, axis=0, keepdims=True), axis=1, keepdims=True)

    def plus(a, factor, b):
        return [x + factor * y for x, y in zip(a, b)]

    def conjugate(right_side):
        residual = right_side
        image = coarse_apply(residual)
        norm_now = inner(residual, residual)
        energy = inner(residual, image)
        further = coarse_apply(image)
        alpha = norm_now / energy
        direction, moved, twice = residual, image, further
        solution = [alpha * d for d in direction]
        for sweep in range(1, COARSE_ITERS):
            residual = plus(residual, -alpha, moved)
            image = plus(image, -alpha, twice)
            norm_next = inner(residual, residual)
            energy = inner(residual, image)
            more = sweep < COARSE_ITERS - 1
            if more:
                further = coarse_apply(image)
            beta = norm_next / norm_now
            alpha = norm_next / (energy - beta * norm_next / alpha)
            direction = plus(residual, beta, direction)
            solution = plus(solution, alpha, direction)
            if more:
                moved = plus(image, beta, moved)
                twice = plus(further, beta, twice)
            norm_now = norm_next
        return solution

    def cycle(it, carry):
        first = SUBSTEPS + 2 * it
        second = first + 1
        pressure = pres[...]
        local = minus_laplace(pressure)
        work[first, 0] = local
        mixed = split(pressure * fields[1][...] + fields[2][...] * local)
        flat = right_dot(mixed, M_JYW).reshape(8, 16, 128)
        bent = right_dot(mixed, M_KY).reshape(8, 16, 128)
        tile = jnp.zeros((8, 128), jnp.float32)
        for zi in range(4):
            total = (0.5 * weighted(kz, zi, flat)) * spans[1][...]
            if zi in (1, 2):
                total = total + (0.5 * weighted(wjz, zi, bent)) * spans[1][...]
                total = total + weighted(wjz, zi, flat) * spans[2][...]
            row = -jnp.sum(total, axis=0, keepdims=True)
            if zi in (1, 2):
                row = csrc[zi : zi + 1, :] + row
            tile = jnp.where(sublane == lax.rem(place + zi + 7, 8), row, tile)
        g1[it, place] = tile
        for copy in a_copies(it):
            copy.start()
        stage_near(first, 1)
        send_near(first, 1)

        take(a_recv.at[it], a_rows)
        lower, upper = sublane < 4, sublane >= 4

        def some(mask, x):
            return jnp.where(mask, x, 0.0)

        first_edge = g1[it, 6] + g1[it, 7] + g1[it, 8]
        last_edge = g1[it, 14] + g1[it, 15]
        base = g1[it, 0]
        tops = [
            (g1[it, 1] + g1[it, 2]) + (g1[it, 3] + g1[it, 4]) + (g1[it, 5] + some(lower, base))
            + some(upper, first_edge),
            (g1[it, 9] + g1[it, 10]) + (g1[it, 11] + g1[it, 12]) + g1[it, 13]
            + (some(lower, first_edge) + some(upper, last_edge)),
            some(lower, last_edge) + some(upper, base),
        ]
        for k in range(3):
            g2[it, slot, 8 * k : 8 * k + 8, :] = pltpu.roll(tops[k], turn, 1)
        for copy in b_copies(it):
            copy.start()

        finish_near(first, 1)
        pressure = pressure + fields[2][...] * acc[0]
        pres[...] = pressure
        work[second, 0] = minus_laplace(pressure)
        stage_near(second, 1)
        send_near(second, 1)

        take(b_recv.at[it], b_rows)
        pieces, walls = [], []
        for x in range(planes):
            before, after = (x - 1) % planes, (x + 1) % planes
            for k in range(2):
                sums = [None] * 3
                for sy in range(4):
                    one = g2[it, 4 * x + sy, 8 * k : 8 * k + 8, :]
                    if k == 0:
                        one = one + some(lower, g2[it, 4 * before + sy, 16:24, :])
                    else:
                        one = one + some(upper, g2[it, 4 * after + sy, 16:24, :])
                    for n in range(3):
                        at = 8 + 3 * sy + n
                        part = one * rows[at : at + 1, :]
                        sums[n] = part if sums[n] is None else sums[n] + part
                pieces.append(sums[0])
                walls.append(pltpu.roll(sums[1], 48, 1) + pltpu.roll(sums[2], 97, 1))
        right_side = [jnp.concatenate(pieces, axis=0), jnp.concatenate(walls, axis=0)]
        answer = conjugate(right_side)
        for half in range(2):
            ext[half, 0:8] = answer[half][count - 8 : count]
            ext[half, 8 : 8 + count] = answer[half]
            ext[half, 8 + count : 16 + count] = answer[half][0:8]
        body = ext[0, pl.ds(elem + 7, 8), :]
        wall = ext[1, pl.ds(elem + 7, 8), :]
        own = rows[20:21, :] * pltpu.roll(body, lax.rem(256 - turn, 128), 1)
        own = own + rows[21:22, :] * pltpu.roll(wall, lax.rem(208 - turn, 128), 1)
        own = own + rows[22:23, :] * pltpu.roll(wall, lax.rem(159 - turn, 128), 1)
        vertex = [own[v : v + 1, :] for v in range(4)]

        interp, image = [], []
        for z in range(8):
            value = float(jz[z, 1]) * vertex[1] + float(jz[z, 2]) * vertex[2]
            interp.append(value * spans[0][...])
            part = (float(waz[z]) * value) * spans[2][...]
            if np.any(kz[z] != 0.0):
                bend = None
                for v in range(4):
                    if kz[z, v] != 0.0:
                        term = (0.5 * float(kz[z, v])) * vertex[v]
                        bend = term if bend is None else bend + term
                part = part + bend * spans[1][...]
            image.append(part)
        interp = split(jnp.concatenate(interp, axis=0))
        image = split(jnp.concatenate(image, axis=0))
        correction = right_dot(interp, M_JYT)
        applied = rows[0:1, :] * right_dot(image, M_JYT)
        applied = applied + fields[3][...] * right_dot(interp, M_KYT)
        finish_near(second, 1)
        pres[...] = pres[...] + correction + fields[2][...] * (acc[0] - applied)
        return carry

    lax.fori_loop(0, MG_ITERS, cycle, 0)
    p_out[...] = pres[...]

    for r in range(ROUNDS):
        take(n_send.at[r], near_rows(3 if r < SUBSTEPS else 1))
    for it in range(MG_ITERS):
        take(a_send.at[it], a_rows)
        take(b_send.at[it], b_rows)


def solution(mesh):
    count = mesh.shape["elem"]
    matrices, small, jz, kz, waz = make_tables()
    planes = count // 16
    f32 = jnp.float32

    def shards(velocity):
        vmem = pl.BlockSpec(memory_space=pltpu.VMEM)
        hbm = pl.BlockSpec(memory_space=pltpu.HBM)
        advected, pressure = pl.pallas_call(
            functools.partial(kernel, (jz, kz, waz), count),
            out_shape=(
                jax.ShapeDtypeStruct((3, 128, 128), f32),
                jax.ShapeDtypeStruct((128, 128), f32),
            ),
            in_specs=[hbm] * 3,
            out_specs=(vmem, vmem),
            scratch_shapes=[
                pltpu.VMEM((3, 128, 128), f32),
                pltpu.VMEM(matrices.shape, jnp.bfloat16),
                pltpu.VMEM(small.shape, f32),
                pltpu.VMEM((128, 128), f32),
                pltpu.VMEM((128, 128), f32),
                pltpu.VMEM((8, 128), f32),
                pltpu.VMEM((ROUNDS, 3, 128, 128), f32),
                pltpu.VMEM((3, 128, 128), f32),
                pltpu.VMEM((ROUNDS, 2, 3, 8, 128), f32),
                pltpu.VMEM((ROUNDS, 4, 8, 128), f32),
                pltpu.VMEM((ROUNDS, 2, 3, 16, 128), f32),
                pltpu.VMEM((ROUNDS, 2, 3, 8, 128), f32),
                pltpu.VMEM((ROUNDS, 4, 8, 128), f32),
                pltpu.VMEM((MG_ITERS, 16, 8, 128), f32),
                pltpu.VMEM((MG_ITERS, 4 * planes, 24, 128), f32),
                pltpu.VMEM((2, count + 16, 128), f32),
                pltpu.VMEM((360, 128), f32),
                pltpu.SemaphoreType.DMA((3,)),
                pltpu.SemaphoreType.DMA((ROUNDS,)),
                pltpu.SemaphoreType.DMA((ROUNDS,)),
                pltpu.SemaphoreType.DMA((MG_ITERS,)),
                pltpu.SemaphoreType.DMA((MG_ITERS,)),
                pltpu.SemaphoreType.DMA((MG_ITERS,)),
                pltpu.SemaphoreType.DMA((MG_ITERS,)),
                pltpu.SemaphoreType.REGULAR,
                pltpu.SemaphoreType.REGULAR,
            ],
            compiler_params=pltpu.CompilerParams(
                collective_id=0, has_side_effects=True, vmem_limit_bytes=54912 * 1024
            ),
        )(
            velocity.reshape(3, 128, 128),
            jnp.asarray(matrices),
            jnp.asarray(small),
        )
        return advected.reshape(3, 8, 16, 128), pressure.reshape(8, 16, 128)

    return jax.shard_map(
        shards,
        mesh=mesh,
        in_specs=(P(None, "elem", "sub", None),),
        out_specs=(P(None, "elem", "sub", None), P("elem", "sub", None)),
        check_vma=False,
    )
```

```python
import functools

import jax
import jax.numpy as jnp
import ml_dtypes
import numpy as np
from jax import lax
from jax.experimental import pallas as pl
from jax.experimental.pallas import tpu as pltpu
from jax.sharding import PartitionSpec as P

POINTS = 8
SUBSTEPS = 3
MG_ITERS = 3
COARSE_ITERS = 4

TIME_STEP = 0.005
SHIFT_COEF = 0.05
RELAXATION = 0.6
SOURCE_GAIN = 20.0

MESH = pl.DeviceIdType.MESH
ROUNDS = SUBSTEPS + 2 * MG_ITERS
WALL_LANES = [95, 111, 127, 94, 110]


CORNERS = (127, 112, 15, 0)


def legendre_last(points, degree):
    previous = points * 0.0 + 1.0
    current = points + 0.0
    for level in range(2, degree + 1):
        following = ((2 * level - 1) * points * current - (level - 1) * previous) / level
        previous = current
        current = following
    return (previous, current)


def gll_tables(count):
    degree = count - 1
    points = -np.cos(np.pi * np.arange(count) / degree)
    for sweep in range(100):
        before_last, last_value = legendre_last(points, degree)
        points = points - (points * last_value - before_last) / (count * last_value)
    before_last, legendre = legendre_last(points, degree)
    weights = 2.0 / (degree * (degree + 1) * legendre**2)
    spacing = points[:, None] - points[None, :] + np.eye(count)
    matrix = legendre[:, None] / (legendre[None, :] * spacing) * (1.0 - np.eye(count))
    matrix[0, 0] = -degree * (degree + 1) / 4.0
    matrix[degree, degree] = degree * (degree + 1) / 4.0
    return (points, weights, matrix)


def assembled(values, walls):
    blocks = values.reshape(-1, POINTS)
    out = blocks.copy()
    out[:, 0] += blocks[:, -1]
    out[:, -1] += blocks[:, 0]
    if walls:
        out[0, 0] = blocks[0, 0]
        out[-1, -1] = blocks[-1, -1]
    return out.reshape(-1)


def coarse_tables(elements, lift, stiff, walls):
    count = elements * POINTS
    vertices = elements + 1
    interp = np.zeros((count, vertices + 2))
    slope = np.zeros((count, vertices + 2))
    edge = stiff @ lift
    for element in range(elements):
        for point in range(POINTS):
            row = element * POINTS + point
            pairs = [(element, point)]
            if point == 0 and not (walls and element == 0):
                pairs.append((element - 1, POINTS - 1))
            if point == POINTS - 1 and not (walls and element == elements - 1):
                pairs.append((element + 1, 0))
            for side in (0, 1):
                interp[row, element + side + 1] += lift[point, side]
                for other, at in pairs:
                    slope[row, other + side + 1] += edge[at, side]
    slope[np.abs(slope) < 1e-12] = 0.0
    return (interp[:, 1:-1], slope[:, 1:-1]) if walls else (interp, slope)


def halves(matrix):
    whole = np.asarray(matrix, np.float32)
    high = whole.astype(ml_dtypes.bfloat16)
    low = (whole - high.astype(np.float32)).astype(ml_dtypes.bfloat16)
    return np.stack([high, low])


def make_tables():
    points, weights, deriv = gll_tables(POINTS)
    stiff = deriv.T @ np.diag(weights) @ deriv
    scaled = np.diag(1.0 / weights) @ stiff
    squares = (deriv * deriv).T @ weights
    lift = np.stack([(1.0 - points) / 2.0, (1.0 + points) / 2.0], axis=1)
    kron, eye = np.kron, np.eye
    wz, wx, wy = weights, np.tile(weights, 2), np.tile(weights, 16)
    waz, wax, way = assembled(wz, False), assembled(wx, False), assembled(wy, True)
    saz = assembled(squares, False)
    sax = assembled(np.tile(squares, 2), False)
    say = assembled(np.tile(squares, 16), True)

    def outer(a, b, c):
        return kron(a, b)[:, None] * c[None, :]

    local = outer(wz, wx, wy) / 8.0
    mass = outer(waz, wax, way) / 8.0
    diagonal = 0.5 * (outer(saz, wax, way) + outer(waz, sax, way) + outer(waz, wax, say))
    diagonal = diagonal + SHIFT_COEF * mass
    jz, kz = coarse_tables(1, lift, stiff, False)
    jx, kx = coarse_tables(2, lift, stiff, False)
    jy, ky = coarse_tables(16, lift, stiff, True)

    def lanes(table):
        out = np.zeros((table.shape[0], 128))
        out[:, :80] = np.tile(table[:, :16], (1, 5))
        out[:, WALL_LANES] = table[:, 16:17]
        return out

    def across(table):
        out = np.zeros((table.shape[0], 128))
        out[:, :80] = np.repeat(table, 16, axis=1)
        out[:, WALL_LANES] = table
        return out

    left = kron(scaled, eye(16)) + kron(eye(8), kron(eye(2), scaled)) + SHIFT_COEF / 4.0 * eye(128)
    matrices = [
        kron(deriv, eye(16)),
        kron(eye(8), kron(eye(2), deriv)),
        left,
        kron(eye(16), deriv).T,
        kron(eye(16), scaled).T,
        lanes(way[:, None] * jy),
        lanes(ky),
        lanes(jy),
        lanes(jy).T,
        lanes(ky).T,
    ]
    pairs = [halves(one) for one in matrices]
    flat = [pairs[0][0], pairs[1][0], pairs[0][1], pairs[1][1]]
    for pair in pairs[2:]:
        flat.extend([pair[0], pair[1]])
    matrices = np.concatenate(flat)
    fields = np.stack(
        [
            4.0 * local,
            local / mass,
            RELAXATION / diagonal,
            0.5 * outer(waz, wax, np.ones(128)),
        ]
    ).astype(np.float32)
    lane = np.arange(128)
    level = lane % 16
    rows = np.zeros((40, 128), np.float32)
    rows[24:32] = deriv[0][:, None]
    rows[32:40] = deriv[-1][:, None]
    rows[0] = way
    rows[1] = np.where(level == 0, 1.0, 2.0)
    rows[2] = level < 15
    rows[3] = level > 0
    rows[4] = level == 15
    for k in range(5):
        spot = lane if k == 4 else (lane - 32 * k + 16) % 128
        rows[8 + 3 * k] = spot < 80
        rows[9 + 3 * k] = (spot >= 80) & (spot % 16 == 15)
        rows[10 + 3 * k] = (spot >= 80) & (spot < 112) & (spot % 16 == 14)
    kinds = [jx, wax[:, None] * jx, 0.5 * kx + SHIFT_COEF / 8.0 * wax[:, None] * jx]
    spans = np.stack([across(one) for one in kinds]).astype(np.float32)
    small = np.concatenate([fields.reshape(-1, 128), rows, spans.reshape(-1, 128)])
    return matrices, small, jz, kz, waz


M_DY, M_RIGHT, M_JYW, M_KY, M_JY, M_JYT, M_KYT = range(768, 768 + 7 * 256, 256)
M_LEFT = 512


def kernel(
    zcoef,
    count,
    vel_in,
    mats_in,
    small_in,
    adv_out,
    p_out,
    vel,
    mats,
    small,
    sloc,
    pres,
    csrc,
    work,
    acc,
    xs,
    co,
    zr,
    xr,
    cr,
    g1,
    g2,
    ext,
    gauge,
    load,
    n_send,
    n_recv,
    a_send,
    a_recv,
    b_send,
    b_recv,
    known_side,
    known_row,
):
    jz, kz, waz = zcoef
    planes = count // 16
    fields = [small.at[pl.ds(128 * k, 128)] for k in range(4)]
    rows = small.at[pl.ds(512, 40)]
    spans = [small.at[pl.ds(552 + 16 * k, 16)] for k in range(3)]
    elem = lax.axis_index("elem")
    sub = lax.axis_index("sub")
    plane = elem // 16
    place = elem % 16
    slot = plane * 4 + sub
    turn = lax.rem(32 * sub + 112, 128)

    def near(de, ds):
        return (lax.rem(elem + de + count, count), lax.rem(sub + ds + 4, 4))

    def along(dj):
        return (plane * 16 + lax.rem(place + dj, 16), sub)

    def over(dx, ds):
        return (lax.rem(plane + dx, planes) * 16 + place, lax.rem(sub + ds, 4))

    near_ids = [
        near(1, 1),
        near(1, -1),
        near(-1, 1),
        near(-1, -1),
        near(1, 0),
        near(-1, 0),
        near(0, 1),
        near(0, -1),
    ]
    a_ids = [along(dj) for dj in sorted(range(1, 16), key=lambda d: -min(d, 16 - d))]
    steps = [(dx, ds) for dx in range(planes) for ds in range(4) if dx or ds]
    steps = sorted(steps, key=lambda d: -(min(d[0], planes - d[0]) + min(d[1], 4 - d[1])))
    b_ids = [over(dx, ds) for dx, ds in steps]
    side_ids = [along(4), along(12)]
    row_ids = [over(dx, 0) for dx in range(1, planes)]

    loads = [
        pltpu.make_async_copy(src, dst, load.at[k])
        for k, (src, dst) in enumerate(
            ((vel_in, vel), (mats_in, mats), (small_in, small))
        )
    ]
    barrier = pltpu.get_barrier_semaphore()
    partners = near_ids + side_ids + [along(2), along(14)] + row_ids
    for one in partners:
        pl.semaphore_signal(barrier, inc=1, device_id=one, device_id_type=MESH)
    for copy in loads:
        copy.start()

    sublane = lax.broadcasted_iota(jnp.int32, (8, 128), 0)
    lane = lax.broadcasted_iota(jnp.int32, (1, 128), 1)
    low_lane = jnp.where((lane % 8 == 0) & (lane > 0), 1.0, 0.0)
    high_lane = jnp.where((lane % 8 == 7) & (lane < 127), 1.0, 0.0)

    def split(x):
        high = x.astype(jnp.bfloat16)
        return high, (x - high.astype(jnp.float32)).astype(jnp.bfloat16)

    def mul(a, b):
        return jnp.dot(a, b, preferred_element_type=jnp.float32)

    def rows_of(at, number):
        return mats[at : at + 128 * number, :]

    def slopes(parts):
        high, low = parts
        big, small_part = mul(rows_of(0, 4), high), mul(rows_of(0, 2), low)
        along_z = big[0:128] + (big[256:384] + small_part[0:128])
        along_x = big[128:256] + (big[384:512] + small_part[128:256])
        return along_z, along_x

    def left_dot(at, parts):
        high, low = parts
        big = mul(rows_of(at, 2), high)
        return big[0:128] + (big[128:256] + mul(rows_of(at, 1), low))

    def right_dot(parts, at, exact=False):
        high, low = parts
        size = high.shape[0]
        big = mul(jnp.concatenate([high, low], axis=0), rows_of(at, 1))
        rest = big[size:]
        if not exact:
            rest = rest + mul(high, rows_of(at + 128, 1))
        return big[:size] + rest

    def near_copies(r, comps, part=slice(None)):
        pairs = [
            (co.at[r, 0], cr.at[r, 0]),
            (co.at[r, 1], cr.at[r, 1]),
            (co.at[r, 2], cr.at[r, 2]),
            (co.at[r, 3], cr.at[r, 3]),
            (work.at[r, pl.ds(0, comps), pl.ds(112, 16)], zr.at[r, 0, pl.ds(0, comps)]),
            (work.at[r, pl.ds(0, comps), pl.ds(0, 16)], zr.at[r, 1, pl.ds(0, comps)]),
            (xs.at[r, 1, pl.ds(0, comps)], xr.at[r, 0, pl.ds(0, comps)]),
            (xs.at[r, 0, pl.ds(0, comps)], xr.at[r, 1, pl.ds(0, comps)]),
        ]
        return [
            pltpu.make_async_remote_copy(
                src_ref=src,
                dst_ref=dst,
                send_sem=n_send.at[r],
                recv_sem=n_recv.at[r],
                device_id=near_ids[k],
                device_id_type=MESH,
            )
            for k, (src, dst) in list(enumerate(pairs))[part]
        ]

    def take(sem, count_rows):
        part = gauge.at[pl.ds(0, count_rows)]
        pltpu.make_async_copy(part, part, sem).wait()

    def near_rows(comps):
        return 32 + 48 * comps

    def stage_corners(r, comps):
        for corner, row in enumerate(CORNERS):
            tile = jnp.zeros((8, 128), jnp.float32)
            for c in range(comps):
                tile = jnp.where(sublane == c, work[r, c, row : row + 1, :], tile)
            co[r, corner] = tile

    def stage_faces(r, comps):
        for c in range(comps):
            xs[r, 0, c] = work[r, c, pl.ds(0, 8, stride=16), :]
            xs[r, 1, c] = work[r, c, pl.ds(15, 8, stride=16), :]

    def send_near(r, comps, part=slice(None)):
        for copy in near_copies(r, comps, part):
            copy.start()

    def share_y(field):
        return (
            field
            + low_lane * pltpu.roll(field, 1, 1)
            + high_lane * pltpu.roll(field, 127, 1)
        )

    def finish_near(r, comps):
        for c in range(comps):
            acc[c] = share_y(work[r, c])
            both = acc[c, pl.ds(7, 8, stride=16), :] + acc[c, pl.ds(8, 8, stride=16), :]
            acc[c, pl.ds(7, 8, stride=16), :] = both
            acc[c, pl.ds(8, 8, stride=16), :] = both
        take(n_recv.at[r], near_rows(comps))
        for c in range(comps):
            for side, row in ((0, 0), (1, 112)):
                first = zr[r, side, c, 0:8]
                second = zr[r, side, c, 8:16]
                both = share_y(first + jnp.where(sublane == 7, pltpu.roll(second, 7, 0), 0.0))
                acc[c, row : row + 8] = acc[c, row : row + 8] + both
                both = share_y(second + jnp.where(sublane == 0, pltpu.roll(first, 1, 0), 0.0))
                acc[c, row + 8 : row + 16] = acc[c, row + 8 : row + 16] + both
            for side, row in ((0, 0), (1, 15)):
                face = xr[r, side, c]
                face = face + jnp.where(sublane == 0, cr[r, side, c : c + 1, :], 0.0)
                face = face + jnp.where(sublane == 7, cr[r, 2 + side, c : c + 1, :], 0.0)
                acc[c, pl.ds(row, 8, stride=16), :] = acc[c, pl.ds(row, 8, stride=16), :] + share_y(face)

    def advect_corners(i):
        ends = (rows[24:32, :], rows[32:40, :])
        values, lines = [], []
        for row in CORNERS:
            last_z, last_x = int(row >= 112), int(row % 16 == 15)
            value = jnp.zeros((8, 128), jnp.float32)
            slope_z, slope_x = value, value
            for c in range(3):
                mine = sublane == c
                value = jnp.where(mine, vel[c, row : row + 1, :], value)
                line = vel[c, pl.ds(15 * last_x, 8, stride=16), :] * ends[last_z]
                slope_z = jnp.where(mine, jnp.sum(line, axis=0, keepdims=True), slope_z)
                at = 112 * last_z + 8 * last_x
                line = vel[c, at : at + 8, :] * ends[last_x]
                slope_x = jnp.where(mine, jnp.sum(line, axis=0, keepdims=True), slope_x)
            values.append(value)
            lines.append((slope_z, slope_x))
        slope_y = right_dot(split(jnp.concatenate(values, axis=0)), M_DY)
        for k, row in enumerate(CORNERS):
            tile = vel[0, row : row + 1, :] * lines[k][0] + vel[1, row : row + 1, :] * lines[k][1]
            tile = tile + vel[2, row : row + 1, :] * slope_y[8 * k : 8 * k + 8]
            co[i, k] = tile * ((2.0 * TIME_STEP) * fields[1][row : row + 1, :])

    def advect(i):
        parts = [split(vel[c]) for c in range(3)]
        stacked = [jnp.concatenate([one[n] for one in parts], axis=0) for n in range(2)]
        along_y = right_dot(stacked, M_DY)
        for c in range(3):
            along_z, along_x = slopes(parts[c])
            term = vel[0] * along_z + vel[1] * along_x
            term = term + vel[2] * along_y[128 * c : 128 * c + 128]
            work[i, c] = term * ((2.0 * TIME_STEP) * fields[1][...])

    for copy in loads:
        copy.wait()
    advect_corners(0)
    advect(0)
    stage_faces(0, 3)
    pl.semaphore_wait(barrier, len(partners))
    send_near(0, 3)

    def pass_on(known, ids):
        for one in ids:
            pl.semaphore_signal(known, inc=1, device_id=one, device_id_type=MESH)
        pl.semaphore_wait(known, len(ids))

    def substep(i, carry):
        @pl.when(i == 0)
        def _():
            pass_on(known_side, side_ids)

        @pl.when(i == 1)
        def _():
            pass_on(known_row, row_ids)

        finish_near(i, 3)
        for c in range(3):
            vel[c] = vel[c] - acc[c]

        @pl.when(i < SUBSTEPS - 1)
        def _():
            advect_corners(i + 1)
            send_near(i + 1, 3, slice(0, 4))
            advect(i + 1)
            stage_faces(i + 1, 3)
            send_near(i + 1, 3, slice(4, 8))

        return carry

    lax.fori_loop(0, SUBSTEPS, substep, 0)

    for c in range(3):
        adv_out[c] = vel[c]
    def weighted(table, zi, field):
        total = None
        for z in range(8):
            if table[z, zi] != 0.0:
                one = float(table[z, zi]) * field[z]
                total = one if total is None else total + one
        return total

    divergence = slopes(split(vel[0]))[0] + slopes(split(vel[1]))[1]
    divergence = divergence + right_dot(split(vel[2]), M_DY)
    source = (-SOURCE_GAIN / 4.0) * fields[0][...] * divergence
    sloc[...] = source
    pres[...] = jnp.zeros_like(source)
    work[SUBSTEPS, 0] = source
    direct = right_dot(split(source), M_JY).reshape(8, 16, 128)
    for zi in (1, 2):
        row = jnp.sum(weighted(jz, zi, direct) * spans[0][...], axis=0, keepdims=True)
        csrc[zi : zi + 1, :] = row

    wjz = waz[:, None] * jz

    def minus_laplace(field):
        parts = split(field)
        return sloc[...] - fields[0][...] * (left_dot(M_LEFT, parts) + right_dot(parts, M_RIGHT))

    a_rows = 8 * len(a_ids)
    b_rows = 19 * len(b_ids)

    def a_copies(it):
        return [
            pltpu.make_async_remote_copy(
                src_ref=g1.at[it, place],
                dst_ref=g1.at[it, place],
                send_sem=a_send.at[it],
                recv_sem=a_recv.at[it],
                device_id=one,
                device_id_type=MESH,
            )
            for one in a_ids
        ]

    def b_copies(it):
        return [
            pltpu.make_async_remote_copy(
                src_ref=g2.at[it, slot, pl.ds(0, 19)],
                dst_ref=g2.at[it, slot, pl.ds(0, 19)],
                send_sem=b_send.at[it],
                recv_sem=b_recv.at[it],
                device_id=one,
                device_id_type=MESH,
            )
            for one in b_ids
        ]

    def coarse_apply(pair):
        my, up, down, top = rows[1:2, :], rows[2:3, :], rows[3:4, :], rows[4:5, :]

        def middle(u):
            near_x = pltpu.roll(u, 16, 1) + pltpu.roll(u, 112, 1)
            near_z = pltpu.roll(u, 1, 0) + pltpu.roll(u, count - 1, 0)
            return 3.025 * u - 0.5 * (near_z + near_x)

        u, wall = pair
        body = my * middle(u) - up * pltpu.roll(u, 127, 1) - down * pltpu.roll(u, 1, 1)
        return [body - top * wall, top * (middle(wall) - u)]

    def inner(a, b):
        total = jnp.sum((a[0] * b[0]).reshape(count // 8, 8, 128), axis=0)
        total = total + jnp.sum((a[1] * b[1]).reshape(-1, 8, 128), axis=0)
        return jnp.sum(jnp.sum(total, axis=0, keepdims=True), axis=1, keepdims=True)

    def plus(a, factor, b):
        return [x + factor * y for x, y in zip(a, b)]

    def conjugate(right_side):
        residual = right_side
        image = coarse_apply(residual)
        norm_now = inner(residual, residual)
        energy = inner(residual, image)
        further = coarse_apply(image)
        alpha = norm_now / energy
        direction, moved, twice = residual, image, further
        solution = [alpha * d for d in direction]
        for sweep in range(1, COARSE_ITERS):
            residual = plus(residual, -alpha, moved)
            image = plus(image, -alpha, twice)
            norm_next = inner(residual, residual)
            energy = inner(residual, image)
            more = sweep < COARSE_ITERS - 1
            if more:
                further = coarse_apply(image)
            beta = norm_next / norm_now
            alpha = norm_next / (energy - beta * norm_next / alpha)
            direction = plus(residual, beta, direction)
            solution = plus(solution, alpha, direction)
            if more:
                moved = plus(image, beta, moved)
                twice = plus(further, beta, twice)
            norm_now = norm_next
        return solution

    def cycle(it, carry):
        first = SUBSTEPS + 2 * it
        second = first + 1
        pressure = pres[...]
        local = work[first, 0]
        mixed = split(pressure * fields[1][...] + fields[2][...] * local)
        flat = right_dot(mixed, M_JYW).reshape(8, 16, 128)
        bent = right_dot(mixed, M_KY, True).reshape(8, 16, 128)
        tile = jnp.zeros((8, 128), jnp.float32)
        for zi in range(4):
            total = (0.5 * weighted(kz, zi, flat)) * spans[1][...]
            if zi in (1, 2):
                total = total + (0.5 * weighted(wjz, zi, bent)) * spans[1][...]
                total = total + weighted(wjz, zi, flat) * spans[2][...]
            row = -jnp.sum(total, axis=0, keepdims=True)
            if zi in (1, 2):
                row = csrc[zi : zi + 1, :] + row
            tile = jnp.where(sublane == lax.rem(place + zi + 7, 8), row, tile)
        g1[it, place] = tile
        for copy in a_copies(it):
            copy.start()
        stage_corners(first, 1)
        stage_faces(first, 1)
        send_near(first, 1)

        take(a_recv.at[it], a_rows)
        lower, upper = sublane < 4, sublane >= 4

        def some(mask, x):
            return jnp.where(mask, x, 0.0)

        first_edge = g1[it, 6] + g1[it, 7] + g1[it, 8]
        last_edge = g1[it, 14] + g1[it, 15]
        base = g1[it, 0]
        tops = [
            (g1[it, 1] + g1[it, 2]) + (g1[it, 3] + g1[it, 4]) + (g1[it, 5] + some(lower, base))
            + some(upper, first_edge),
            (g1[it, 9] + g1[it, 10]) + (g1[it, 11] + g1[it, 12]) + g1[it, 13]
            + (some(lower, first_edge) + some(upper, last_edge)),
            some(lower, last_edge) + pltpu.roll(some(upper, base), 3, 0),
        ]
        for k in range(3):
            g2[it, slot, 8 * k : 8 * k + 8, :] = pltpu.roll(tops[k], turn, 1)
        for copy in b_copies(it):
            copy.start()

        finish_near(first, 1)
        pressure = pressure + fields[2][...] * acc[0]
        pres[...] = pressure
        work[second, 0] = minus_laplace(pressure)
        stage_corners(second, 1)
        stage_faces(second, 1)
        send_near(second, 1)

        take(b_recv.at[it], b_rows)
        pieces, walls = [], []
        for x in range(planes):
            before, after = (x - 1) % planes, (x + 1) % planes
            for k in range(2):
                sums = [None] * 3
                for sy in range(4):
                    one = g2[it, 4 * x + sy, 8 * k : 8 * k + 8, :]
                    if k == 0:
                        one = one + some(sublane < 2, g2[it, 4 * before + sy, 16:24, :])
                    else:
                        extra = pltpu.roll(g2[it, 4 * after + sy, 16:24, :], 5, 0)
                        one = one + some(sublane == 7, extra)
                    for n in range(3):
                        at = 8 + 3 * sy + n
                        part = one * rows[at : at + 1, :]
                        sums[n] = part if sums[n] is None else sums[n] + part
                pieces.append(sums[0])
                walls.append(pltpu.roll(sums[1], 48, 1) + pltpu.roll(sums[2], 97, 1))
        right_side = [jnp.concatenate(pieces, axis=0), jnp.concatenate(walls, axis=0)]
        answer = conjugate(right_side)
        for half in range(2):
            ext[half, 0:8] = answer[half][count - 8 : count]
            ext[half, 8 : 8 + count] = answer[half]
            ext[half, 8 + count : 16 + count] = answer[half][0:8]
        body = ext[0, pl.ds(elem + 7, 8), :]
        wall = ext[1, pl.ds(elem + 7, 8), :]
        own = rows[20:21, :] * pltpu.roll(body, lax.rem(256 - turn, 128), 1)
        own = own + rows[21:22, :] * pltpu.roll(wall, lax.rem(208 - turn, 128), 1)
        own = own + rows[22:23, :] * pltpu.roll(wall, lax.rem(159 - turn, 128), 1)
        vertex = [own[v : v + 1, :] for v in range(4)]

        interp, image = [], []
        for z in range(8):
            value = float(jz[z, 1]) * vertex[1] + float(jz[z, 2]) * vertex[2]
            interp.append(value * spans[0][...])
            part = (float(waz[z]) * value) * spans[2][...]
            if np.any(kz[z] != 0.0):
                bend = None
                for v in range(4):
                    if kz[z, v] != 0.0:
                        term = (0.5 * float(kz[z, v])) * vertex[v]
                        bend = term if bend is None else bend + term
                part = part + bend * spans[1][...]
            image.append(part)
        interp = split(jnp.concatenate(interp, axis=0))
        image = split(jnp.concatenate(image, axis=0))
        correction = right_dot(interp, M_JYT)
        applied = rows[0:1, :] * right_dot(image, M_JYT)
        applied = applied + fields[3][...] * right_dot(interp, M_KYT, True)
        finish_near(second, 1)
        pressure = pres[...] + correction + fields[2][...] * (acc[0] - applied)
        pres[...] = pressure

        @pl.when(it < MG_ITERS - 1)
        def _():
            work[first + 2, 0] = minus_laplace(pressure)

        return carry

    lax.fori_loop(0, MG_ITERS, cycle, 0)
    p_out[...] = pres[...]

    for r in range(ROUNDS):
        take(n_send.at[r], near_rows(3 if r < SUBSTEPS else 1))
    for it in range(MG_ITERS):
        take(a_send.at[it], a_rows)
        take(b_send.at[it], b_rows)


def solution(mesh):
    count = mesh.shape["elem"]
    matrices, small, jz, kz, waz = make_tables()
    planes = count // 16
    f32 = jnp.float32

    def shards(velocity):
        vmem = pl.BlockSpec(memory_space=pltpu.VMEM)
        hbm = pl.BlockSpec(memory_space=pltpu.HBM)
        advected, pressure = pl.pallas_call(
            functools.partial(kernel, (jz, kz, waz), count),
            out_shape=(
                jax.ShapeDtypeStruct((3, 128, 128), f32),
                jax.ShapeDtypeStruct((128, 128), f32),
            ),
            in_specs=[hbm] * 3,
            out_specs=(vmem, vmem),
            scratch_shapes=[
                pltpu.VMEM((3, 128, 128), f32),
                pltpu.VMEM(matrices.shape, jnp.bfloat16),
                pltpu.VMEM(small.shape, f32),
                pltpu.VMEM((128, 128), f32),
                pltpu.VMEM((128, 128), f32),
                pltpu.VMEM((8, 128), f32),
                pltpu.VMEM((ROUNDS, 3, 128, 128), f32),
                pltpu.VMEM((3, 128, 128), f32),
                pltpu.VMEM((ROUNDS, 2, 3, 8, 128), f32),
                pltpu.VMEM((ROUNDS, 4, 8, 128), f32),
                pltpu.VMEM((ROUNDS, 2, 3, 16, 128), f32),
                pltpu.VMEM((ROUNDS, 2, 3, 8, 128), f32),
                pltpu.VMEM((ROUNDS, 4, 8, 128), f32),
                pltpu.VMEM((MG_ITERS, 16, 8, 128), f32),
                pltpu.VMEM((MG_ITERS, 4 * planes, 24, 128), f32),
                pltpu.VMEM((2, count + 16, 128), f32),
                pltpu.VMEM((360, 128), f32),
                pltpu.SemaphoreType.DMA((3,)),
                pltpu.SemaphoreType.DMA((ROUNDS,)),
                pltpu.SemaphoreType.DMA((ROUNDS,)),
                pltpu.SemaphoreType.DMA((MG_ITERS,)),
                pltpu.SemaphoreType.DMA((MG_ITERS,)),
                pltpu.SemaphoreType.DMA((MG_ITERS,)),
                pltpu.SemaphoreType.DMA((MG_ITERS,)),
                pltpu.SemaphoreType.REGULAR,
                pltpu.SemaphoreType.REGULAR,
            ],
            compiler_params=pltpu.CompilerParams(
                collective_id=0, has_side_effects=True, vmem_limit_bytes=54912 * 1024
            ),
        )(
            velocity.reshape(3, 128, 128),
            jnp.asarray(matrices),
            jnp.asarray(small),
        )
        return advected.reshape(3, 8, 16, 128), pressure.reshape(8, 16, 128)

    return jax.shard_map(
        shards,
        mesh=mesh,
        in_specs=(P(None, "elem", "sub", None),),
        out_specs=(P(None, "elem", "sub", None), P("elem", "sub", None)),
        check_vma=False,
    )
```

```python
import functools

import jax
import jax.numpy as jnp
import ml_dtypes
import numpy as np
from jax import lax
from jax.experimental import pallas as pl
from jax.experimental.pallas import tpu as pltpu
from jax.sharding import PartitionSpec as P

POINTS = 8
SUBSTEPS = 3
MG_ITERS = 3
COARSE_ITERS = 4

TIME_STEP = 0.005
SHIFT_COEF = 0.05
RELAXATION = 0.6
SOURCE_GAIN = 20.0

MESH = pl.DeviceIdType.MESH
ROUNDS = SUBSTEPS + 2 * MG_ITERS
WALL_LANES = [95, 111, 127, 94, 110]


CORNERS = (127, 112, 15, 0)


def legendre_last(points, degree):
    previous = points * 0.0 + 1.0
    current = points + 0.0
    for level in range(2, degree + 1):
        following = ((2 * level - 1) * points * current - (level - 1) * previous) / level
        previous = current
        current = following
    return (previous, current)


def gll_tables(count):
    degree = count - 1
    points = -np.cos(np.pi * np.arange(count) / degree)
    for sweep in range(100):
        before_last, last_value = legendre_last(points, degree)
        points = points - (points * last_value - before_last) / (count * last_value)
    before_last, legendre = legendre_last(points, degree)
    weights = 2.0 / (degree * (degree + 1) * legendre**2)
    spacing = points[:, None] - points[None, :] + np.eye(count)
    matrix = legendre[:, None] / (legendre[None, :] * spacing) * (1.0 - np.eye(count))
    matrix[0, 0] = -degree * (degree + 1) / 4.0
    matrix[degree, degree] = degree * (degree + 1) / 4.0
    return (points, weights, matrix)


def assembled(values, walls):
    blocks = values.reshape(-1, POINTS)
    out = blocks.copy()
    out[:, 0] += blocks[:, -1]
    out[:, -1] += blocks[:, 0]
    if walls:
        out[0, 0] = blocks[0, 0]
        out[-1, -1] = blocks[-1, -1]
    return out.reshape(-1)


def coarse_tables(elements, lift, stiff, walls):
    count = elements * POINTS
    vertices = elements + 1
    interp = np.zeros((count, vertices + 2))
    slope = np.zeros((count, vertices + 2))
    edge = stiff @ lift
    for element in range(elements):
        for point in range(POINTS):
            row = element * POINTS + point
            pairs = [(element, point)]
            if point == 0 and not (walls and element == 0):
                pairs.append((element - 1, POINTS - 1))
            if point == POINTS - 1 and not (walls and element == elements - 1):
                pairs.append((element + 1, 0))
            for side in (0, 1):
                interp[row, element + side + 1] += lift[point, side]
                for other, at in pairs:
                    slope[row, other + side + 1] += edge[at, side]
    slope[np.abs(slope) < 1e-12] = 0.0
    return (interp[:, 1:-1], slope[:, 1:-1]) if walls else (interp, slope)


def halves(matrix):
    whole = np.asarray(matrix, np.float32)
    high = whole.astype(ml_dtypes.bfloat16)
    low = (whole - high.astype(np.float32)).astype(ml_dtypes.bfloat16)
    return np.stack([high, low])


def make_tables():
    points, weights, deriv = gll_tables(POINTS)
    stiff = deriv.T @ np.diag(weights) @ deriv
    scaled = np.diag(1.0 / weights) @ stiff
    squares = (deriv * deriv).T @ weights
    lift = np.stack([(1.0 - points) / 2.0, (1.0 + points) / 2.0], axis=1)
    kron, eye = np.kron, np.eye
    wz, wx, wy = weights, np.tile(weights, 2), np.tile(weights, 16)
    waz, wax, way = assembled(wz, False), assembled(wx, False), assembled(wy, True)
    saz = assembled(squares, False)
    sax = assembled(np.tile(squares, 2), False)
    say = assembled(np.tile(squares, 16), True)

    def outer(a, b, c):
        return kron(a, b)[:, None] * c[None, :]

    local = outer(wz, wx, wy) / 8.0
    mass = outer(waz, wax, way) / 8.0
    diagonal = 0.5 * (outer(saz, wax, way) + outer(waz, sax, way) + outer(waz, wax, say))
    diagonal = diagonal + SHIFT_COEF * mass
    jz, kz = coarse_tables(1, lift, stiff, False)
    jx, kx = coarse_tables(2, lift, stiff, False)
    jy, ky = coarse_tables(16, lift, stiff, True)

    def lanes(table):
        out = np.zeros((table.shape[0], 128))
        out[:, :80] = np.tile(table[:, :16], (1, 5))
        out[:, WALL_LANES] = table[:, 16:17]
        return out

    def across(table):
        out = np.zeros((table.shape[0], 128))
        out[:, :80] = np.repeat(table, 16, axis=1)
        out[:, WALL_LANES] = table
        return out

    left = kron(scaled, eye(16)) + kron(eye(8), kron(eye(2), scaled)) + SHIFT_COEF / 4.0 * eye(128)
    matrices = [
        kron(deriv, eye(16)),
        kron(eye(8), kron(eye(2), deriv)),
        left,
        kron(eye(16), deriv).T,
        kron(eye(16), scaled).T,
        lanes(way[:, None] * jy),
        lanes(ky),
        lanes(jy),
        lanes(jy).T,
        lanes(ky).T,
    ]
    pairs = [halves(one) for one in matrices]
    flat = [pairs[0][0], pairs[1][0], pairs[0][1], pairs[1][1]]
    for pair in pairs[2:]:
        flat.extend([pair[0], pair[1]])
    matrices = np.concatenate(flat)
    fields = np.stack(
        [
            4.0 * local,
            local / mass,
            RELAXATION / diagonal,
            0.5 * outer(waz, wax, np.ones(128)),
        ]
    ).astype(np.float32)
    lane = np.arange(128)
    level = lane % 16
    rows = np.zeros((40, 128), np.float32)
    rows[24:32] = deriv[0][:, None]
    rows[32:40] = deriv[-1][:, None]
    rows[0] = way
    rows[1] = np.where(level == 0, 1.0, 2.0)
    rows[2] = level < 15
    rows[3] = level > 0
    rows[4] = level == 15
    for k in range(5):
        spot = lane if k == 4 else (lane - 32 * k + 16) % 128
        rows[8 + 3 * k] = spot < 80
        rows[9 + 3 * k] = (spot >= 80) & (spot % 16 == 15)
        rows[10 + 3 * k] = (spot >= 80) & (spot < 112) & (spot % 16 == 14)
    kinds = [jx, wax[:, None] * jx, 0.5 * kx + SHIFT_COEF / 8.0 * wax[:, None] * jx]
    spans = np.stack([across(one) for one in kinds]).astype(np.float32)
    small = np.concatenate([fields.reshape(-1, 128), rows, spans.reshape(-1, 128)])
    return matrices, small, jz, kz, waz


M_DY, M_RIGHT, M_JYW, M_KY, M_JY, M_JYT, M_KYT = range(768, 768 + 7 * 256, 256)
M_LEFT = 512


def kernel(
    zcoef,
    count,
    vel_in,
    mats_in,
    small_in,
    adv_out,
    p_out,
    vel,
    mats,
    small,
    sloc,
    pres,
    csrc,
    work,
    acc,
    xs,
    co,
    zr,
    xr,
    cr,
    g1,
    g2,
    ext,
    gauge,
    load,
    n_send,
    n_recv,
    a_send,
    a_recv,
    b_send,
    b_recv,
    known_side,
    known_row,
):
    jz, kz, waz = zcoef
    planes = count // 16
    fields = [small.at[pl.ds(128 * k, 128)] for k in range(4)]
    rows = small.at[pl.ds(512, 40)]
    spans = [small.at[pl.ds(552 + 16 * k, 16)] for k in range(3)]
    elem = lax.axis_index("elem")
    sub = lax.axis_index("sub")
    plane = elem // 16
    place = elem % 16
    slot = plane * 4 + sub
    turn = lax.rem(32 * sub + 112, 128)

    def near(de, ds):
        return (lax.rem(elem + de + count, count), lax.rem(sub + ds + 4, 4))

    def along(dj):
        return (plane * 16 + lax.rem(place + dj, 16), sub)

    def over(dx, ds):
        return (lax.rem(plane + dx, planes) * 16 + place, lax.rem(sub + ds, 4))

    near_ids = [
        near(1, 1),
        near(1, -1),
        near(-1, 1),
        near(-1, -1),
        near(1, 0),
        near(-1, 0),
        near(0, 1),
        near(0, -1),
    ]
    a_ids = [along(dj) for dj in sorted(range(1, 16), key=lambda d: -min(d, 16 - d))]
    steps = [(dx, ds) for dx in range(planes) for ds in range(4) if dx or ds]
    steps = sorted(steps, key=lambda d: -(min(d[0], planes - d[0]) + min(d[1], 4 - d[1])))
    b_ids = [over(dx, ds) for dx, ds in steps]
    side_ids = [along(4), along(12)]
    row_ids = [over(dx, 0) for dx in range(1, planes)]

    loads = [
        pltpu.make_async_copy(src, dst, load.at[k])
        for k, (src, dst) in enumerate(
            ((vel_in, vel), (mats_in, mats), (small_in, small))
        )
    ]
    barrier = pltpu.get_barrier_semaphore()
    partners = near_ids + side_ids + [along(2), along(14)] + row_ids
    for one in partners:
        pl.semaphore_signal(barrier, inc=1, device_id=one, device_id_type=MESH)
    for copy in loads:
        copy.start()

    sublane = lax.broadcasted_iota(jnp.int32, (8, 128), 0)
    lane = lax.broadcasted_iota(jnp.int32, (1, 128), 1)
    low_lane = jnp.where((lane % 8 == 0) & (lane > 0), 1.0, 0.0)
    high_lane = jnp.where((lane % 8 == 7) & (lane < 127), 1.0, 0.0)

    def split(x):
        high = x.astype(jnp.bfloat16)
        return high, (x - high.astype(jnp.float32)).astype(jnp.bfloat16)

    def mul(a, b):
        return jnp.dot(a, b, preferred_element_type=jnp.float32)

    def rows_of(at, number):
        return mats[at : at + 128 * number, :]

    def slopes(parts):
        high, low = parts
        big, small_part = mul(rows_of(0, 4), high), mul(rows_of(0, 2), low)
        along_z = big[0:128] + (big[256:384] + small_part[0:128])
        along_x = big[128:256] + (big[384:512] + small_part[128:256])
        return along_z, along_x

    def left_dot(at, parts):
        high, low = parts
        big = mul(rows_of(at, 2), high)
        return big[0:128] + (big[128:256] + mul(rows_of(at, 1), low))

    def right_dot(parts, at, exact=False):
        high, low = parts
        size = high.shape[0]
        rest = mul(low, rows_of(at, 1))
        if exact:
            return mul(high, rows_of(at, 1)) + rest
        return mul(jnp.concatenate([high, high], axis=1), rows_of(at, 2)) + rest

    def near_copies(r, comps, part=slice(None)):
        pairs = [
            (co.at[r, 0], cr.at[r, 0]),
            (co.at[r, 1], cr.at[r, 1]),
            (co.at[r, 2], cr.at[r, 2]),
            (co.at[r, 3], cr.at[r, 3]),
            (work.at[r, pl.ds(0, comps), pl.ds(112, 16)], zr.at[r, 0, pl.ds(0, comps)]),
            (work.at[r, pl.ds(0, comps), pl.ds(0, 16)], zr.at[r, 1, pl.ds(0, comps)]),
            (xs.at[r, 1, pl.ds(0, comps)], xr.at[r, 0, pl.ds(0, comps)]),
            (xs.at[r, 0, pl.ds(0, comps)], xr.at[r, 1, pl.ds(0, comps)]),
        ]
        return [
            pltpu.make_async_remote_copy(
                src_ref=src,
                dst_ref=dst,
                send_sem=n_send.at[r],
                recv_sem=n_recv.at[r],
                device_id=near_ids[k],
                device_id_type=MESH,
            )
            for k, (src, dst) in list(enumerate(pairs))[part]
        ]

    def take(sem, count_rows):
        part = gauge.at[pl.ds(0, count_rows)]
        pltpu.make_async_copy(part, part, sem).wait()

    def near_rows(comps):
        return 32 + 48 * comps

    def stage_corners(r, comps):
        for corner, row in enumerate(CORNERS):
            tile = jnp.zeros((8, 128), jnp.float32)
            for c in range(comps):
                tile = jnp.where(sublane == c, work[r, c, row : row + 1, :], tile)
            co[r, corner] = tile

    def stage_faces(r, comps):
        for c in range(comps):
            xs[r, 0, c] = work[r, c, pl.ds(0, 8, stride=16), :]
            xs[r, 1, c] = work[r, c, pl.ds(15, 8, stride=16), :]

    def send_near(r, comps, part=slice(None)):
        for copy in near_copies(r, comps, part):
            copy.start()

    def share_y(field):
        return (
            field
            + low_lane * pltpu.roll(field, 1, 1)
            + high_lane * pltpu.roll(field, 127, 1)
        )

    def begin_near(r, comps):
        for c in range(comps):
            acc[c] = share_y(work[r, c])
            both = acc[c, pl.ds(7, 8, stride=16), :] + acc[c, pl.ds(8, 8, stride=16), :]
            acc[c, pl.ds(7, 8, stride=16), :] = both
            acc[c, pl.ds(8, 8, stride=16), :] = both

    def finish_near(r, comps):
        take(n_recv.at[r], near_rows(comps))
        for c in range(comps):
            for side, row in ((0, 0), (1, 112)):
                first = zr[r, side, c, 0:8]
                second = zr[r, side, c, 8:16]
                both = share_y(first + jnp.where(sublane == 7, pltpu.roll(second, 7, 0), 0.0))
                acc[c, row : row + 8] = acc[c, row : row + 8] + both
                both = share_y(second + jnp.where(sublane == 0, pltpu.roll(first, 1, 0), 0.0))
                acc[c, row + 8 : row + 16] = acc[c, row + 8 : row + 16] + both
            for side, row in ((0, 0), (1, 15)):
                face = xr[r, side, c]
                face = face + jnp.where(sublane == 0, cr[r, side, c : c + 1, :], 0.0)
                face = face + jnp.where(sublane == 7, cr[r, 2 + side, c : c + 1, :], 0.0)
                acc[c, pl.ds(row, 8, stride=16), :] = acc[c, pl.ds(row, 8, stride=16), :] + share_y(face)

    def advect_corners(i):
        ends = (rows[24:32, :], rows[32:40, :])
        values, lines = [], []
        for row in CORNERS:
            last_z, last_x = int(row >= 112), int(row % 16 == 15)
            value = jnp.zeros((8, 128), jnp.float32)
            slope_z, slope_x = value, value
            for c in range(3):
                mine = sublane == c
                value = jnp.where(mine, vel[c, row : row + 1, :], value)
                line = vel[c, pl.ds(15 * last_x, 8, stride=16), :] * ends[last_z]
                slope_z = jnp.where(mine, jnp.sum(line, axis=0, keepdims=True), slope_z)
                at = 112 * last_z + 8 * last_x
                line = vel[c, at : at + 8, :] * ends[last_x]
                slope_x = jnp.where(mine, jnp.sum(line, axis=0, keepdims=True), slope_x)
            values.append(value)
            lines.append((slope_z, slope_x))
        slope_y = right_dot(split(jnp.concatenate(values, axis=0)), M_DY)
        for k, row in enumerate(CORNERS):
            tile = vel[0, row : row + 1, :] * lines[k][0] + vel[1, row : row + 1, :] * lines[k][1]
            tile = tile + vel[2, row : row + 1, :] * slope_y[8 * k : 8 * k + 8]
            co[i, k] = tile * ((2.0 * TIME_STEP) * fields[1][row : row + 1, :])

    def advect(i):
        parts = [split(vel[c]) for c in range(3)]
        stacked = [jnp.concatenate([one[n] for one in parts], axis=0) for n in range(2)]
        along_y = right_dot(stacked, M_DY)
        for c in range(3):
            along_z, along_x = slopes(parts[c])
            term = vel[0] * along_z + vel[1] * along_x
            term = term + vel[2] * along_y[128 * c : 128 * c + 128]
            work[i, c] = term * ((2.0 * TIME_STEP) * fields[1][...])

    for copy in loads:
        copy.wait()
    advect_corners(0)
    advect(0)
    stage_faces(0, 3)
    pl.semaphore_wait(barrier, len(partners))
    send_near(0, 3)

    def pass_on(known, ids):
        for one in ids:
            pl.semaphore_signal(known, inc=1, device_id=one, device_id_type=MESH)
        pl.semaphore_wait(known, len(ids))

    def substep(i, carry):
        @pl.when(i == 0)
        def _():
            pass_on(known_side, side_ids)

        @pl.when(i == 1)
        def _():
            pass_on(known_row, row_ids)

        begin_near(i, 3)
        finish_near(i, 3)
        for c in range(3):
            vel[c] = vel[c] - acc[c]

        @pl.when(i < SUBSTEPS - 1)
        def _():
            advect_corners(i + 1)
            send_near(i + 1, 3, slice(0, 4))
            advect(i + 1)
            stage_faces(i + 1, 3)
            send_near(i + 1, 3, slice(4, 8))

        return carry

    lax.fori_loop(0, SUBSTEPS, substep, 0)

    for c in range(3):
        adv_out[c] = vel[c]
    def weighted(table, zi, field):
        total = None
        for z in range(8):
            if table[z, zi] != 0.0:
                one = float(table[z, zi]) * field[z]
                total = one if total is None else total + one
        return total

    divergence = slopes(split(vel[0]))[0] + slopes(split(vel[1]))[1]
    divergence = divergence + right_dot(split(vel[2]), M_DY)
    source = (-SOURCE_GAIN / 4.0) * fields[0][...] * divergence
    sloc[...] = source
    pres[...] = jnp.zeros_like(source)
    work[SUBSTEPS, 0] = source
    direct = right_dot(split(source), M_JY).reshape(8, 16, 128)
    for zi in (1, 2):
        row = jnp.sum(weighted(jz, zi, direct) * spans[0][...], axis=0, keepdims=True)
        csrc[zi : zi + 1, :] = row

    wjz = waz[:, None] * jz

    def minus_laplace(field):
        parts = split(field)
        return sloc[...] - fields[0][...] * (left_dot(M_LEFT, parts) + right_dot(parts, M_RIGHT))

    a_rows = 8 * len(a_ids)
    b_rows = 19 * len(b_ids)

    def a_copies(it):
        return [
            pltpu.make_async_remote_copy(
                src_ref=g1.at[it, place],
                dst_ref=g1.at[it, place],
                send_sem=a_send.at[it],
                recv_sem=a_recv.at[it],
                device_id=one,
                device_id_type=MESH,
            )
            for one in a_ids
        ]

    def b_copies(it):
        return [
            pltpu.make_async_remote_copy(
                src_ref=g2.at[it, slot, pl.ds(0, 19)],
                dst_ref=g2.at[it, slot, pl.ds(0, 19)],
                send_sem=b_send.at[it],
                recv_sem=b_recv.at[it],
                device_id=one,
                device_id_type=MESH,
            )
            for one in b_ids
        ]

    def coarse_apply(pair):
        my, up, down, top = rows[1:2, :], rows[2:3, :], rows[3:4, :], rows[4:5, :]

        def middle(u):
            near_x = pltpu.roll(u, 16, 1) + pltpu.roll(u, 112, 1)
            near_z = pltpu.roll(u, 1, 0) + pltpu.roll(u, count - 1, 0)
            return 3.025 * u - 0.5 * (near_z + near_x)

        u, wall = pair
        body = my * middle(u) - up * pltpu.roll(u, 127, 1) - down * pltpu.roll(u, 1, 1)
        return [body - top * wall, top * (middle(wall) - u)]

    def inner(a, b):
        total = jnp.sum((a[0] * b[0]).reshape(count // 8, 8, 128), axis=0)
        total = total + jnp.sum((a[1] * b[1]).reshape(-1, 8, 128), axis=0)
        return jnp.sum(jnp.sum(total, axis=0, keepdims=True), axis=1, keepdims=True)

    def plus(a, factor, b):
        return [x + factor * y for x, y in zip(a, b)]

    def own_planes(k, pair):
        for half in range(2):
            ext[k, half, 0:8] = pair[half][count - 8 : count]
            ext[k, half, 8 : 8 + count] = pair[half]
            ext[k, half, 8 + count : 16 + count] = pair[half][0:8]
        body = ext[k, 0, pl.ds(elem + 7, 8), :]
        wall = ext[k, 1, pl.ds(elem + 7, 8), :]
        own = rows[20:21, :] * pltpu.roll(body, lax.rem(256 - turn, 128), 1)
        own = own + rows[21:22, :] * pltpu.roll(wall, lax.rem(208 - turn, 128), 1)
        return own + rows[22:23, :] * pltpu.roll(wall, lax.rem(159 - turn, 128), 1)

    def conjugate(right_side):
        residual = right_side
        image = coarse_apply(residual)
        norm_now = inner(residual, residual)
        energy = inner(residual, image)
        further = coarse_apply(image)
        planes_of = [own_planes(0, residual)]
        alpha = norm_now / energy
        inverse = 1.0 / norm_now
        turned = energy * inverse
        moved, twice = image, further
        along = [jnp.ones_like(alpha)]
        weights = [alpha]
        for sweep in range(1, COARSE_ITERS):
            residual = plus(residual, -alpha, moved)
            image = plus(image, -alpha, twice)
            norm_next = inner(residual, residual)
            energy = inner(residual, image)
            more = sweep < COARSE_ITERS - 1
            if more:
                further = coarse_apply(image)
            planes_of.append(own_planes(sweep, residual))
            beta = norm_next * inverse
            energy = energy - (beta * turned) * norm_next
            alpha = norm_next / energy
            along = [beta * a for a in along] + [jnp.ones_like(alpha)]
            weights = [w + alpha * a for w, a in zip(weights + [jnp.zeros_like(alpha)], along)]
            if more:
                inverse = 1.0 / norm_next
                turned = energy * inverse
                moved = plus(image, beta, moved)
                twice = plus(further, beta, twice)
        out = [w * one for w, one in zip(weights, planes_of)]
        return (out[0] + out[1]) + (out[2] + out[3])

    def cycle(it, carry):
        first = SUBSTEPS + 2 * it
        second = first + 1
        pressure = pres[...]
        local = work[first, 0]
        mixed = split(pressure * fields[1][...] + fields[2][...] * local)
        flat = right_dot(mixed, M_JYW).reshape(8, 16, 128)
        bent = right_dot(mixed, M_KY, True).reshape(8, 16, 128)
        tile = jnp.zeros((8, 128), jnp.float32)
        for zi in range(4):
            total = (0.5 * weighted(kz, zi, flat)) * spans[1][...]
            if zi in (1, 2):
                total = total + (0.5 * weighted(wjz, zi, bent)) * spans[1][...]
                total = total + weighted(wjz, zi, flat) * spans[2][...]
            row = -jnp.sum(total, axis=0, keepdims=True)
            if zi in (1, 2):
                row = csrc[zi : zi + 1, :] + row
            tile = jnp.where(sublane == lax.rem(place + zi + 7, 8), row, tile)
        g1[it, place] = tile
        for copy in a_copies(it):
            copy.start()
        stage_corners(first, 1)
        stage_faces(first, 1)
        send_near(first, 1)
        begin_near(first, 1)

        take(a_recv.at[it], a_rows)
        lower, upper = sublane < 4, sublane >= 4

        def some(mask, x):
            return jnp.where(mask, x, 0.0)

        first_edge = g1[it, 6] + g1[it, 7] + g1[it, 8]
        last_edge = g1[it, 14] + g1[it, 15]
        base = g1[it, 0]
        tops = [
            (g1[it, 1] + g1[it, 2]) + (g1[it, 3] + g1[it, 4]) + (g1[it, 5] + some(lower, base))
            + some(upper, first_edge),
            (g1[it, 9] + g1[it, 10]) + (g1[it, 11] + g1[it, 12]) + g1[it, 13]
            + (some(lower, first_edge) + some(upper, last_edge)),
            some(lower, last_edge) + pltpu.roll(some(upper, base), 3, 0),
        ]
        for k in range(3):
            g2[it, slot, 8 * k : 8 * k + 8, :] = pltpu.roll(tops[k], turn, 1)
        for copy in b_copies(it):
            copy.start()

        finish_near(first, 1)
        pressure = pressure + fields[2][...] * acc[0]
        pres[...] = pressure
        work[second, 0] = minus_laplace(pressure)
        stage_corners(second, 1)
        stage_faces(second, 1)
        send_near(second, 1)
        begin_near(second, 1)

        take(b_recv.at[it], b_rows)
        pieces, walls = [], []
        for x in range(planes):
            before, after = (x - 1) % planes, (x + 1) % planes
            for k in range(2):
                sums = [None] * 3
                for sy in range(4):
                    one = g2[it, 4 * x + sy, 8 * k : 8 * k + 8, :]
                    if k == 0:
                        one = one + some(sublane < 2, g2[it, 4 * before + sy, 16:24, :])
                    else:
                        extra = pltpu.roll(g2[it, 4 * after + sy, 16:24, :], 5, 0)
                        one = one + some(sublane == 7, extra)
                    for n in range(3):
                        at = 8 + 3 * sy + n
                        part = one * rows[at : at + 1, :]
                        sums[n] = part if sums[n] is None else sums[n] + part
                pieces.append(sums[0])
                walls.append(pltpu.roll(sums[1], 48, 1) + pltpu.roll(sums[2], 97, 1))
        right_side = [jnp.concatenate(pieces, axis=0), jnp.concatenate(walls, axis=0)]
        own = conjugate(right_side)
        vertex = [own[v : v + 1, :] for v in range(4)]

        interp, image = [], []
        for z in range(8):
            value = float(jz[z, 1]) * vertex[1] + float(jz[z, 2]) * vertex[2]
            interp.append(value * spans[0][...])
            part = (float(waz[z]) * value) * spans[2][...]
            if np.any(kz[z] != 0.0):
                bend = None
                for v in range(4):
                    if kz[z, v] != 0.0:
                        term = (0.5 * float(kz[z, v])) * vertex[v]
                        bend = term if bend is None else bend + term
                part = part + bend * spans[1][...]
            image.append(part)
        interp = split(jnp.concatenate(interp, axis=0))
        image = split(jnp.concatenate(image, axis=0))
        correction = right_dot(interp, M_JYT)
        applied = rows[0:1, :] * right_dot(image, M_JYT)
        applied = applied + fields[3][...] * right_dot(interp, M_KYT, True)
        finish_near(second, 1)
        pressure = pres[...] + correction + fields[2][...] * (acc[0] - applied)
        pres[...] = pressure

        @pl.when(it < MG_ITERS - 1)
        def _():
            work[first + 2, 0] = minus_laplace(pressure)

        return carry

    lax.fori_loop(0, MG_ITERS, cycle, 0)
    p_out[...] = pres[...]

    for r in range(ROUNDS):
        take(n_send.at[r], near_rows(3 if r < SUBSTEPS else 1))
    for it in range(MG_ITERS):
        take(a_send.at[it], a_rows)
        take(b_send.at[it], b_rows)


def solution(mesh):
    count = mesh.shape["elem"]
    matrices, small, jz, kz, waz = make_tables()
    planes = count // 16
    f32 = jnp.float32

    def shards(velocity):
        vmem = pl.BlockSpec(memory_space=pltpu.VMEM)
        hbm = pl.BlockSpec(memory_space=pltpu.HBM)
        advected, pressure = pl.pallas_call(
            functools.partial(kernel, (jz, kz, waz), count),
            out_shape=(
                jax.ShapeDtypeStruct((3, 128, 128), f32),
                jax.ShapeDtypeStruct((128, 128), f32),
            ),
            in_specs=[hbm] * 3,
            out_specs=(vmem, vmem),
            scratch_shapes=[
                pltpu.VMEM((3, 128, 128), f32),
                pltpu.VMEM(matrices.shape, jnp.bfloat16),
                pltpu.VMEM(small.shape, f32),
                pltpu.VMEM((128, 128), f32),
                pltpu.VMEM((128, 128), f32),
                pltpu.VMEM((8, 128), f32),
                pltpu.VMEM((ROUNDS, 3, 128, 128), f32),
                pltpu.VMEM((3, 128, 128), f32),
                pltpu.VMEM((ROUNDS, 2, 3, 8, 128), f32),
                pltpu.VMEM((ROUNDS, 4, 8, 128), f32),
                pltpu.VMEM((ROUNDS, 2, 3, 16, 128), f32),
                pltpu.VMEM((ROUNDS, 2, 3, 8, 128), f32),
                pltpu.VMEM((ROUNDS, 4, 8, 128), f32),
                pltpu.VMEM((MG_ITERS, 16, 8, 128), f32),
                pltpu.VMEM((MG_ITERS, 4 * planes, 24, 128), f32),
                pltpu.VMEM((COARSE_ITERS, 2, count + 16, 128), f32),
                pltpu.VMEM((360, 128), f32),
                pltpu.SemaphoreType.DMA((3,)),
                pltpu.SemaphoreType.DMA((ROUNDS,)),
                pltpu.SemaphoreType.DMA((ROUNDS,)),
                pltpu.SemaphoreType.DMA((MG_ITERS,)),
                pltpu.SemaphoreType.DMA((MG_ITERS,)),
                pltpu.SemaphoreType.DMA((MG_ITERS,)),
                pltpu.SemaphoreType.DMA((MG_ITERS,)),
                pltpu.SemaphoreType.REGULAR,
                pltpu.SemaphoreType.REGULAR,
            ],
            compiler_params=pltpu.CompilerParams(
                collective_id=0, has_side_effects=True, vmem_limit_bytes=54912 * 1024
            ),
        )(
            velocity.reshape(3, 128, 128),
            jnp.asarray(matrices),
            jnp.asarray(small),
        )
        return advected.reshape(3, 8, 16, 128), pressure.reshape(8, 16, 128)

    return jax.shard_map(
        shards,
        mesh=mesh,
        in_specs=(P(None, "elem", "sub", None),),
        out_specs=(P(None, "elem", "sub", None), P("elem", "sub", None)),
        check_vma=False,
    )
```

```python
import functools

import jax
import jax.numpy as jnp
import ml_dtypes
import numpy as np
from jax import lax
from jax.experimental import pallas as pl
from jax.experimental.pallas import tpu as pltpu
from jax.sharding import PartitionSpec as P

POINTS = 8
SUBSTEPS = 3
MG_ITERS = 3
COARSE_ITERS = 4

TIME_STEP = 0.005
SHIFT_COEF = 0.05
RELAXATION = 0.6
SOURCE_GAIN = 20.0

MESH = pl.DeviceIdType.MESH
ROUNDS = SUBSTEPS + 2 * MG_ITERS
WALL_LANES = [95, 111, 127, 94, 110]


CORNERS = (127, 112, 15, 0)


def legendre_last(points, degree):
    previous = points * 0.0 + 1.0
    current = points + 0.0
    for level in range(2, degree + 1):
        following = ((2 * level - 1) * points * current - (level - 1) * previous) / level
        previous = current
        current = following
    return (previous, current)


def gll_tables(count):
    degree = count - 1
    points = -np.cos(np.pi * np.arange(count) / degree)
    for sweep in range(100):
        before_last, last_value = legendre_last(points, degree)
        points = points - (points * last_value - before_last) / (count * last_value)
    before_last, legendre = legendre_last(points, degree)
    weights = 2.0 / (degree * (degree + 1) * legendre**2)
    spacing = points[:, None] - points[None, :] + np.eye(count)
    matrix = legendre[:, None] / (legendre[None, :] * spacing) * (1.0 - np.eye(count))
    matrix[0, 0] = -degree * (degree + 1) / 4.0
    matrix[degree, degree] = degree * (degree + 1) / 4.0
    return (points, weights, matrix)


def assembled(values, walls):
    blocks = values.reshape(-1, POINTS)
    out = blocks.copy()
    out[:, 0] += blocks[:, -1]
    out[:, -1] += blocks[:, 0]
    if walls:
        out[0, 0] = blocks[0, 0]
        out[-1, -1] = blocks[-1, -1]
    return out.reshape(-1)


def coarse_tables(elements, lift, stiff, walls):
    count = elements * POINTS
    vertices = elements + 1
    interp = np.zeros((count, vertices + 2))
    slope = np.zeros((count, vertices + 2))
    edge = stiff @ lift
    for element in range(elements):
        for point in range(POINTS):
            row = element * POINTS + point
            pairs = [(element, point)]
            if point == 0 and not (walls and element == 0):
                pairs.append((element - 1, POINTS - 1))
            if point == POINTS - 1 and not (walls and element == elements - 1):
                pairs.append((element + 1, 0))
            for side in (0, 1):
                interp[row, element + side + 1] += lift[point, side]
                for other, at in pairs:
                    slope[row, other + side + 1] += edge[at, side]
    slope[np.abs(slope) < 1e-12] = 0.0
    return (interp[:, 1:-1], slope[:, 1:-1]) if walls else (interp, slope)


def halves(matrix):
    whole = np.asarray(matrix, np.float32)
    high = whole.astype(ml_dtypes.bfloat16)
    low = (whole - high.astype(np.float32)).astype(ml_dtypes.bfloat16)
    return np.stack([high, low])


def make_tables():
    points, weights, deriv = gll_tables(POINTS)
    stiff = deriv.T @ np.diag(weights) @ deriv
    scaled = np.diag(1.0 / weights) @ stiff
    squares = (deriv * deriv).T @ weights
    lift = np.stack([(1.0 - points) / 2.0, (1.0 + points) / 2.0], axis=1)
    kron, eye = np.kron, np.eye
    wz, wx, wy = weights, np.tile(weights, 2), np.tile(weights, 16)
    waz, wax, way = assembled(wz, False), assembled(wx, False), assembled(wy, True)
    saz = assembled(squares, False)
    sax = assembled(np.tile(squares, 2), False)
    say = assembled(np.tile(squares, 16), True)

    def outer(a, b, c):
        return kron(a, b)[:, None] * c[None, :]

    local = outer(wz, wx, wy) / 8.0
    mass = outer(waz, wax, way) / 8.0
    diagonal = 0.5 * (outer(saz, wax, way) + outer(waz, sax, way) + outer(waz, wax, say))
    diagonal = diagonal + SHIFT_COEF * mass
    jz, kz = coarse_tables(1, lift, stiff, False)
    jx, kx = coarse_tables(2, lift, stiff, False)
    jy, ky = coarse_tables(16, lift, stiff, True)

    def lanes(table):
        out = np.zeros((table.shape[0], 128))
        out[:, :80] = np.tile(table[:, :16], (1, 5))
        out[:, WALL_LANES] = table[:, 16:17]
        return out

    def across(table):
        out = np.zeros((table.shape[0], 128))
        out[:, :80] = np.repeat(table, 16, axis=1)
        out[:, WALL_LANES] = table
        return out

    left = kron(scaled, eye(16)) + kron(eye(8), kron(eye(2), scaled)) + SHIFT_COEF / 4.0 * eye(128)
    matrices = [
        kron(deriv, eye(16)),
        kron(eye(8), kron(eye(2), deriv)),
        left,
        kron(eye(16), deriv).T,
        kron(eye(16), scaled).T,
        lanes(way[:, None] * jy),
        lanes(ky),
        lanes(jy),
        lanes(jy).T,
        lanes(ky).T,
    ]
    pairs = [halves(one) for one in matrices]
    flat = [pairs[0][0], pairs[1][0], pairs[0][1], pairs[1][1]]
    for pair in pairs[2:]:
        flat.extend([pair[0], pair[1]])
    matrices = np.concatenate(flat)
    fields = np.stack(
        [
            4.0 * local,
            local / mass,
            RELAXATION / diagonal,
            0.5 * outer(waz, wax, np.ones(128)),
        ]
    ).astype(np.float32)
    lane = np.arange(128)
    level = lane % 16
    rows = np.zeros((40, 128), np.float32)
    rows[24:32] = deriv[0][:, None]
    rows[32:40] = deriv[-1][:, None]
    rows[0] = way
    rows[1] = np.where(level == 0, 1.0, 2.0)
    rows[2] = level < 15
    rows[3] = level > 0
    rows[4] = level == 15
    for k in range(5):
        spot = lane if k == 4 else (lane - 32 * k + 16) % 128
        rows[8 + 3 * k] = spot < 80
        rows[9 + 3 * k] = (spot >= 80) & (spot % 16 == 15)
        rows[10 + 3 * k] = (spot >= 80) & (spot < 112) & (spot % 16 == 14)
    kinds = [jx, wax[:, None] * jx, 0.5 * kx + SHIFT_COEF / 8.0 * wax[:, None] * jx]
    spans = np.stack([across(one) for one in kinds]).astype(np.float32)
    small = np.concatenate([fields.reshape(-1, 128), rows, spans.reshape(-1, 128)])
    return matrices, small, jz, kz, waz


M_DY, M_RIGHT, M_JYW, M_KY, M_JY, M_JYT, M_KYT = range(768, 768 + 7 * 256, 256)
M_LEFT = 512


def kernel(
    zcoef,
    count,
    vel_in,
    mats_in,
    small_in,
    adv_out,
    p_out,
    vel,
    mats,
    small,
    sloc,
    pres,
    csrc,
    work,
    acc,
    xs,
    co,
    zr,
    xr,
    cr,
    g1,
    g2,
    ext,
    gauge,
    load,
    n_send,
    n_recv,
    a_send,
    a_recv,
    b_send,
    b_recv,
    known_side,
    known_row,
):
    jz, kz, waz = zcoef
    planes = count // 16
    fields = [small.at[pl.ds(128 * k, 128)] for k in range(4)]
    rows = small.at[pl.ds(512, 40)]
    spans = [small.at[pl.ds(552 + 16 * k, 16)] for k in range(3)]
    elem = lax.axis_index("elem")
    sub = lax.axis_index("sub")
    plane = elem // 16
    place = elem % 16
    slot = plane * 4 + sub
    turn = lax.rem(32 * sub + 112, 128)

    def near(de, ds):
        return (lax.rem(elem + de + count, count), lax.rem(sub + ds + 4, 4))

    def along(dj):
        return (plane * 16 + lax.rem(place + dj, 16), sub)

    def over(dx, ds):
        return (lax.rem(plane + dx, planes) * 16 + place, lax.rem(sub + ds, 4))

    near_ids = [
        near(1, 1),
        near(1, -1),
        near(-1, 1),
        near(-1, -1),
        near(1, 0),
        near(-1, 0),
        near(0, 1),
        near(0, -1),
    ]
    a_ids = [along(dj) for dj in sorted(range(1, 16), key=lambda d: -min(d, 16 - d))]
    steps = [(dx, ds) for dx in range(planes) for ds in range(4) if dx or ds]
    steps = sorted(steps, key=lambda d: -(min(d[0], planes - d[0]) + min(d[1], 4 - d[1])))
    b_ids = [over(dx, ds) for dx, ds in steps]
    side_ids = [along(4), along(12)]
    row_ids = [over(dx, 0) for dx in range(1, planes)]

    loads = [
        pltpu.make_async_copy(src, dst, load.at[k])
        for k, (src, dst) in enumerate(
            ((vel_in, vel), (mats_in, mats), (small_in, small))
        )
    ]
    barrier = pltpu.get_barrier_semaphore()
    partners = near_ids + side_ids + [along(2), along(14)] + row_ids
    for one in partners:
        pl.semaphore_signal(barrier, inc=1, device_id=one, device_id_type=MESH)
    for copy in loads:
        copy.start()

    sublane = lax.broadcasted_iota(jnp.int32, (8, 128), 0)
    lane = lax.broadcasted_iota(jnp.int32, (1, 128), 1)
    low_lane = jnp.where((lane % 8 == 0) & (lane > 0), 1.0, 0.0)
    high_lane = jnp.where((lane % 8 == 7) & (lane < 127), 1.0, 0.0)

    def split(x):
        high = x.astype(jnp.bfloat16)
        return high, (x - high.astype(jnp.float32)).astype(jnp.bfloat16)

    def mul(a, b):
        return jnp.dot(a, b, preferred_element_type=jnp.float32)

    def rows_of(at, number):
        return mats[at : at + 128 * number, :]

    def slopes(parts):
        high, low = parts
        big, small_part = mul(rows_of(0, 4), high), mul(rows_of(0, 2), low)
        along_z = big[0:128] + (big[256:384] + small_part[0:128])
        along_x = big[128:256] + (big[384:512] + small_part[128:256])
        return along_z, along_x

    def left_dot(at, parts):
        high, low = parts
        big = mul(rows_of(at, 2), high)
        return big[0:128] + (big[128:256] + mul(rows_of(at, 1), low))

    def right_dot(parts, at, exact=False):
        high, low = parts
        size = high.shape[0]
        rest = mul(low, rows_of(at, 1))
        if exact:
            return mul(high, rows_of(at, 1)) + rest
        return mul(jnp.concatenate([high, high], axis=1), rows_of(at, 2)) + rest

    def near_copies(r, comps, part=slice(None)):
        pairs = [
            (co.at[r, 0], cr.at[r, 0]),
            (co.at[r, 1], cr.at[r, 1]),
            (co.at[r, 2], cr.at[r, 2]),
            (co.at[r, 3], cr.at[r, 3]),
            (work.at[r, pl.ds(0, comps), pl.ds(112, 16)], zr.at[r, 0, pl.ds(0, comps)]),
            (work.at[r, pl.ds(0, comps), pl.ds(0, 16)], zr.at[r, 1, pl.ds(0, comps)]),
            (xs.at[r, 1, pl.ds(0, comps)], xr.at[r, 0, pl.ds(0, comps)]),
            (xs.at[r, 0, pl.ds(0, comps)], xr.at[r, 1, pl.ds(0, comps)]),
        ]
        return [
            pltpu.make_async_remote_copy(
                src_ref=src,
                dst_ref=dst,
                send_sem=n_send.at[r],
                recv_sem=n_recv.at[r],
                device_id=near_ids[k],
                device_id_type=MESH,
            )
            for k, (src, dst) in list(enumerate(pairs))[part]
        ]

    def take(sem, count_rows):
        part = gauge.at[pl.ds(0, count_rows)]
        pltpu.make_async_copy(part, part, sem).wait()

    def near_rows(comps):
        return 32 + 48 * comps

    def stage_corners(r, comps):
        for corner, row in enumerate(CORNERS):
            tile = jnp.zeros((8, 128), jnp.float32)
            for c in range(comps):
                tile = jnp.where(sublane == c, work[r, c, row : row + 1, :], tile)
            co[r, corner] = tile

    def stage_faces(r, comps):
        for c in range(comps):
            xs[r, 0, c] = work[r, c, pl.ds(0, 8, stride=16), :]
            xs[r, 1, c] = work[r, c, pl.ds(15, 8, stride=16), :]

    def send_near(r, comps, part=slice(None)):
        for copy in near_copies(r, comps, part):
            copy.start()

    def share_y(field):
        return (
            field
            + low_lane * pltpu.roll(field, 1, 1)
            + high_lane * pltpu.roll(field, 127, 1)
        )

    def begin_near(r, comps):
        for c in range(comps):
            acc[c] = share_y(work[r, c])
            both = acc[c, pl.ds(7, 8, stride=16), :] + acc[c, pl.ds(8, 8, stride=16), :]
            acc[c, pl.ds(7, 8, stride=16), :] = both
            acc[c, pl.ds(8, 8, stride=16), :] = both

    def finish_near(r, comps):
        take(n_recv.at[r], near_rows(comps))
        for c in range(comps):
            for side, row in ((0, 0), (1, 112)):
                first = zr[r, side, c, 0:8]
                second = zr[r, side, c, 8:16]
                both = share_y(first + jnp.where(sublane == 7, pltpu.roll(second, 7, 0), 0.0))
                acc[c, row : row + 8] = acc[c, row : row + 8] + both
                both = share_y(second + jnp.where(sublane == 0, pltpu.roll(first, 1, 0), 0.0))
                acc[c, row + 8 : row + 16] = acc[c, row + 8 : row + 16] + both
            for side, row in ((0, 0), (1, 15)):
                face = xr[r, side, c]
                face = face + jnp.where(sublane == 0, cr[r, side, c : c + 1, :], 0.0)
                face = face + jnp.where(sublane == 7, cr[r, 2 + side, c : c + 1, :], 0.0)
                acc[c, pl.ds(row, 8, stride=16), :] = acc[c, pl.ds(row, 8, stride=16), :] + share_y(face)

    def advect_corners(i):
        ends = (rows[24:32, :], rows[32:40, :])
        values, lines = [], []
        for row in CORNERS:
            last_z, last_x = int(row >= 112), int(row % 16 == 15)
            value = jnp.zeros((8, 128), jnp.float32)
            slope_z, slope_x = value, value
            for c in range(3):
                mine = sublane == c
                value = jnp.where(mine, vel[c, row : row + 1, :], value)
                line = vel[c, pl.ds(15 * last_x, 8, stride=16), :] * ends[last_z]
                slope_z = jnp.where(mine, jnp.sum(line, axis=0, keepdims=True), slope_z)
                at = 112 * last_z + 8 * last_x
                line = vel[c, at : at + 8, :] * ends[last_x]
                slope_x = jnp.where(mine, jnp.sum(line, axis=0, keepdims=True), slope_x)
            values.append(value)
            lines.append((slope_z, slope_x))
        slope_y = right_dot(split(jnp.concatenate(values, axis=0)), M_DY)
        for k, row in enumerate(CORNERS):
            tile = vel[0, row : row + 1, :] * lines[k][0] + vel[1, row : row + 1, :] * lines[k][1]
            tile = tile + vel[2, row : row + 1, :] * slope_y[8 * k : 8 * k + 8]
            co[i, k] = tile * ((2.0 * TIME_STEP) * fields[1][row : row + 1, :])

    def advect(i):
        parts = [split(vel[c]) for c in range(3)]
        stacked = [jnp.concatenate([one[n] for one in parts], axis=0) for n in range(2)]
        along_y = right_dot(stacked, M_DY)
        for c in range(3):
            along_z, along_x = slopes(parts[c])
            term = vel[0] * along_z + vel[1] * along_x
            term = term + vel[2] * along_y[128 * c : 128 * c + 128]
            work[i, c] = term * ((2.0 * TIME_STEP) * fields[1][...])

    for copy in loads:
        copy.wait()
    advect_corners(0)
    advect(0)
    stage_faces(0, 3)
    pl.semaphore_wait(barrier, len(partners))
    send_near(0, 3)

    def pass_on(known, ids):
        for one in ids:
            pl.semaphore_signal(known, inc=1, device_id=one, device_id_type=MESH)
        pl.semaphore_wait(known, len(ids))

    def substep(i, carry):
        @pl.when(i == 0)
        def _():
            pass_on(known_side, side_ids)

        @pl.when(i == 1)
        def _():
            pass_on(known_row, row_ids)

        begin_near(i, 3)
        finish_near(i, 3)
        for c in range(3):
            vel[c] = vel[c] - acc[c]

        @pl.when(i < SUBSTEPS - 1)
        def _():
            advect_corners(i + 1)
            send_near(i + 1, 3, slice(0, 4))
            advect(i + 1)
            stage_faces(i + 1, 3)
            send_near(i + 1, 3, slice(4, 8))

        return carry

    lax.fori_loop(0, SUBSTEPS, substep, 0)

    for c in range(3):
        adv_out[c] = vel[c]
    def weighted(table, zi, field):
        total = None
        for z in range(8):
            if table[z, zi] != 0.0:
                one = float(table[z, zi]) * field[z]
                total = one if total is None else total + one
        return total

    divergence = slopes(split(vel[0]))[0] + slopes(split(vel[1]))[1]
    divergence = divergence + right_dot(split(vel[2]), M_DY)
    source = (-SOURCE_GAIN / 4.0) * fields[0][...] * divergence
    sloc[...] = source
    pres[...] = jnp.zeros_like(source)
    work[SUBSTEPS, 0] = source
    direct = right_dot(split(source), M_JY).reshape(8, 16, 128)
    for zi in (1, 2):
        row = jnp.sum(weighted(jz, zi, direct) * spans[0][...], axis=0, keepdims=True)
        csrc[zi : zi + 1, :] = row

    wjz = waz[:, None] * jz

    def minus_laplace(field):
        parts = split(field)
        return sloc[...] - fields[0][...] * (left_dot(M_LEFT, parts) + right_dot(parts, M_RIGHT))

    a_rows = 4 * len(a_ids)
    b_rows = 19 * len(b_ids)

    def a_copies(it):
        return [
            pltpu.make_async_remote_copy(
                src_ref=g1.at[it, place, pl.ds(0, 4)],
                dst_ref=g1.at[it, place, pl.ds(0, 4)],
                send_sem=a_send.at[it],
                recv_sem=a_recv.at[it],
                device_id=one,
                device_id_type=MESH,
            )
            for one in a_ids
        ]

    def b_copies(it):
        return [
            pltpu.make_async_remote_copy(
                src_ref=g2.at[it, slot, pl.ds(0, 19)],
                dst_ref=g2.at[it, slot, pl.ds(0, 19)],
                send_sem=b_send.at[it],
                recv_sem=b_recv.at[it],
                device_id=one,
                device_id_type=MESH,
            )
            for one in b_ids
        ]

    def coarse_apply(pair):
        my, up, down, top = rows[1:2, :], rows[2:3, :], rows[3:4, :], rows[4:5, :]

        def middle(u):
            near_x = pltpu.roll(u, 16, 1) + pltpu.roll(u, 112, 1)
            near_z = pltpu.roll(u, 1, 0) + pltpu.roll(u, count - 1, 0)
            return 3.025 * u - 0.5 * (near_z + near_x)

        u, wall = pair
        body = my * middle(u) - up * pltpu.roll(u, 127, 1) - down * pltpu.roll(u, 1, 1)
        return [body - top * wall, top * (middle(wall) - u)]

    def inner(a, b):
        total = jnp.sum((a[0] * b[0]).reshape(count // 8, 8, 128), axis=0)
        total = total + jnp.sum((a[1] * b[1]).reshape(-1, 8, 128), axis=0)
        return jnp.sum(jnp.sum(total, axis=0, keepdims=True), axis=1, keepdims=True)

    def plus(a, factor, b):
        return [x + factor * y for x, y in zip(a, b)]

    def own_planes(k, pair):
        for half in range(2):
            ext[k, half, 0:8] = pair[half][count - 8 : count]
            ext[k, half, 8 : 8 + count] = pair[half]
            ext[k, half, 8 + count : 16 + count] = pair[half][0:8]
        body = ext[k, 0, pl.ds(elem + 7, 8), :]
        wall = ext[k, 1, pl.ds(elem + 7, 8), :]
        own = rows[20:21, :] * pltpu.roll(body, lax.rem(256 - turn, 128), 1)
        own = own + rows[21:22, :] * pltpu.roll(wall, lax.rem(208 - turn, 128), 1)
        return own + rows[22:23, :] * pltpu.roll(wall, lax.rem(159 - turn, 128), 1)

    def conjugate(right_side):
        residual = right_side
        image = coarse_apply(residual)
        norm_now = inner(residual, residual)
        energy = inner(residual, image)
        further = coarse_apply(image)
        planes_of = [own_planes(0, residual)]
        alpha = norm_now / energy
        inverse = 1.0 / norm_now
        turned = energy * inverse
        moved, twice = image, further
        along = [jnp.ones_like(alpha)]
        weights = [alpha]
        for sweep in range(1, COARSE_ITERS):
            residual = plus(residual, -alpha, moved)
            image = plus(image, -alpha, twice)
            norm_next = inner(residual, residual)
            energy = inner(residual, image)
            more = sweep < COARSE_ITERS - 1
            if more:
                further = coarse_apply(image)
            planes_of.append(own_planes(sweep, residual))
            beta = norm_next * inverse
            energy = energy - (beta * turned) * norm_next
            alpha = norm_next / energy
            along = [beta * a for a in along] + [jnp.ones_like(alpha)]
            weights = [w + alpha * a for w, a in zip(weights + [jnp.zeros_like(alpha)], along)]
            if more:
                inverse = 1.0 / norm_next
                turned = energy * inverse
                moved = plus(image, beta, moved)
                twice = plus(further, beta, twice)
        out = [w * one for w, one in zip(weights, planes_of)]
        return (out[0] + out[1]) + (out[2] + out[3])

    def cycle(it, carry):
        first = SUBSTEPS + 2 * it
        second = first + 1
        pressure = pres[...]
        local = work[first, 0]
        mixed = split(pressure * fields[1][...] + fields[2][...] * local)
        flat = right_dot(mixed, M_JYW).reshape(8, 16, 128)
        bent = right_dot(mixed, M_KY, True).reshape(8, 16, 128)
        tile = jnp.zeros((8, 128), jnp.float32)
        for zi in range(4):
            total = (0.5 * weighted(kz, zi, flat)) * spans[1][...]
            if zi in (1, 2):
                total = total + (0.5 * weighted(wjz, zi, bent)) * spans[1][...]
                total = total + weighted(wjz, zi, flat) * spans[2][...]
            row = -jnp.sum(total, axis=0, keepdims=True)
            if zi in (1, 2):
                row = csrc[zi : zi + 1, :] + row
            tile = jnp.where(sublane == zi, row, tile)
        g1[it, place] = tile
        for copy in a_copies(it):
            copy.start()
        stage_corners(first, 1)
        stage_faces(first, 1)
        send_near(first, 1)
        begin_near(first, 1)

        take(a_recv.at[it], a_rows)
        lower, upper = sublane < 4, sublane >= 4

        def some(mask, x):
            return jnp.where(mask, x, 0.0)

        part = []
        for n in range(16):
            one = some(lower, g1[it, n])
            part.append(pltpu.roll(one, (n + 7) % 8, 0) if n % 8 != 1 else one)
        first_edge = part[6] + part[7] + part[8]
        last_edge = part[14] + part[15]
        base = part[0]
        tops = [
            (part[1] + part[2]) + (part[3] + part[4]) + (part[5] + some(lower, base))
            + some(upper, first_edge),
            (part[9] + part[10]) + (part[11] + part[12]) + part[13]
            + (some(lower, first_edge) + some(upper, last_edge)),
            some(lower, last_edge) + pltpu.roll(some(upper, base), 3, 0),
        ]
        for k in range(3):
            g2[it, slot, 8 * k : 8 * k + 8, :] = pltpu.roll(tops[k], turn, 1)
        for copy in b_copies(it):
            copy.start()

        finish_near(first, 1)
        pressure = pressure + fields[2][...] * acc[0]
        pres[...] = pressure
        work[second, 0] = minus_laplace(pressure)
        stage_corners(second, 1)
        stage_faces(second, 1)
        send_near(second, 1)
        begin_near(second, 1)

        take(b_recv.at[it], b_rows)
        pieces, walls = [], []
        for x in range(planes):
            before, after = (x - 1) % planes, (x + 1) % planes
            for k in range(2):
                sums = [None] * 3
                for sy in range(4):
                    one = g2[it, 4 * x + sy, 8 * k : 8 * k + 8, :]
                    if k == 0:
                        one = one + some(sublane < 2, g2[it, 4 * before + sy, 16:24, :])
                    else:
                        extra = pltpu.roll(g2[it, 4 * after + sy, 16:24, :], 5, 0)
                        one = one + some(sublane == 7, extra)
                    for n in range(3):
                        at = 8 + 3 * sy + n
                        part = one * rows[at : at + 1, :]
                        sums[n] = part if sums[n] is None else sums[n] + part
                pieces.append(sums[0])
                walls.append(pltpu.roll(sums[1], 48, 1) + pltpu.roll(sums[2], 97, 1))
        right_side = [jnp.concatenate(pieces, axis=0), jnp.concatenate(walls, axis=0)]
        own = conjugate(right_side)
        vertex = [own[v : v + 1, :] for v in range(4)]

        interp, image = [], []
        for z in range(8):
            value = float(jz[z, 1]) * vertex[1] + float(jz[z, 2]) * vertex[2]
            interp.append(value * spans[0][...])
            part = (float(waz[z]) * value) * spans[2][...]
            if np.any(kz[z] != 0.0):
                bend = None
                for v in range(4):
                    if kz[z, v] != 0.0:
                        term = (0.5 * float(kz[z, v])) * vertex[v]
                        bend = term if bend is None else bend + term
                part = part + bend * spans[1][...]
            image.append(part)
        interp = split(jnp.concatenate(interp, axis=0))
        image = split(jnp.concatenate(image, axis=0))
        correction = right_dot(interp, M_JYT)
        applied = rows[0:1, :] * right_dot(image, M_JYT)
        applied = applied + fields[3][...] * right_dot(interp, M_KYT, True)
        finish_near(second, 1)
        pressure = pres[...] + correction + fields[2][...] * (acc[0] - applied)
        pres[...] = pressure

        @pl.when(it < MG_ITERS - 1)
        def _():
            work[first + 2, 0] = minus_laplace(pressure)

        return carry

    lax.fori_loop(0, MG_ITERS, cycle, 0)
    p_out[...] = pres[...]

    for r in range(ROUNDS):
        take(n_send.at[r], near_rows(3 if r < SUBSTEPS else 1))
    for it in range(MG_ITERS):
        take(a_send.at[it], a_rows)
        take(b_send.at[it], b_rows)


def solution(mesh):
    count = mesh.shape["elem"]
    matrices, small, jz, kz, waz = make_tables()
    planes = count // 16
    f32 = jnp.float32

    def shards(velocity):
        vmem = pl.BlockSpec(memory_space=pltpu.VMEM)
        hbm = pl.BlockSpec(memory_space=pltpu.HBM)
        advected, pressure = pl.pallas_call(
            functools.partial(kernel, (jz, kz, waz), count),
            out_shape=(
                jax.ShapeDtypeStruct((3, 128, 128), f32),
                jax.ShapeDtypeStruct((128, 128), f32),
            ),
            in_specs=[hbm] * 3,
            out_specs=(vmem, vmem),
            scratch_shapes=[
                pltpu.VMEM((3, 128, 128), f32),
                pltpu.VMEM(matrices.shape, jnp.bfloat16),
                pltpu.VMEM(small.shape, f32),
                pltpu.VMEM((128, 128), f32),
                pltpu.VMEM((128, 128), f32),
                pltpu.VMEM((8, 128), f32),
                pltpu.VMEM((ROUNDS, 3, 128, 128), f32),
                pltpu.VMEM((3, 128, 128), f32),
                pltpu.VMEM((ROUNDS, 2, 3, 8, 128), f32),
                pltpu.VMEM((ROUNDS, 4, 8, 128), f32),
                pltpu.VMEM((ROUNDS, 2, 3, 16, 128), f32),
                pltpu.VMEM((ROUNDS, 2, 3, 8, 128), f32),
                pltpu.VMEM((ROUNDS, 4, 8, 128), f32),
                pltpu.VMEM((MG_ITERS, 16, 8, 128), f32),
                pltpu.VMEM((MG_ITERS, 4 * planes, 24, 128), f32),
                pltpu.VMEM((COARSE_ITERS, 2, count + 16, 128), f32),
                pltpu.VMEM((360, 128), f32),
                pltpu.SemaphoreType.DMA((3,)),
                pltpu.SemaphoreType.DMA((ROUNDS,)),
                pltpu.SemaphoreType.DMA((ROUNDS,)),
                pltpu.SemaphoreType.DMA((MG_ITERS,)),
                pltpu.SemaphoreType.DMA((MG_ITERS,)),
                pltpu.SemaphoreType.DMA((MG_ITERS,)),
                pltpu.SemaphoreType.DMA((MG_ITERS,)),
                pltpu.SemaphoreType.REGULAR,
                pltpu.SemaphoreType.REGULAR,
            ],
            compiler_params=pltpu.CompilerParams(
                collective_id=0, has_side_effects=True, vmem_limit_bytes=54912 * 1024
            ),
        )(
            velocity.reshape(3, 128, 128),
            jnp.asarray(matrices),
            jnp.asarray(small),
        )
        return advected.reshape(3, 8, 16, 128), pressure.reshape(8, 16, 128)

    return jax.shard_map(
        shards,
        mesh=mesh,
        in_specs=(P(None, "elem", "sub", None),),
        out_specs=(P(None, "elem", "sub", None), P("elem", "sub", None)),
        check_vma=False,
    )
```

```python
import functools

import jax
import jax.numpy as jnp
import ml_dtypes
import numpy as np
from jax import lax
from jax.experimental import pallas as pl
from jax.experimental.pallas import tpu as pltpu
from jax.sharding import PartitionSpec as P

POINTS = 8
SUBSTEPS = 3
MG_ITERS = 3
COARSE_ITERS = 4

TIME_STEP = 0.005
SHIFT_COEF = 0.05
RELAXATION = 0.6
SOURCE_GAIN = 20.0

MESH = pl.DeviceIdType.MESH
ROUNDS = SUBSTEPS + 2 * MG_ITERS
WALL_LANES = [95, 111, 127, 94, 110]


CORNERS = (127, 112, 15, 0)


def legendre_last(points, degree):
    previous = points * 0.0 + 1.0
    current = points + 0.0
    for level in range(2, degree + 1):
        following = ((2 * level - 1) * points * current - (level - 1) * previous) / level
        previous = current
        current = following
    return (previous, current)


def gll_tables(count):
    degree = count - 1
    points = -np.cos(np.pi * np.arange(count) / degree)
    for sweep in range(100):
        before_last, last_value = legendre_last(points, degree)
        points = points - (points * last_value - before_last) / (count * last_value)
    before_last, legendre = legendre_last(points, degree)
    weights = 2.0 / (degree * (degree + 1) * legendre**2)
    spacing = points[:, None] - points[None, :] + np.eye(count)
    matrix = legendre[:, None] / (legendre[None, :] * spacing) * (1.0 - np.eye(count))
    matrix[0, 0] = -degree * (degree + 1) / 4.0
    matrix[degree, degree] = degree * (degree + 1) / 4.0
    return (points, weights, matrix)


def assembled(values, walls):
    blocks = values.reshape(-1, POINTS)
    out = blocks.copy()
    out[:, 0] += blocks[:, -1]
    out[:, -1] += blocks[:, 0]
    if walls:
        out[0, 0] = blocks[0, 0]
        out[-1, -1] = blocks[-1, -1]
    return out.reshape(-1)


def coarse_tables(elements, lift, stiff, walls):
    count = elements * POINTS
    vertices = elements + 1
    interp = np.zeros((count, vertices + 2))
    slope = np.zeros((count, vertices + 2))
    edge = stiff @ lift
    for element in range(elements):
        for point in range(POINTS):
            row = element * POINTS + point
            pairs = [(element, point)]
            if point == 0 and not (walls and element == 0):
                pairs.append((element - 1, POINTS - 1))
            if point == POINTS - 1 and not (walls and element == elements - 1):
                pairs.append((element + 1, 0))
            for side in (0, 1):
                interp[row, element + side + 1] += lift[point, side]
                for other, at in pairs:
                    slope[row, other + side + 1] += edge[at, side]
    slope[np.abs(slope) < 1e-12] = 0.0
    return (interp[:, 1:-1], slope[:, 1:-1]) if walls else (interp, slope)


def halves(matrix):
    whole = np.asarray(matrix, np.float32)
    high = whole.astype(ml_dtypes.bfloat16)
    low = (whole - high.astype(np.float32)).astype(ml_dtypes.bfloat16)
    return np.stack([high, low])


def make_tables():
    points, weights, deriv = gll_tables(POINTS)
    stiff = deriv.T @ np.diag(weights) @ deriv
    scaled = np.diag(1.0 / weights) @ stiff
    squares = (deriv * deriv).T @ weights
    lift = np.stack([(1.0 - points) / 2.0, (1.0 + points) / 2.0], axis=1)
    kron, eye = np.kron, np.eye
    wz, wx, wy = weights, np.tile(weights, 2), np.tile(weights, 16)
    waz, wax, way = assembled(wz, False), assembled(wx, False), assembled(wy, True)
    saz = assembled(squares, False)
    sax = assembled(np.tile(squares, 2), False)
    say = assembled(np.tile(squares, 16), True)

    def outer(a, b, c):
        return kron(a, b)[:, None] * c[None, :]

    local = outer(wz, wx, wy) / 8.0
    mass = outer(waz, wax, way) / 8.0
    diagonal = 0.5 * (outer(saz, wax, way) + outer(waz, sax, way) + outer(waz, wax, say))
    diagonal = diagonal + SHIFT_COEF * mass
    jz, kz = coarse_tables(1, lift, stiff, False)
    jx, kx = coarse_tables(2, lift, stiff, False)
    jy, ky = coarse_tables(16, lift, stiff, True)

    def lanes(table):
        out = np.zeros((table.shape[0], 128))
        out[:, :80] = np.tile(table[:, :16], (1, 5))
        out[:, WALL_LANES] = table[:, 16:17]
        return out

    def across(table):
        out = np.zeros((table.shape[0], 128))
        out[:, :80] = np.repeat(table, 16, axis=1)
        out[:, WALL_LANES] = table
        return out

    left = kron(scaled, eye(16)) + kron(eye(8), kron(eye(2), scaled)) + SHIFT_COEF / 4.0 * eye(128)
    matrices = [
        kron(deriv, eye(16)),
        kron(eye(8), kron(eye(2), deriv)),
        left,
        kron(eye(16), deriv).T,
        kron(eye(16), scaled).T,
        lanes(way[:, None] * jy),
        lanes(ky),
        lanes(jy),
        lanes(jy).T,
        lanes(ky).T,
    ]
    pairs = [halves(one) for one in matrices]
    flat = [pairs[0][0], pairs[1][0], pairs[0][1], pairs[1][1]]
    for pair in pairs[2:]:
        flat.extend([pair[0], pair[1]])
    matrices = np.concatenate(flat)
    fields = np.stack(
        [
            4.0 * local,
            local / mass,
            RELAXATION / diagonal,
            0.5 * outer(waz, wax, np.ones(128)),
        ]
    ).astype(np.float32)
    lane = np.arange(128)
    level = lane % 16
    rows = np.zeros((40, 128), np.float32)
    rows[24:32] = deriv[0][:, None]
    rows[32:40] = deriv[-1][:, None]
    rows[0] = way
    rows[1] = np.where(level == 0, 1.0, 2.0)
    rows[2] = level < 15
    rows[3] = level > 0
    rows[4] = level == 15
    for k in range(5):
        spot = lane if k == 4 else (lane - 32 * k + 16) % 128
        rows[8 + 3 * k] = spot < 80
        rows[9 + 3 * k] = (spot >= 80) & (spot % 16 == 15)
        rows[10 + 3 * k] = (spot >= 80) & (spot < 112) & (spot % 16 == 14)
    kinds = [jx, wax[:, None] * jx, 0.5 * kx + SHIFT_COEF / 8.0 * wax[:, None] * jx]
    spans = np.stack([across(one) for one in kinds]).astype(np.float32)
    small = np.concatenate([fields.reshape(-1, 128), rows, spans.reshape(-1, 128)])
    return matrices, small, jz, kz, waz


M_DY, M_RIGHT, M_JYW, M_KY, M_JY, M_JYT, M_KYT = range(768, 768 + 7 * 256, 256)
M_LEFT = 512


def kernel(
    zcoef,
    count,
    vel_in,
    mats_in,
    small_in,
    adv_out,
    p_out,
    vel,
    mats,
    small,
    sloc,
    pres,
    csrc,
    work,
    acc,
    xs,
    co,
    zr,
    xr,
    cr,
    g1,
    g2,
    ext,
    gauge,
    load,
    n_send,
    n_recv,
    a_send,
    a_recv,
    b_send,
    b_recv,
    known_side,
    known_row,
):
    jz, kz, waz = zcoef
    planes = count // 16
    fields = [small.at[pl.ds(128 * k, 128)] for k in range(4)]
    rows = small.at[pl.ds(512, 40)]
    spans = [small.at[pl.ds(552 + 16 * k, 16)] for k in range(3)]
    elem = lax.axis_index("elem")
    sub = lax.axis_index("sub")
    plane = elem // 16
    place = elem % 16
    slot = plane * 4 + sub
    turn = lax.rem(32 * sub + 112, 128)

    def near(de, ds):
        return (lax.rem(elem + de + count, count), lax.rem(sub + ds + 4, 4))

    def along(dj):
        return (plane * 16 + lax.rem(place + dj, 16), sub)

    def over(dx, ds):
        return (lax.rem(plane + dx, planes) * 16 + place, lax.rem(sub + ds, 4))

    near_ids = [
        near(1, 1),
        near(1, -1),
        near(-1, 1),
        near(-1, -1),
        near(1, 0),
        near(-1, 0),
        near(0, 1),
        near(0, -1),
    ]
    a_ids = [along(dj) for dj in sorted(range(1, 16), key=lambda d: -min(d, 16 - d))]
    steps = [(dx, ds) for dx in range(planes) for ds in range(4) if dx or ds]
    steps = sorted(steps, key=lambda d: -(min(d[0], planes - d[0]) + min(d[1], 4 - d[1])))
    b_ids = [over(dx, ds) for dx, ds in steps]
    side_ids = [along(4), along(12)]
    row_ids = [over(dx, 0) for dx in range(1, planes)]

    loads = [
        pltpu.make_async_copy(src, dst, load.at[k])
        for k, (src, dst) in enumerate(
            ((vel_in, vel), (mats_in, mats), (small_in, small))
        )
    ]
    barrier = pltpu.get_barrier_semaphore()
    partners = near_ids + side_ids + [along(2), along(14)] + row_ids
    for one in partners:
        pl.semaphore_signal(barrier, inc=1, device_id=one, device_id_type=MESH)
    for copy in loads:
        copy.start()

    sublane = lax.broadcasted_iota(jnp.int32, (8, 128), 0)
    lane = lax.broadcasted_iota(jnp.int32, (1, 128), 1)
    low_lane = jnp.where((lane % 8 == 0) & (lane > 0), 1.0, 0.0)
    high_lane = jnp.where((lane % 8 == 7) & (lane < 127), 1.0, 0.0)

    def split(x):
        high = x.astype(jnp.bfloat16)
        return high, (x - high.astype(jnp.float32)).astype(jnp.bfloat16)

    def mul(a, b):
        return jnp.dot(a, b, preferred_element_type=jnp.float32)

    def rows_of(at, number):
        return mats[at : at + 128 * number, :]

    def slopes(parts):
        high, low = parts
        big, small_part = mul(rows_of(0, 4), high), mul(rows_of(0, 2), low)
        along_z = big[0:128] + (big[256:384] + small_part[0:128])
        along_x = big[128:256] + (big[384:512] + small_part[128:256])
        return along_z, along_x

    def left_dot(at, parts):
        high, low = parts
        big = mul(rows_of(at, 2), high)
        return big[0:128] + (big[128:256] + mul(rows_of(at, 1), low))

    def right_dot(parts, at, exact=False):
        high, low = parts
        size = high.shape[0]
        rest = mul(low, rows_of(at, 1))
        if exact:
            return mul(high, rows_of(at, 1)) + rest
        return mul(jnp.concatenate([high, high], axis=1), rows_of(at, 2)) + rest

    def near_copies(r, comps, part=slice(None)):
        pairs = [
            (co.at[r, 0, pl.ds(0, comps)], cr.at[r, 0, pl.ds(0, comps)]),
            (co.at[r, 1, pl.ds(0, comps)], cr.at[r, 1, pl.ds(0, comps)]),
            (co.at[r, 2, pl.ds(0, comps)], cr.at[r, 2, pl.ds(0, comps)]),
            (co.at[r, 3, pl.ds(0, comps)], cr.at[r, 3, pl.ds(0, comps)]),
            (work.at[r, pl.ds(0, comps), pl.ds(112, 16)], zr.at[r, 0, pl.ds(0, comps)]),
            (work.at[r, pl.ds(0, comps), pl.ds(0, 16)], zr.at[r, 1, pl.ds(0, comps)]),
            (xs.at[r, 1, pl.ds(0, comps)], xr.at[r, 0, pl.ds(0, comps)]),
            (xs.at[r, 0, pl.ds(0, comps)], xr.at[r, 1, pl.ds(0, comps)]),
        ]
        return [
            pltpu.make_async_remote_copy(
                src_ref=src,
                dst_ref=dst,
                send_sem=n_send.at[r],
                recv_sem=n_recv.at[r],
                device_id=near_ids[k],
                device_id_type=MESH,
            )
            for k, (src, dst) in list(enumerate(pairs))[part]
        ]

    def take(sem, count_rows):
        part = gauge.at[pl.ds(0, count_rows)]
        pltpu.make_async_copy(part, part, sem).wait()

    def near_rows(comps):
        return 52 * comps

    def stage_corners(r, comps):
        for corner, row in enumerate(CORNERS):
            tile = jnp.zeros((8, 128), jnp.float32)
            for c in range(comps):
                tile = jnp.where(sublane == c, work[r, c, row : row + 1, :], tile)
            co[r, corner] = tile

    def stage_faces(r, comps):
        for c in range(comps):
            xs[r, 0, c] = work[r, c, pl.ds(0, 8, stride=16), :]
            xs[r, 1, c] = work[r, c, pl.ds(15, 8, stride=16), :]

    def send_near(r, comps, part=slice(None)):
        for copy in near_copies(r, comps, part):
            copy.start()

    def share_y(field):
        return (
            field
            + low_lane * pltpu.roll(field, 1, 1)
            + high_lane * pltpu.roll(field, 127, 1)
        )

    def begin_near(r, comps):
        for c in range(comps):
            acc[c] = share_y(work[r, c])
            both = acc[c, pl.ds(7, 8, stride=16), :] + acc[c, pl.ds(8, 8, stride=16), :]
            acc[c, pl.ds(7, 8, stride=16), :] = both
            acc[c, pl.ds(8, 8, stride=16), :] = both

    def finish_near(r, comps):
        take(n_recv.at[r], near_rows(comps))
        for c in range(comps):
            for side, row in ((0, 0), (1, 112)):
                first = zr[r, side, c, 0:8]
                second = zr[r, side, c, 8:16]
                both = share_y(first + jnp.where(sublane == 7, pltpu.roll(second, 7, 0), 0.0))
                acc[c, row : row + 8] = acc[c, row : row + 8] + both
                both = share_y(second + jnp.where(sublane == 0, pltpu.roll(first, 1, 0), 0.0))
                acc[c, row + 8 : row + 16] = acc[c, row + 8 : row + 16] + both
            for side, row in ((0, 0), (1, 15)):
                face = xr[r, side, c]
                face = face + jnp.where(sublane == 0, cr[r, side, c : c + 1, :], 0.0)
                face = face + jnp.where(sublane == 7, cr[r, 2 + side, c : c + 1, :], 0.0)
                acc[c, pl.ds(row, 8, stride=16), :] = acc[c, pl.ds(row, 8, stride=16), :] + share_y(face)

    def advect_corners(i):
        ends = (rows[24:32, :], rows[32:40, :])
        values, lines = [], []
        for row in CORNERS:
            last_z, last_x = int(row >= 112), int(row % 16 == 15)
            value = jnp.zeros((8, 128), jnp.float32)
            slope_z, slope_x = value, value
            for c in range(3):
                mine = sublane == c
                value = jnp.where(mine, vel[c, row : row + 1, :], value)
                line = vel[c, pl.ds(15 * last_x, 8, stride=16), :] * ends[last_z]
                slope_z = jnp.where(mine, jnp.sum(line, axis=0, keepdims=True), slope_z)
                at = 112 * last_z + 8 * last_x
                line = vel[c, at : at + 8, :] * ends[last_x]
                slope_x = jnp.where(mine, jnp.sum(line, axis=0, keepdims=True), slope_x)
            values.append(value)
            lines.append((slope_z, slope_x))
        slope_y = right_dot(split(jnp.concatenate(values, axis=0)), M_DY)
        for k, row in enumerate(CORNERS):
            tile = vel[0, row : row + 1, :] * lines[k][0] + vel[1, row : row + 1, :] * lines[k][1]
            tile = tile + vel[2, row : row + 1, :] * slope_y[8 * k : 8 * k + 8]
            co[i, k] = tile * ((2.0 * TIME_STEP) * fields[1][row : row + 1, :])

    def advect(i):
        parts = [split(vel[c]) for c in range(3)]
        stacked = [jnp.concatenate([one[n] for one in parts], axis=0) for n in range(2)]
        along_y = right_dot(stacked, M_DY)
        for c in range(3):
            along_z, along_x = slopes(parts[c])
            term = vel[0] * along_z + vel[1] * along_x
            term = term + vel[2] * along_y[128 * c : 128 * c + 128]
            work[i, c] = term * ((2.0 * TIME_STEP) * fields[1][...])

    for copy in loads:
        copy.wait()
    advect_corners(0)
    advect(0)
    stage_faces(0, 3)
    pl.semaphore_wait(barrier, len(partners))
    send_near(0, 3)

    def pass_on(known, ids):
        for one in ids:
            pl.semaphore_signal(known, inc=1, device_id=one, device_id_type=MESH)
        pl.semaphore_wait(known, len(ids))

    def substep(i, carry):
        @pl.when(i == 0)
        def _():
            pass_on(known_side, side_ids)

        @pl.when(i == 1)
        def _():
            pass_on(known_row, row_ids)

        begin_near(i, 3)
        finish_near(i, 3)
        for c in range(3):
            vel[c] = vel[c] - acc[c]

        @pl.when(i < SUBSTEPS - 1)
        def _():
            advect_corners(i + 1)
            send_near(i + 1, 3, slice(0, 4))
            advect(i + 1)
            stage_faces(i + 1, 3)
            send_near(i + 1, 3, slice(4, 8))

        return carry

    lax.fori_loop(0, SUBSTEPS, substep, 0)

    for c in range(3):
        adv_out[c] = vel[c]
    def weighted(table, zi, field):
        total = None
        for z in range(8):
            if table[z, zi] != 0.0:
                one = float(table[z, zi]) * field[z]
                total = one if total is None else total + one
        return total

    divergence = slopes(split(vel[0]))[0] + slopes(split(vel[1]))[1]
    divergence = divergence + right_dot(split(vel[2]), M_DY)
    source = (-SOURCE_GAIN / 4.0) * fields[0][...] * divergence
    sloc[...] = source
    pres[...] = jnp.zeros_like(source)
    work[SUBSTEPS, 0] = source
    direct = right_dot(split(source), M_JY).reshape(8, 16, 128)
    for zi in (1, 2):
        row = jnp.sum(weighted(jz, zi, direct) * spans[0][...], axis=0, keepdims=True)
        csrc[zi : zi + 1, :] = row

    wjz = waz[:, None] * jz

    def minus_laplace(field):
        parts = split(field)
        return sloc[...] - fields[0][...] * (left_dot(M_LEFT, parts) + right_dot(parts, M_RIGHT))

    a_rows = 4 * len(a_ids)
    b_rows = 19 * len(b_ids)

    def a_copies(it):
        return [
            pltpu.make_async_remote_copy(
                src_ref=g1.at[it, place, pl.ds(0, 4)],
                dst_ref=g1.at[it, place, pl.ds(0, 4)],
                send_sem=a_send.at[it],
                recv_sem=a_recv.at[it],
                device_id=one,
                device_id_type=MESH,
            )
            for one in a_ids
        ]

    def b_copies(it):
        return [
            pltpu.make_async_remote_copy(
                src_ref=g2.at[it, slot, pl.ds(0, 19)],
                dst_ref=g2.at[it, slot, pl.ds(0, 19)],
                send_sem=b_send.at[it],
                recv_sem=b_recv.at[it],
                device_id=one,
                device_id_type=MESH,
            )
            for one in b_ids
        ]

    def coarse_apply(pair):
        my, up, down, top = rows[1:2, :], rows[2:3, :], rows[3:4, :], rows[4:5, :]

        def middle(u):
            near_x = pltpu.roll(u, 16, 1) + pltpu.roll(u, 112, 1)
            near_z = pltpu.roll(u, 1, 0) + pltpu.roll(u, count - 1, 0)
            return 3.025 * u - 0.5 * (near_z + near_x)

        u, wall = pair
        body = my * middle(u) - up * pltpu.roll(u, 127, 1) - down * pltpu.roll(u, 1, 1)
        return [body - top * wall, top * (middle(wall) - u)]

    def inner(a, b):
        total = jnp.sum((a[0] * b[0]).reshape(count // 8, 8, 128), axis=0)
        total = total + jnp.sum((a[1] * b[1]).reshape(-1, 8, 128), axis=0)
        return jnp.sum(jnp.sum(total, axis=0, keepdims=True), axis=1, keepdims=True)

    def plus(a, factor, b):
        return [x + factor * y for x, y in zip(a, b)]

    def own_planes(k, pair):
        for half in range(2):
            ext[k, half, 0:8] = pair[half][count - 8 : count]
            ext[k, half, 8 : 8 + count] = pair[half]
            ext[k, half, 8 + count : 16 + count] = pair[half][0:8]
        body = ext[k, 0, pl.ds(elem + 7, 8), :]
        wall = ext[k, 1, pl.ds(elem + 7, 8), :]
        own = rows[20:21, :] * pltpu.roll(body, lax.rem(256 - turn, 128), 1)
        own = own + rows[21:22, :] * pltpu.roll(wall, lax.rem(208 - turn, 128), 1)
        return own + rows[22:23, :] * pltpu.roll(wall, lax.rem(159 - turn, 128), 1)

    def conjugate(right_side):
        residual = right_side
        image = coarse_apply(residual)
        norm_now = inner(residual, residual)
        energy = inner(residual, image)
        further = coarse_apply(image)
        planes_of = [own_planes(0, residual)]
        alpha = norm_now / energy
        inverse = 1.0 / norm_now
        turned = energy * inverse
        moved, twice = image, further
        along = [jnp.ones_like(alpha)]
        weights = [alpha]
        for sweep in range(1, COARSE_ITERS):
            residual = plus(residual, -alpha, moved)
            image = plus(image, -alpha, twice)
            norm_next = inner(residual, residual)
            energy = inner(residual, image)
            more = sweep < COARSE_ITERS - 1
            if more:
                further = coarse_apply(image)
            planes_of.append(own_planes(sweep, residual))
            beta = norm_next * inverse
            energy = energy - (beta * turned) * norm_next
            alpha = norm_next / energy
            along = [beta * a for a in along] + [jnp.ones_like(alpha)]
            weights = [w + alpha * a for w, a in zip(weights + [jnp.zeros_like(alpha)], along)]
            if more:
                inverse = 1.0 / norm_next
                turned = energy * inverse
                moved = plus(image, beta, moved)
                twice = plus(further, beta, twice)
        out = [w * one for w, one in zip(weights, planes_of)]
        return (out[0] + out[1]) + (out[2] + out[3])

    def cycle(it, carry):
        first = SUBSTEPS + 2 * it
        second = first + 1
        pressure = pres[...]
        local = work[first, 0]
        mixed = split(pressure * fields[1][...] + fields[2][...] * local)
        flat = right_dot(mixed, M_JYW).reshape(8, 16, 128)
        bent = right_dot(mixed, M_KY, True).reshape(8, 16, 128)
        tile = jnp.zeros((8, 128), jnp.float32)
        for zi in range(4):
            total = (0.5 * weighted(kz, zi, flat)) * spans[1][...]
            if zi in (1, 2):
                total = total + (0.5 * weighted(wjz, zi, bent)) * spans[1][...]
                total = total + weighted(wjz, zi, flat) * spans[2][...]
            row = -jnp.sum(total, axis=0, keepdims=True)
            if zi in (1, 2):
                row = csrc[zi : zi + 1, :] + row
            tile = jnp.where(sublane == zi, row, tile)
        g1[it, place] = tile
        for copy in a_copies(it):
            copy.start()
        stage_corners(first, 1)
        stage_faces(first, 1)
        send_near(first, 1)
        begin_near(first, 1)

        take(a_recv.at[it], a_rows)
        lower, upper = sublane < 4, sublane >= 4

        def some(mask, x):
            return jnp.where(mask, x, 0.0)

        part = []
        for n in range(16):
            one = some(lower, g1[it, n])
            part.append(pltpu.roll(one, (n + 7) % 8, 0) if n % 8 != 1 else one)
        first_edge = part[6] + part[7] + part[8]
        last_edge = part[14] + part[15]
        base = part[0]
        tops = [
            (part[1] + part[2]) + (part[3] + part[4]) + (part[5] + some(lower, base))
            + some(upper, first_edge),
            (part[9] + part[10]) + (part[11] + part[12]) + part[13]
            + (some(lower, first_edge) + some(upper, last_edge)),
            some(lower, last_edge) + pltpu.roll(some(upper, base), 3, 0),
        ]
        for k in range(3):
            g2[it, slot, 8 * k : 8 * k + 8, :] = pltpu.roll(tops[k], turn, 1)
        for copy in b_copies(it):
            copy.start()

        finish_near(first, 1)
        pressure = pressure + fields[2][...] * acc[0]
        pres[...] = pressure
        work[second, 0] = minus_laplace(pressure)
        stage_corners(second, 1)
        stage_faces(second, 1)
        send_near(second, 1)
        begin_near(second, 1)

        take(b_recv.at[it], b_rows)
        pieces, walls = [], []
        for x in range(planes):
            before, after = (x - 1) % planes, (x + 1) % planes
            for k in range(2):
                sums = [None] * 3
                for sy in range(4):
                    one = g2[it, 4 * x + sy, 8 * k : 8 * k + 8, :]
                    if k == 0:
                        one = one + some(sublane < 2, g2[it, 4 * before + sy, 16:24, :])
                    else:
                        extra = pltpu.roll(g2[it, 4 * after + sy, 16:24, :], 5, 0)
                        one = one + some(sublane == 7, extra)
                    for n in range(3):
                        at = 8 + 3 * sy + n
                        part = one * rows[at : at + 1, :]
                        sums[n] = part if sums[n] is None else sums[n] + part
                pieces.append(sums[0])
                walls.append(pltpu.roll(sums[1], 48, 1) + pltpu.roll(sums[2], 97, 1))
        right_side = [jnp.concatenate(pieces, axis=0), jnp.concatenate(walls, axis=0)]
        own = conjugate(right_side)
        vertex = [own[v : v + 1, :] for v in range(4)]

        interp, image = [], []
        for z in range(8):
            value = float(jz[z, 1]) * vertex[1] + float(jz[z, 2]) * vertex[2]
            interp.append(value * spans[0][...])
            part = (float(waz[z]) * value) * spans[2][...]
            if np.any(kz[z] != 0.0):
                bend = None
                for v in range(4):
                    if kz[z, v] != 0.0:
                        term = (0.5 * float(kz[z, v])) * vertex[v]
                        bend = term if bend is None else bend + term
                part = part + bend * spans[1][...]
            image.append(part)
        interp = split(jnp.concatenate(interp, axis=0))
        image = split(jnp.concatenate(image, axis=0))
        correction = right_dot(interp, M_JYT)
        applied = rows[0:1, :] * right_dot(image, M_JYT)
        applied = applied + fields[3][...] * right_dot(interp, M_KYT, True)
        finish_near(second, 1)
        pressure = pres[...] + correction + fields[2][...] * (acc[0] - applied)
        pres[...] = pressure

        @pl.when(it < MG_ITERS - 1)
        def _():
            work[first + 2, 0] = minus_laplace(pressure)

        return carry

    lax.fori_loop(0, MG_ITERS, cycle, 0)
    p_out[...] = pres[...]

    for r in range(ROUNDS):
        take(n_send.at[r], near_rows(3 if r < SUBSTEPS else 1))
    for it in range(MG_ITERS):
        take(a_send.at[it], a_rows)
        take(b_send.at[it], b_rows)


def solution(mesh):
    count = mesh.shape["elem"]
    matrices, small, jz, kz, waz = make_tables()
    planes = count // 16
    f32 = jnp.float32

    def shards(velocity):
        vmem = pl.BlockSpec(memory_space=pltpu.VMEM)
        hbm = pl.BlockSpec(memory_space=pltpu.HBM)
        advected, pressure = pl.pallas_call(
            functools.partial(kernel, (jz, kz, waz), count),
            out_shape=(
                jax.ShapeDtypeStruct((3, 128, 128), f32),
                jax.ShapeDtypeStruct((128, 128), f32),
            ),
            in_specs=[hbm] * 3,
            out_specs=(vmem, vmem),
            scratch_shapes=[
                pltpu.VMEM((3, 128, 128), f32),
                pltpu.VMEM(matrices.shape, jnp.bfloat16),
                pltpu.VMEM(small.shape, f32),
                pltpu.VMEM((128, 128), f32),
                pltpu.VMEM((128, 128), f32),
                pltpu.VMEM((8, 128), f32),
                pltpu.VMEM((ROUNDS, 3, 128, 128), f32),
                pltpu.VMEM((3, 128, 128), f32),
                pltpu.VMEM((ROUNDS, 2, 3, 8, 128), f32),
                pltpu.VMEM((ROUNDS, 4, 8, 128), f32),
                pltpu.VMEM((ROUNDS, 2, 3, 16, 128), f32),
                pltpu.VMEM((ROUNDS, 2, 3, 8, 128), f32),
                pltpu.VMEM((ROUNDS, 4, 8, 128), f32),
                pltpu.VMEM((MG_ITERS, 16, 8, 128), f32),
                pltpu.VMEM((MG_ITERS, 4 * planes, 24, 128), f32),
                pltpu.VMEM((COARSE_ITERS, 2, count + 16, 128), f32),
                pltpu.VMEM((360, 128), f32),
                pltpu.SemaphoreType.DMA((3,)),
                pltpu.SemaphoreType.DMA((ROUNDS,)),
                pltpu.SemaphoreType.DMA((ROUNDS,)),
                pltpu.SemaphoreType.DMA((MG_ITERS,)),
                pltpu.SemaphoreType.DMA((MG_ITERS,)),
                pltpu.SemaphoreType.DMA((MG_ITERS,)),
                pltpu.SemaphoreType.DMA((MG_ITERS,)),
                pltpu.SemaphoreType.REGULAR,
                pltpu.SemaphoreType.REGULAR,
            ],
            compiler_params=pltpu.CompilerParams(
                collective_id=0, has_side_effects=True, vmem_limit_bytes=54912 * 1024
            ),
        )(
            velocity.reshape(3, 128, 128),
            jnp.asarray(matrices),
            jnp.asarray(small),
        )
        return advected.reshape(3, 8, 16, 128), pressure.reshape(8, 16, 128)

    return jax.shard_map(
        shards,
        mesh=mesh,
        in_specs=(P(None, "elem", "sub", None),),
        out_specs=(P(None, "elem", "sub", None), P("elem", "sub", None)),
        check_vma=False,
    )
```

```python
import functools

import jax
import jax.numpy as jnp
import ml_dtypes
import numpy as np
from jax import lax
from jax.experimental import pallas as pl
from jax.experimental.pallas import tpu as pltpu
from jax.sharding import PartitionSpec as P

POINTS = 8
SUBSTEPS = 3
MG_ITERS = 3
COARSE_ITERS = 4

TIME_STEP = 0.005
SHIFT_COEF = 0.05
RELAXATION = 0.6
SOURCE_GAIN = 20.0

MESH = pl.DeviceIdType.MESH
ROUNDS = SUBSTEPS + 2 * MG_ITERS
WALL_LANES = [95, 111, 127, 94, 110]


CORNERS = (127, 112, 15, 0)


def legendre_last(points, degree):
    previous = points * 0.0 + 1.0
    current = points + 0.0
    for level in range(2, degree + 1):
        following = ((2 * level - 1) * points * current - (level - 1) * previous) / level
        previous = current
        current = following
    return (previous, current)


def gll_tables(count):
    degree = count - 1
    points = -np.cos(np.pi * np.arange(count) / degree)
    for sweep in range(100):
        before_last, last_value = legendre_last(points, degree)
        points = points - (points * last_value - before_last) / (count * last_value)
    before_last, legendre = legendre_last(points, degree)
    weights = 2.0 / (degree * (degree + 1) * legendre**2)
    spacing = points[:, None] - points[None, :] + np.eye(count)
    matrix = legendre[:, None] / (legendre[None, :] * spacing) * (1.0 - np.eye(count))
    matrix[0, 0] = -degree * (degree + 1) / 4.0
    matrix[degree, degree] = degree * (degree + 1) / 4.0
    return (points, weights, matrix)


def assembled(values, walls):
    blocks = values.reshape(-1, POINTS)
    out = blocks.copy()
    out[:, 0] += blocks[:, -1]
    out[:, -1] += blocks[:, 0]
    if walls:
        out[0, 0] = blocks[0, 0]
        out[-1, -1] = blocks[-1, -1]
    return out.reshape(-1)


def coarse_tables(elements, lift, stiff, walls):
    count = elements * POINTS
    vertices = elements + 1
    interp = np.zeros((count, vertices + 2))
    slope = np.zeros((count, vertices + 2))
    edge = stiff @ lift
    for element in range(elements):
        for point in range(POINTS):
            row = element * POINTS + point
            pairs = [(element, point)]
            if point == 0 and not (walls and element == 0):
                pairs.append((element - 1, POINTS - 1))
            if point == POINTS - 1 and not (walls and element == elements - 1):
                pairs.append((element + 1, 0))
            for side in (0, 1):
                interp[row, element + side + 1] += lift[point, side]
                for other, at in pairs:
                    slope[row, other + side + 1] += edge[at, side]
    slope[np.abs(slope) < 1e-12] = 0.0
    return (interp[:, 1:-1], slope[:, 1:-1]) if walls else (interp, slope)


def halves(matrix):
    whole = np.asarray(matrix, np.float32)
    high = whole.astype(ml_dtypes.bfloat16)
    low = (whole - high.astype(np.float32)).astype(ml_dtypes.bfloat16)
    return np.stack([high, low])


def make_tables():
    points, weights, deriv = gll_tables(POINTS)
    stiff = deriv.T @ np.diag(weights) @ deriv
    scaled = np.diag(1.0 / weights) @ stiff
    squares = (deriv * deriv).T @ weights
    lift = np.stack([(1.0 - points) / 2.0, (1.0 + points) / 2.0], axis=1)
    kron, eye = np.kron, np.eye
    wz, wx, wy = weights, np.tile(weights, 2), np.tile(weights, 16)
    waz, wax, way = assembled(wz, False), assembled(wx, False), assembled(wy, True)
    saz = assembled(squares, False)
    sax = assembled(np.tile(squares, 2), False)
    say = assembled(np.tile(squares, 16), True)

    def outer(a, b, c):
        return kron(a, b)[:, None] * c[None, :]

    local = outer(wz, wx, wy) / 8.0
    mass = outer(waz, wax, way) / 8.0
    diagonal = 0.5 * (outer(saz, wax, way) + outer(waz, sax, way) + outer(waz, wax, say))
    diagonal = diagonal + SHIFT_COEF * mass
    jz, kz = coarse_tables(1, lift, stiff, False)
    jx, kx = coarse_tables(2, lift, stiff, False)
    jy, ky = coarse_tables(16, lift, stiff, True)

    def lanes(table):
        out = np.zeros((table.shape[0], 128))
        out[:, :80] = np.tile(table[:, :16], (1, 5))
        out[:, WALL_LANES] = table[:, 16:17]
        return out

    def across(table):
        out = np.zeros((table.shape[0], 128))
        out[:, :80] = np.repeat(table, 16, axis=1)
        out[:, WALL_LANES] = table
        return out

    left = kron(scaled, eye(16)) + kron(eye(8), kron(eye(2), scaled)) + SHIFT_COEF / 4.0 * eye(128)
    matrices = [
        kron(deriv, eye(16)),
        kron(eye(8), kron(eye(2), deriv)),
        left,
        kron(eye(16), deriv).T,
        kron(eye(16), scaled).T,
        lanes(way[:, None] * jy),
        lanes(ky),
        lanes(jy),
        lanes(jy).T,
        lanes(ky).T,
    ]
    pairs = [halves(one) for one in matrices]
    flat = [pairs[0][0], pairs[1][0], pairs[0][1], pairs[1][1]]
    for pair in pairs[2:]:
        flat.extend([pair[0], pair[1]])
    matrices = np.concatenate(flat)
    fields = np.stack(
        [
            4.0 * local,
            local / mass,
            RELAXATION / diagonal,
            0.5 * outer(waz, wax, np.ones(128)),
        ]
    ).astype(np.float32)
    lane = np.arange(128)
    level = lane % 16
    rows = np.zeros((40, 128), np.float32)
    rows[24:32] = deriv[0][:, None]
    rows[32:40] = deriv[-1][:, None]
    rows[0] = way
    rows[1] = np.where(level == 0, 1.0, 2.0)
    rows[2] = level < 15
    rows[3] = level > 0
    rows[4] = level == 15
    for k in range(5):
        spot = lane if k == 4 else (lane - 32 * k + 16) % 128
        rows[8 + 3 * k] = spot < 80
        rows[9 + 3 * k] = (spot >= 80) & (spot % 16 == 15)
        rows[10 + 3 * k] = (spot >= 80) & (spot < 112) & (spot % 16 == 14)
    kinds = [jx, wax[:, None] * jx, 0.5 * kx + SHIFT_COEF / 8.0 * wax[:, None] * jx]
    spans = np.stack([across(one) for one in kinds]).astype(np.float32)
    small = np.concatenate([fields.reshape(-1, 128), rows, spans.reshape(-1, 128)])
    return matrices, small, jz, kz, waz


M_DY, M_RIGHT, M_JYW, M_KY, M_JY, M_JYT, M_KYT = range(768, 768 + 7 * 256, 256)
M_LEFT = 512


def kernel(
    zcoef,
    count,
    vel_in,
    mats_in,
    small_in,
    adv_out,
    p_out,
    vel,
    mats,
    small,
    sloc,
    pres,
    csrc,
    work,
    acc,
    xs,
    co,
    zr,
    xr,
    cr,
    g1,
    g2,
    ext,
    gauge,
    load,
    n_send,
    n_recv,
    a_send,
    a_recv,
    b_send,
    b_recv,
    known_side,
    known_row,
):
    jz, kz, waz = zcoef
    planes = count // 16
    fields = [small.at[pl.ds(128 * k, 128)] for k in range(4)]
    rows = small.at[pl.ds(512, 40)]
    spans = [small.at[pl.ds(552 + 16 * k, 16)] for k in range(3)]
    elem = lax.axis_index("elem")
    sub = lax.axis_index("sub")
    plane = elem // 16
    place = elem % 16
    slot = plane * 4 + sub
    turn = lax.rem(32 * sub + 112, 128)

    def near(de, ds):
        return (lax.rem(elem + de + count, count), lax.rem(sub + ds + 4, 4))

    def along(dj):
        return (plane * 16 + lax.rem(place + dj, 16), sub)

    def over(dx, ds):
        return (lax.rem(plane + dx, planes) * 16 + place, lax.rem(sub + ds, 4))

    near_ids = [
        near(1, 1),
        near(1, -1),
        near(-1, 1),
        near(-1, -1),
        near(1, 0),
        near(-1, 0),
        near(0, 1),
        near(0, -1),
    ]
    a_ids = [along(dj) for dj in sorted(range(1, 16), key=lambda d: -min(d, 16 - d))]
    steps = [(dx, ds) for dx in range(planes) for ds in range(4) if dx or ds]
    steps = sorted(steps, key=lambda d: -(min(d[0], planes - d[0]) + min(d[1], 4 - d[1])))
    b_ids = [over(dx, ds) for dx, ds in steps]
    side_ids = [along(4), along(12)]
    row_ids = [over(dx, 0) for dx in range(1, planes)]

    loads = [
        pltpu.make_async_copy(src, dst, load.at[k])
        for k, (src, dst) in enumerate(
            ((vel_in, vel), (mats_in, mats), (small_in, small))
        )
    ]
    barrier = pltpu.get_barrier_semaphore()
    partners = near_ids + side_ids + [along(2), along(14)] + row_ids
    for one in partners:
        pl.semaphore_signal(barrier, inc=1, device_id=one, device_id_type=MESH)
    for copy in loads:
        copy.start()

    sublane = lax.broadcasted_iota(jnp.int32, (8, 128), 0)
    lane = lax.broadcasted_iota(jnp.int32, (1, 128), 1)
    low_lane = jnp.where((lane % 8 == 0) & (lane > 0), 1.0, 0.0)
    high_lane = jnp.where((lane % 8 == 7) & (lane < 127), 1.0, 0.0)

    def split(x):
        high = x.astype(jnp.bfloat16)
        return high, (x - high.astype(jnp.float32)).astype(jnp.bfloat16)

    def mul(a, b):
        return jnp.dot(a, b, preferred_element_type=jnp.float32)

    def rows_of(at, number):
        return mats[at : at + 128 * number, :]

    def slopes(parts):
        high, low = parts
        big, small_part = mul(rows_of(0, 4), high), mul(rows_of(0, 2), low)
        along_z = big[0:128] + (big[256:384] + small_part[0:128])
        along_x = big[128:256] + (big[384:512] + small_part[128:256])
        return along_z, along_x

    def left_dot(at, parts):
        high, low = parts
        big = mul(rows_of(at, 2), high)
        return big[0:128] + (big[128:256] + mul(rows_of(at, 1), low))

    def right_dot(parts, at, exact=False):
        high, low = parts
        size = high.shape[0]
        rest = mul(low, rows_of(at, 1))
        if exact:
            return mul(high, rows_of(at, 1)) + rest
        return mul(jnp.concatenate([high, high], axis=1), rows_of(at, 2)) + rest

    def near_copies(r, comps, part=slice(None)):
        pairs = [
            (co.at[r, 0, pl.ds(0, comps)], cr.at[r, 0, pl.ds(0, comps)]),
            (co.at[r, 1, pl.ds(0, comps)], cr.at[r, 1, pl.ds(0, comps)]),
            (co.at[r, 2, pl.ds(0, comps)], cr.at[r, 2, pl.ds(0, comps)]),
            (co.at[r, 3, pl.ds(0, comps)], cr.at[r, 3, pl.ds(0, comps)]),
            (work.at[r, pl.ds(0, comps), pl.ds(112, 16)], zr.at[r, 0, pl.ds(0, comps)]),
            (work.at[r, pl.ds(0, comps), pl.ds(0, 16)], zr.at[r, 1, pl.ds(0, comps)]),
            (xs.at[r, 1, pl.ds(0, comps)], xr.at[r, 0, pl.ds(0, comps)]),
            (xs.at[r, 0, pl.ds(0, comps)], xr.at[r, 1, pl.ds(0, comps)]),
        ]
        return [
            pltpu.make_async_remote_copy(
                src_ref=src,
                dst_ref=dst,
                send_sem=n_send.at[r],
                recv_sem=n_recv.at[r],
                device_id=near_ids[k],
                device_id_type=MESH,
            )
            for k, (src, dst) in list(enumerate(pairs))[part]
        ]

    def take(sem, count_rows):
        part = gauge.at[pl.ds(0, count_rows)]
        pltpu.make_async_copy(part, part, sem).wait()

    def near_rows(comps):
        return 52 * comps

    def stage_corners(r, comps):
        for corner, row in enumerate(CORNERS):
            tile = jnp.zeros((8, 128), jnp.float32)
            for c in range(comps):
                tile = jnp.where(sublane == c, work[r, c, row : row + 1, :], tile)
            co[r, corner] = tile

    def stage_faces(r, comps):
        for c in range(comps):
            xs[r, 0, c] = work[r, c, pl.ds(0, 8, stride=16), :]
            xs[r, 1, c] = work[r, c, pl.ds(15, 8, stride=16), :]

    def send_near(r, comps, part=slice(None)):
        for copy in near_copies(r, comps, part):
            copy.start()

    def share_y(field):
        return (
            field
            + low_lane * pltpu.roll(field, 1, 1)
            + high_lane * pltpu.roll(field, 127, 1)
        )

    def begin_near(r, comps):
        for c in range(comps):
            acc[c] = share_y(work[r, c])
            both = acc[c, pl.ds(7, 8, stride=16), :] + acc[c, pl.ds(8, 8, stride=16), :]
            acc[c, pl.ds(7, 8, stride=16), :] = both
            acc[c, pl.ds(8, 8, stride=16), :] = both

    def finish_near(r, comps):
        take(n_recv.at[r], near_rows(comps))
        for c in range(comps):
            for side, row in ((0, 0), (1, 112)):
                first = zr[r, side, c, 0:8]
                second = zr[r, side, c, 8:16]
                both = share_y(first + jnp.where(sublane == 7, pltpu.roll(second, 7, 0), 0.0))
                acc[c, row : row + 8] = acc[c, row : row + 8] + both
                both = share_y(second + jnp.where(sublane == 0, pltpu.roll(first, 1, 0), 0.0))
                acc[c, row + 8 : row + 16] = acc[c, row + 8 : row + 16] + both
            for side, row in ((0, 0), (1, 15)):
                face = xr[r, side, c]
                face = face + jnp.where(sublane == 0, cr[r, side, c : c + 1, :], 0.0)
                face = face + jnp.where(sublane == 7, cr[r, 2 + side, c : c + 1, :], 0.0)
                acc[c, pl.ds(row, 8, stride=16), :] = acc[c, pl.ds(row, 8, stride=16), :] + share_y(face)

    def advect_corners(i):
        ends = (rows[24:32, :], rows[32:40, :])
        values, lines = [], []
        for row in CORNERS:
            last_z, last_x = int(row >= 112), int(row % 16 == 15)
            value = jnp.zeros((8, 128), jnp.float32)
            slope_z, slope_x = value, value
            for c in range(3):
                mine = sublane == c
                value = jnp.where(mine, vel[c, row : row + 1, :], value)
                line = vel[c, pl.ds(15 * last_x, 8, stride=16), :] * ends[last_z]
                slope_z = jnp.where(mine, jnp.sum(line, axis=0, keepdims=True), slope_z)
                at = 112 * last_z + 8 * last_x
                line = vel[c, at : at + 8, :] * ends[last_x]
                slope_x = jnp.where(mine, jnp.sum(line, axis=0, keepdims=True), slope_x)
            values.append(value)
            lines.append((slope_z, slope_x))
        slope_y = right_dot(split(jnp.concatenate(values, axis=0)), M_DY)
        for k, row in enumerate(CORNERS):
            tile = vel[0, row : row + 1, :] * lines[k][0] + vel[1, row : row + 1, :] * lines[k][1]
            tile = tile + vel[2, row : row + 1, :] * slope_y[8 * k : 8 * k + 8]
            co[i, k] = tile * ((2.0 * TIME_STEP) * fields[1][row : row + 1, :])

    def advect(i):
        parts = [split(vel[c]) for c in range(3)]
        stacked = [jnp.concatenate([one[n] for one in parts], axis=0) for n in range(2)]
        along_y = right_dot(stacked, M_DY)
        for c in range(3):
            along_z, along_x = slopes(parts[c])
            term = vel[0] * along_z + vel[1] * along_x
            term = term + vel[2] * along_y[128 * c : 128 * c + 128]
            work[i, c] = term * ((2.0 * TIME_STEP) * fields[1][...])

    for copy in loads:
        copy.wait()
    advect_corners(0)
    advect(0)
    stage_faces(0, 3)
    pl.semaphore_wait(barrier, len(partners))
    send_near(0, 3)

    def pass_on(known, ids):
        for one in ids:
            pl.semaphore_signal(known, inc=1, device_id=one, device_id_type=MESH)
        pl.semaphore_wait(known, len(ids))

    def substep(i, carry):
        @pl.when(i == 0)
        def _():
            pass_on(known_side, side_ids)

        @pl.when(i == 1)
        def _():
            pass_on(known_row, row_ids)

        begin_near(i, 3)
        finish_near(i, 3)
        for c in range(3):
            vel[c] = vel[c] - acc[c]

        @pl.when(i < SUBSTEPS - 1)
        def _():
            advect_corners(i + 1)
            send_near(i + 1, 3, slice(0, 4))
            advect(i + 1)
            stage_faces(i + 1, 3)
            send_near(i + 1, 3, slice(4, 8))

        return carry

    lax.fori_loop(0, SUBSTEPS, substep, 0)

    for c in range(3):
        adv_out[c] = vel[c]
    def weighted(table, zi, field):
        total = None
        for z in range(8):
            if table[z, zi] != 0.0:
                one = float(table[z, zi]) * field[z]
                total = one if total is None else total + one
        return total

    divergence = slopes(split(vel[0]))[0] + slopes(split(vel[1]))[1]
    divergence = divergence + right_dot(split(vel[2]), M_DY)
    source = (-SOURCE_GAIN / 4.0) * fields[0][...] * divergence
    sloc[...] = source
    pres[...] = jnp.zeros_like(source)
    work[SUBSTEPS, 0] = source
    direct = right_dot(split(source), M_JY).reshape(8, 16, 128)
    for zi in (1, 2):
        row = jnp.sum(weighted(jz, zi, direct) * spans[0][...], axis=0, keepdims=True)
        csrc[zi : zi + 1, :] = row

    wjz = waz[:, None] * jz

    def minus_laplace(field):
        parts = split(field)
        return sloc[...] - fields[0][...] * (left_dot(M_LEFT, parts) + right_dot(parts, M_RIGHT))

    a_rows = 4 * len(a_ids)
    b_rows = 19 * len(b_ids)

    def a_copies(it):
        return [
            pltpu.make_async_remote_copy(
                src_ref=g1.at[it, place, pl.ds(0, 4)],
                dst_ref=g1.at[it, place, pl.ds(0, 4)],
                send_sem=a_send.at[it],
                recv_sem=a_recv.at[it],
                device_id=one,
                device_id_type=MESH,
            )
            for one in a_ids
        ]

    def b_copies(it):
        return [
            pltpu.make_async_remote_copy(
                src_ref=g2.at[it, slot, pl.ds(0, 19)],
                dst_ref=g2.at[it, slot, pl.ds(0, 19)],
                send_sem=b_send.at[it],
                recv_sem=b_recv.at[it],
                device_id=one,
                device_id_type=MESH,
            )
            for one in b_ids
        ]

    def coarse_apply(pair):
        my, up, down, top = rows[1:2, :], rows[2:3, :], rows[3:4, :], rows[4:5, :]

        def middle(u):
            near_x = pltpu.roll(u, 16, 1) + pltpu.roll(u, 112, 1)
            near_z = pltpu.roll(u, 1, 0) + pltpu.roll(u, count - 1, 0)
            return 3.025 * u - 0.5 * (near_z + near_x)

        u, wall = pair
        body = my * middle(u) - up * pltpu.roll(u, 127, 1) - down * pltpu.roll(u, 1, 1)
        return [body - top * wall, top * (middle(wall) - u)]

    def inner(a, b):
        total = jnp.sum((a[0] * b[0]).reshape(count // 8, 8, 128), axis=0)
        total = total + jnp.sum((a[1] * b[1]).reshape(-1, 8, 128), axis=0)
        return jnp.sum(jnp.sum(total, axis=0, keepdims=True), axis=1, keepdims=True)

    def plus(a, factor, b):
        return [x + factor * y for x, y in zip(a, b)]

    def own_planes(k, pair):
        for half in range(2):
            ext[k, half, 0:8] = pair[half][count - 8 : count]
            ext[k, half, 8 : 8 + count] = pair[half]
            ext[k, half, 8 + count : 16 + count] = pair[half][0:8]
        body = ext[k, 0, pl.ds(elem + 7, 8), :]
        wall = ext[k, 1, pl.ds(elem + 7, 8), :]
        own = rows[20:21, :] * pltpu.roll(body, lax.rem(256 - turn, 128), 1)
        own = own + rows[21:22, :] * pltpu.roll(wall, lax.rem(208 - turn, 128), 1)
        return own + rows[22:23, :] * pltpu.roll(wall, lax.rem(159 - turn, 128), 1)

    def conjugate(right_side):
        residual = right_side
        image = coarse_apply(residual)
        norm_now = inner(residual, residual)
        energy = inner(residual, image)
        further = coarse_apply(image)
        planes_of = [own_planes(0, residual)]
        alpha = norm_now / energy
        inverse = 1.0 / norm_now
        turned = energy * inverse
        moved, twice = image, further
        along = [jnp.ones_like(alpha)]
        weights = [alpha]
        for sweep in range(1, COARSE_ITERS):
            residual = plus(residual, -alpha, moved)
            image = plus(image, -alpha, twice)
            norm_next = inner(residual, residual)
            energy = inner(residual, image)
            more = sweep < COARSE_ITERS - 1
            if more:
                further = coarse_apply(image)
            planes_of.append(own_planes(sweep, residual))
            beta = norm_next * inverse
            energy = energy - (beta * turned) * norm_next
            alpha = norm_next / energy
            along = [beta * a for a in along] + [jnp.ones_like(alpha)]
            weights = [w + alpha * a for w, a in zip(weights + [jnp.zeros_like(alpha)], along)]
            if more:
                inverse = 1.0 / norm_next
                turned = energy * inverse
                moved = plus(image, beta, moved)
                twice = plus(further, beta, twice)
        out = [w * one for w, one in zip(weights, planes_of)]
        return (out[0] + out[1]) + (out[2] + out[3])

    def cycle(it, carry):
        first = SUBSTEPS + 2 * it
        second = first + 1
        pressure = pres[...]
        local = work[first, 0]
        stage_corners(first, 1)
        send_near(first, 1, slice(0, 4))
        mixed = split(pressure * fields[1][...] + fields[2][...] * local)
        flat = right_dot(mixed, M_JYW).reshape(8, 16, 128)
        bent = right_dot(mixed, M_KY, True).reshape(8, 16, 128)
        tile = jnp.zeros((8, 128), jnp.float32)
        for zi in range(4):
            total = (0.5 * weighted(kz, zi, flat)) * spans[1][...]
            if zi in (1, 2):
                total = total + (0.5 * weighted(wjz, zi, bent)) * spans[1][...]
                total = total + weighted(wjz, zi, flat) * spans[2][...]
            row = -jnp.sum(total, axis=0, keepdims=True)
            if zi in (1, 2):
                row = csrc[zi : zi + 1, :] + row
            tile = jnp.where(sublane == zi, row, tile)
        g1[it, place] = tile
        for copy in a_copies(it):
            copy.start()
        stage_faces(first, 1)
        send_near(first, 1, slice(4, 8))
        begin_near(first, 1)

        take(a_recv.at[it], a_rows)
        lower, upper = sublane < 4, sublane >= 4

        def some(mask, x):
            return jnp.where(mask, x, 0.0)

        part = []
        for n in range(16):
            one = some(lower, g1[it, n])
            part.append(pltpu.roll(one, (n + 7) % 8, 0) if n % 8 != 1 else one)
        first_edge = part[6] + part[7] + part[8]
        last_edge = part[14] + part[15]
        base = part[0]
        tops = [
            (part[1] + part[2]) + (part[3] + part[4]) + (part[5] + some(lower, base))
            + some(upper, first_edge),
            (part[9] + part[10]) + (part[11] + part[12]) + part[13]
            + (some(lower, first_edge) + some(upper, last_edge)),
            some(lower, last_edge) + pltpu.roll(some(upper, base), 3, 0),
        ]
        for k in range(3):
            g2[it, slot, 8 * k : 8 * k + 8, :] = pltpu.roll(tops[k], turn, 1)
        for copy in b_copies(it):
            copy.start()

        finish_near(first, 1)
        pressure = pressure + fields[2][...] * acc[0]
        pres[...] = pressure
        work[second, 0] = minus_laplace(pressure)
        stage_corners(second, 1)
        stage_faces(second, 1)
        send_near(second, 1)
        begin_near(second, 1)

        take(b_recv.at[it], b_rows)
        pieces, walls = [], []
        for x in range(planes):
            before, after = (x - 1) % planes, (x + 1) % planes
            for k in range(2):
                sums = [None] * 3
                for sy in range(4):
                    one = g2[it, 4 * x + sy, 8 * k : 8 * k + 8, :]
                    if k == 0:
                        one = one + some(sublane < 2, g2[it, 4 * before + sy, 16:24, :])
                    else:
                        extra = pltpu.roll(g2[it, 4 * after + sy, 16:24, :], 5, 0)
                        one = one + some(sublane == 7, extra)
                    for n in range(3):
                        at = 8 + 3 * sy + n
                        part = one * rows[at : at + 1, :]
                        sums[n] = part if sums[n] is None else sums[n] + part
                pieces.append(sums[0])
                walls.append(pltpu.roll(sums[1], 48, 1) + pltpu.roll(sums[2], 97, 1))
        right_side = [jnp.concatenate(pieces, axis=0), jnp.concatenate(walls, axis=0)]
        own = conjugate(right_side)
        vertex = [own[v : v + 1, :] for v in range(4)]

        interp, image = [], []
        for z in range(8):
            value = float(jz[z, 1]) * vertex[1] + float(jz[z, 2]) * vertex[2]
            interp.append(value * spans[0][...])
            part = (float(waz[z]) * value) * spans[2][...]
            if np.any(kz[z] != 0.0):
                bend = None
                for v in range(4):
                    if kz[z, v] != 0.0:
                        term = (0.5 * float(kz[z, v])) * vertex[v]
                        bend = term if bend is None else bend + term
                part = part + bend * spans[1][...]
            image.append(part)
        interp = split(jnp.concatenate(interp, axis=0))
        image = split(jnp.concatenate(image, axis=0))
        correction = right_dot(interp, M_JYT)
        applied = rows[0:1, :] * right_dot(image, M_JYT)
        applied = applied + fields[3][...] * right_dot(interp, M_KYT, True)
        finish_near(second, 1)
        pressure = pres[...] + correction + fields[2][...] * (acc[0] - applied)
        pres[...] = pressure

        @pl.when(it < MG_ITERS - 1)
        def _():
            work[first + 2, 0] = minus_laplace(pressure)

        return carry

    lax.fori_loop(0, MG_ITERS, cycle, 0)
    p_out[...] = pres[...]

    for r in range(ROUNDS):
        take(n_send.at[r], near_rows(3 if r < SUBSTEPS else 1))
    for it in range(MG_ITERS):
        take(a_send.at[it], a_rows)
        take(b_send.at[it], b_rows)


def solution(mesh):
    count = mesh.shape["elem"]
    matrices, small, jz, kz, waz = make_tables()
    planes = count // 16
    f32 = jnp.float32

    def shards(velocity):
        vmem = pl.BlockSpec(memory_space=pltpu.VMEM)
        hbm = pl.BlockSpec(memory_space=pltpu.HBM)
        advected, pressure = pl.pallas_call(
            functools.partial(kernel, (jz, kz, waz), count),
            out_shape=(
                jax.ShapeDtypeStruct((3, 128, 128), f32),
                jax.ShapeDtypeStruct((128, 128), f32),
            ),
            in_specs=[hbm] * 3,
            out_specs=(vmem, vmem),
            scratch_shapes=[
                pltpu.VMEM((3, 128, 128), f32),
                pltpu.VMEM(matrices.shape, jnp.bfloat16),
                pltpu.VMEM(small.shape, f32),
                pltpu.VMEM((128, 128), f32),
                pltpu.VMEM((128, 128), f32),
                pltpu.VMEM((8, 128), f32),
                pltpu.VMEM((ROUNDS, 3, 128, 128), f32),
                pltpu.VMEM((3, 128, 128), f32),
                pltpu.VMEM((ROUNDS, 2, 3, 8, 128), f32),
                pltpu.VMEM((ROUNDS, 4, 8, 128), f32),
                pltpu.VMEM((ROUNDS, 2, 3, 16, 128), f32),
                pltpu.VMEM((ROUNDS, 2, 3, 8, 128), f32),
                pltpu.VMEM((ROUNDS, 4, 8, 128), f32),
                pltpu.VMEM((MG_ITERS, 16, 8, 128), f32),
                pltpu.VMEM((MG_ITERS, 4 * planes, 24, 128), f32),
                pltpu.VMEM((COARSE_ITERS, 2, count + 16, 128), f32),
                pltpu.VMEM((360, 128), f32),
                pltpu.SemaphoreType.DMA((3,)),
                pltpu.SemaphoreType.DMA((ROUNDS,)),
                pltpu.SemaphoreType.DMA((ROUNDS,)),
                pltpu.SemaphoreType.DMA((MG_ITERS,)),
                pltpu.SemaphoreType.DMA((MG_ITERS,)),
                pltpu.SemaphoreType.DMA((MG_ITERS,)),
                pltpu.SemaphoreType.DMA((MG_ITERS,)),
                pltpu.SemaphoreType.REGULAR,
                pltpu.SemaphoreType.REGULAR,
            ],
            compiler_params=pltpu.CompilerParams(
                collective_id=0, has_side_effects=True, vmem_limit_bytes=54912 * 1024
            ),
        )(
            velocity.reshape(3, 128, 128),
            jnp.asarray(matrices),
            jnp.asarray(small),
        )
        return advected.reshape(3, 8, 16, 128), pressure.reshape(8, 16, 128)

    return jax.shard_map(
        shards,
        mesh=mesh,
        in_specs=(P(None, "elem", "sub", None),),
        out_specs=(P(None, "elem", "sub", None), P("elem", "sub", None)),
        check_vma=False,
    )
```
